256 devices in a mesh: row: 16 (over y_hi, x, core), col: 16 (over z, y_lo).
Axes of the slice: x: 4, y: 4 (y_hi: 2, y_lo: 2; y = y_hi * 2 + y_lo), z: 8, core: 2. Of those that a mesh axis runs over, the one named last changes fastest.
Arguments:
- bottom_in: bfloat16 [256, 256, 256], P('row', 'col'), may hold values from -6 to 6
- skip_feat: bfloat16 [512, 512, 128], P('row', 'col'), may hold values from -6 to 6
- cotangent: bfloat16 [512, 512, 128], P('row', 'col'), may hold values from -6 to 6
- bot_kernel: bfloat16 [3, 3, 256, 256], replicated, may hold values from -0.125 to 0.125
- up_kernel: bfloat16 [4, 4, 256, 128], replicated, may hold values from -0.1875 to 0.1875
- lvl_kernel: bfloat16 [3, 3, 128, 128], replicated, may hold values from -0.1875 to 0.1875
Outputs:
- level_out: bfloat16 [512, 512, 128], P('row', 'col')
- bottom_grad: bfloat16 [256, 256, 256], P('row', 'col')
- lvl_grad: float32 [3, 3, 128, 128], replicated
- up_grad: float32 [4, 4, 256, 128], replicated
- bot_grad: float32 [3, 3, 256, 256], replicated
The draws below stay inside these ranges and needn't reach their ends.
All inputs are finite; a program needn't handle non-finite values.
Results may differ from the reference program's by a relative error of at most 0.013.
Values may be sent and summed in bfloat16 or wider, within the bound.
No kernel may reach another device: no remote copies, remote signals or barrier semaphores. Data moves between devices by JAX's collectives and lax.ppermute only.
A program may use at most 64 MiB of HBM per device.

```python
import jax
import jax.numpy as jnp

C_LVL = 128
C_BOT = 256
H = 512
W = 512
HB = 256
WB = 256


def block_levels(key, extent, shards, smallest, high):
    loudness = 1.0
    for dim, blocks in shards:
        heights = jax.random.uniform(jax.random.fold_in(jax.random.fold_in(key, 6), dim), (blocks,), jnp.float32, smallest / len(shards), high / len(shards))
        loudness = loudness * jnp.repeat(jnp.exp(heights), extent[dim] // blocks).reshape((-1,) + (1,) * (len(extent) - 1 - dim))
    return loudness


def gaussian(key, extent, scale, most, shards=(), dtype=jnp.bfloat16):
    drawn = scale * jax.random.normal(key, extent, jnp.float32)
    if shards:
        drawn = drawn * block_levels(key, extent, shards, -0.22, 0.18)
    return jnp.clip(drawn, -most, most).astype(dtype)


def setup_inputs(seed: int = 0) -> dict:
    key_list = jax.random.split(jax.random.key(seed), 7)
    return {
        "bottom_in": gaussian(key_list[0], (HB, WB, C_BOT), 1.0, 6.0, ((0, 16), (1, 16))),
        "skip_feat": gaussian(key_list[1], (H, W, C_LVL), 1.0, 6.0, ((0, 16), (1, 16))),
        "cotangent": gaussian(key_list[2], (H, W, C_LVL), 1.0, 6.0, ((0, 16), (1, 16))),
        "bot_kernel": gaussian(key_list[3], (3, 3, C_BOT, C_BOT), (9 * C_BOT) ** -0.5, 0.125),
        "up_kernel": gaussian(key_list[4], (4, 4, C_BOT, C_LVL), (4 * C_BOT) ** -0.5, 0.1875),
        "lvl_kernel": gaussian(key_list[5], (3, 3, C_LVL, C_LVL), (9 * C_LVL) ** -0.5, 0.1875),
    }


up_taps = (((1, 0), (3, -1)), ((0, 1), (2, 0)))

def spatial_pad(field):
    return jnp.pad(field, ((1, 1), (1, 1), (0, 0)))

def conv_taps(padded, kernel, height, width):
    total = jnp.zeros((height, width, kernel.shape[3]), jnp.float32)
    for row_tap in range(3):
        for col_tap in range(3):
            window = padded[row_tap:row_tap + height, col_tap:col_tap + width]
            total = total + jnp.einsum('hwc,cd->hwd', window.astype(jnp.float32), kernel[row_tap, col_tap].astype(jnp.float32))
    return total

def conv_back(padded_grad, kernel, height, width):
    total = jnp.zeros((height, width, kernel.shape[2]), jnp.float32)
    for row_tap in range(3):
        for col_tap in range(3):
            window = padded_grad[2 - row_tap:2 - row_tap + height, 2 - col_tap:2 - col_tap + width]
            total = total + jnp.einsum('hwd,cd->hwc', window.astype(jnp.float32), kernel[row_tap, col_tap].astype(jnp.float32))
    return total

def kernel_grad(padded_in, grad, height, width):
    pieces = []
    for row_tap in range(3):
        for col_tap in range(3):
            window = padded_in[row_tap:row_tap + height, col_tap:col_tap + width]
            pieces.append(jnp.einsum('hwc,hwd->cd', window.astype(jnp.float32), grad.astype(jnp.float32)))
    stacked = jnp.stack(pieces, axis=0)
    return stacked.reshape(3, 3, stacked.shape[1], stacked.shape[2])

def up_conv(padded, kernel, height, width):
    rows_out = []
    for row_par in range(2):
        cols_out = []
        for col_par in range(2):
            total = jnp.zeros((height, width, kernel.shape[3]), jnp.float32)
            for row_k, row_s in up_taps[row_par]:
                for col_k, col_s in up_taps[col_par]:
                    window = padded[1 + row_s:1 + row_s + height, 1 + col_s:1 + col_s + width]
                    total = total + jnp.einsum('hwc,cd->hwd', window.astype(jnp.float32), kernel[row_k, col_k].astype(jnp.float32))
            cols_out.append(total)
        rows_out.append(jnp.stack(cols_out, axis=2))
    joined = jnp.stack(rows_out, axis=1)
    return joined.reshape(2 * height, 2 * width, kernel.shape[3])

def up_back(padded_grad, kernel, height, width):
    total = jnp.zeros((height, width, kernel.shape[2]), jnp.float32)
    for row_k in range(4):
        for col_k in range(4):
            window = padded_grad[row_k:row_k + 2 * height:2, col_k:col_k + 2 * width:2]
            total = total + jnp.einsum('hwd,cd->hwc', window.astype(jnp.float32), kernel[row_k, col_k].astype(jnp.float32))
    return total

def up_kernel_grad(coarse, padded_grad, height, width):
    pieces = []
    for row_k in range(4):
        for col_k in range(4):
            window = padded_grad[row_k:row_k + 2 * height:2, col_k:col_k + 2 * width:2]
            pieces.append(jnp.einsum('hwc,hwd->cd', coarse.astype(jnp.float32), window.astype(jnp.float32)))
    stacked = jnp.stack(pieces, axis=0)
    return stacked.reshape(4, 4, stacked.shape[1], stacked.shape[2])

def reference(bottom_in, skip_feat, cotangent, bot_kernel, up_kernel, lvl_kernel):
    scale = 1.0 / float(H * W) ** 0.5
    bot_pad = spatial_pad(bottom_in)
    pre_act = conv_taps(bot_pad, bot_kernel, HB, WB)
    activ = jax.nn.silu(pre_act).astype(jnp.bfloat16)
    upsampled = up_conv(spatial_pad(activ), up_kernel, HB, WB)
    mixed = (upsampled + skip_feat.astype(jnp.float32)).astype(jnp.bfloat16)
    mix_pad = spatial_pad(mixed)
    level_out = conv_taps(mix_pad, lvl_kernel, H, W).astype(jnp.bfloat16)
    lvl_grad = kernel_grad(mix_pad, cotangent, H, W) * scale
    mixed_grad = conv_back(spatial_pad(cotangent), lvl_kernel, H, W).astype(jnp.bfloat16)
    mgrad_pad = spatial_pad(mixed_grad)
    up_grad = up_kernel_grad(activ, mgrad_pad, HB, WB) * scale
    activ_grad = up_back(mgrad_pad, up_kernel, HB, WB)
    sigma = jax.nn.sigmoid(pre_act)
    pre_grad = (activ_grad * sigma * (1.0 + pre_act * (1.0 - sigma))).astype(jnp.bfloat16)
    bot_grad = kernel_grad(bot_pad, pre_grad, HB, WB) * scale
    bottom_grad = conv_back(spatial_pad(pre_grad), bot_kernel, HB, WB).astype(jnp.bfloat16)
    return (level_out, bottom_grad, lvl_grad, up_grad, bot_grad)
```

```python
import functools

import jax
import jax.numpy as jnp
from jax import lax
from jax.experimental import pallas as pl
from jax.experimental.pallas import tpu as pltpu
from jax.sharding import PartitionSpec as P

AXES = ("row", "col")
F32 = jnp.float32
BF16 = jnp.bfloat16
TILE = 16
EXT = TILE + 4
PITCH = 32
CORE = 8
HALF = 5120


def place(x, y, z, core):
    row = (((y >> 1) & 1) * 4 + x % 4) * 2 + core
    col = (z % 8) * 2 + (y & 1)
    return row * 16 + col


PLANE_GROUPS = [
    [place(x, y, z, core) for x in range(4) for y in range(4)]
    for z in range(8)
    for core in range(2)
]
DEPTH_GROUPS = [
    [place(x, y, z, core) for z in range(8)]
    for x in range(4)
    for y in range(4)
    for core in range(2)
]
CORE_SWAP = [(i, i ^ 1) for i in range(16)]


def split_kernel(bot_ref, skip_ref, cot_ref, out_ref, wide):
    out_ref[0] = bot_ref[...]
    for plane, ref in ((1, cot_ref), (3, skip_ref)):
        wide[...] = ref[...].astype(F32)
        for col_par in range(2):
            part = wide[:, pl.ds(col_par, TILE, stride=2), :].astype(BF16)
            part = part.reshape(TILE, 2, TILE, 128)
            lanes = slice(col_par * 128, col_par * 128 + 128)
            out_ref[plane, :, :, lanes] = part[:, 0]
            out_ref[plane + 1, :, :, lanes] = part[:, 1]


def split(bottom_in, skip_feat, cotangent):
    return pl.pallas_call(
        split_kernel,
        out_shape=jax.ShapeDtypeStruct((5, TILE, TILE, 256), BF16),
        scratch_shapes=[pltpu.VMEM((2 * TILE, 2 * TILE, 128), F32)],
        compiler_params=pltpu.CompilerParams(vmem_limit_bytes=16 << 20),
    )(bottom_in, skip_feat, cotangent)


def nn(a, b):
    return lax.dot_general(a, b, (((1,), (0,)), ((), ())), preferred_element_type=F32)


def nt(a, b):
    return lax.dot_general(a, b, (((1,), (1,)), ((), ())), preferred_element_type=F32)


def tn(a, b):
    return lax.dot_general(a, b, (((0,), (0,)), ((), ())), preferred_element_type=F32)


def flat(x):
    return x.reshape(-1, x.shape[-1])


def left(x):
    return pltpu.roll(x, 1, 0)


def right(x):
    return pltpu.roll(x, x.shape[0] - 1, 0)


def core_of(x):
    rows = x.shape[0] // PITCH
    return x.reshape(rows, PITCH, x.shape[1])[:, CORE : CORE + TILE]


def three(x):
    return (left(x), x, right(x))


def four(x):
    return (left(x[:, 128:]), x, right(x[:, :128]))


def fine_row(offset):
    return offset % 2, offset // 2


def pair_weight(taps, zero):
    first = jnp.concatenate([taps[0], taps[1], taps[2], zero], axis=0)
    second = jnp.concatenate([zero, taps[0], taps[1], taps[2]], axis=0)
    return jnp.concatenate([first, second], axis=1)


def pair_weight_back(taps, zero):
    first = jnp.concatenate([taps[0], taps[1], taps[2], zero], axis=1)
    second = jnp.concatenate([zero, taps[0], taps[1], taps[2]], axis=1)
    return jnp.concatenate([first, second], axis=0)


def main_kernel(
    scale, pos_ref, z_ref, up_ref, down_ref, lo_ref, hi_ref, bk_ref, uk_ref, lk_ref,
    level_ref, bgrad_ref, grad_ref,
    ext, bot3, botc, act3, actc, dsilu, cot4, mg4, mg4c, mix4c, pg3c, pgc, inter,
):
    row0 = pos_ref[0] * TILE
    col0 = pos_ref[1] * TILE
    image_h = pos_ref[2]
    image_w = pos_ref[3]
    mine = pos_ref[4]

    ext[...] = jnp.zeros_like(ext)
    ext[:, 0:2, CORE : CORE + TILE, :] = up_ref[...].astype(F32)
    ext[:, 2 : 2 + TILE, CORE : CORE + TILE, :] = z_ref[...].astype(F32)
    ext[:, 2 + TILE : EXT, CORE : CORE + TILE, :] = down_ref[...].astype(F32)
    ext[:, :, CORE - 2 : CORE, :] = lo_ref[...].astype(F32)
    ext[:, :, CORE + TILE : CORE + TILE + 2, :] = hi_ref[...].astype(F32)

    def masked(x, first):
        rows = x.shape[0] // PITCH
        x = x.reshape(rows, PITCH, x.shape[1])
        i = lax.broadcasted_iota(jnp.int32, x.shape, 0) + (row0 + first - 2)
        w = lax.broadcasted_iota(jnp.int32, x.shape, 1)
        j = w + (col0 - CORE)
        keep = (i >= 0) & (i < image_h) & (j >= 0) & (j < image_w)
        keep = keep & (w >= CORE - 2) & (w < CORE + TILE + 2)
        return flat(jnp.where(keep, x, 0.0))

    zero = jnp.zeros((128, 128), BF16)

    for b, part in enumerate(three(flat(ext[0]))):
        lanes = slice(256 * b, 256 * b + 256)
        bot3[:, :, lanes] = part.reshape(EXT, PITCH, 256).astype(BF16)
        botc[:, :, lanes] = core_of(part)[1 : 19].astype(BF16)
    pre = jnp.zeros((18 * PITCH, 256), F32)
    for a in range(3):
        pre = pre + nn(flat(bot3[a : a + 18]), bk_ref[a].reshape(768, 256))
    sigma = jax.nn.sigmoid(pre)
    dsilu[...] = sigma * (1.0 + pre * (1.0 - sigma))
    activ = masked((pre * sigma).astype(BF16).astype(F32), 1)
    act3[0] = jnp.zeros((PITCH, 768), BF16)
    act3[EXT - 1] = jnp.zeros((PITCH, 768), BF16)
    for b, part in enumerate(three(activ)):
        act3[1:19, :, 256 * b : 256 * b + 256] = part.reshape(18, PITCH, 256).astype(BF16)
    actc[...] = flat(core_of(activ)[1:17]).astype(BF16)

    for par in range(2):
        a, b, c = four(flat(ext[1 + par]))
        cot4[par, :, :, 0:128] = a.reshape(EXT, PITCH, 128).astype(BF16)
        cot4[par, :, :, 128:384] = b.reshape(EXT, PITCH, 256).astype(BF16)
        cot4[par, :, :, 384:512] = c.reshape(EXT, PITCH, 128).astype(BF16)
    for par in range(2):
        first = 1 - par
        total = jnp.zeros((19 * PITCH, 256), F32)
        for a in range(3):
            src, shift = fine_row(par + a - 1)
            weight = pair_weight_back([lk_ref[2 - a, 2 - b] for b in range(3)], zero)
            total = total + nt(flat(cot4[src, first + shift : first + shift + 19]), weight)
        grad = masked(total.astype(BF16).astype(F32), first)
        a, b, c = four(grad)
        mg4[par, first : first + 19, :, 0:128] = a.reshape(19, PITCH, 128).astype(BF16)
        mg4[par, first : first + 19, :, 128:384] = b.reshape(19, PITCH, 256).astype(BF16)
        mg4[par, first : first + 19, :, 384:512] = c.reshape(19, PITCH, 128).astype(BF16)
        mg4c[par, first : first + 19, :, 0:128] = core_of(a).astype(BF16)
        mg4c[par, first : first + 19, :, 128:384] = core_of(b).astype(BF16)
        mg4c[par, first : first + 19, :, 384:512] = core_of(c).astype(BF16)

    def put(half, row, value):
        slot = lax.rem(half + mine, 2)
        grad_ref[slot, pl.ds(row, value.shape[0]), :] = (value * scale).astype(BF16)

    act_t = actc[...].T
    for a in range(4):
        src, shift = fine_row(a - 1)
        prod = nn(act_t, flat(mg4c[src, 2 + shift : 18 + shift]))
        for b in range(4):
            put(0, (4 * a + b) * 256, prod[:, 128 * b : 128 * b + 128])

    agrad = jnp.zeros((18 * PITCH, 256), F32)
    for a in range(4):
        src, shift = fine_row(a - 1)
        weight = jnp.concatenate([uk_ref[a, b] for b in range(4)], axis=1)
        agrad = agrad + nt(flat(mg4[src, 1 + shift : 19 + shift]), weight)
    pgrad = masked((agrad * dsilu[...]).astype(BF16).astype(F32), 1)
    for b, part in enumerate(three(pgrad)):
        pg3c[:, :, 256 * b : 256 * b + 256] = core_of(part).astype(BF16)
    pgc[...] = flat(core_of(pgrad)[1:17]).astype(BF16)

    for a in range(3):
        prod = tn(flat(botc[a : a + 16]), pgc[...])
        put(1, 768 * a, prod[:, :128])
        put(1, 2304 + 768 * a, prod[:, 128:])

    for par in range(2):
        total = flat(ext[3 + par, 1:19])
        for row_k, shift in (((1, 0), (3, -1)), ((0, 1), (2, 0)))[par]:
            k = [uk_ref[row_k, b] for b in range(4)]
            none = jnp.zeros((256, 128), BF16)
            weight = jnp.concatenate(
                [
                    jnp.concatenate([k[3], k[1], none], axis=0),
                    jnp.concatenate([none, k[2], k[0]], axis=0),
                ],
                axis=1,
            )
            total = total + nn(flat(act3[1 + shift : 19 + shift]), weight)
        mixed = masked(total.astype(BF16).astype(F32), 1)
        a, b, c = four(mixed)
        mix4c[par, :, :, 0:128] = core_of(a).astype(BF16)
        mix4c[par, :, :, 128:384] = core_of(b).astype(BF16)
        mix4c[par, :, :, 384:512] = core_of(c).astype(BF16)

    for a in range(3):
        prod = jnp.zeros((512, 256), F32)
        for par in range(2):
            src, shift = fine_row(par + a - 1)
            prod = prod + tn(
                flat(mix4c[src, 1 + shift : 17 + shift]), flat(z_ref[1 + par])
            )
        for b in range(3):
            tap = prod[128 * b : 128 * b + 128, :128] + prod[128 * b + 128 : 128 * b + 256, 128:]
            if a < 2:
                put(0, 4096 + (3 * a + b) * 128, tap)
            else:
                put(1, 4608 + b * 128, tap)
    put(0, 4864, jnp.zeros((HALF - 4864, 128), F32))
    put(1, 4992, jnp.zeros((HALF - 4992, 128), F32))

    for par in range(2):
        total = jnp.zeros((TILE * TILE, 256), F32)
        for a in range(3):
            src, shift = fine_row(par + a - 1)
            weight = pair_weight([lk_ref[a, b] for b in range(3)], zero)
            total = total + nn(flat(mix4c[src, 1 + shift : 17 + shift]), weight)
        total = total.reshape(TILE, TILE, 256)
        for col_par in range(2):
            inter[:, par, pl.ds(col_par, TILE, stride=2), :] = total[
                :, :, 128 * col_par : 128 * col_par + 128
            ]
    level_ref[...] = inter[...].reshape(2 * TILE, 2 * TILE, 128).astype(BF16)

    total = jnp.zeros((TILE * TILE, 256), F32)
    for a in range(3):
        weight = jnp.concatenate([bk_ref[2 - a, 2 - b] for b in range(3)], axis=1)
        total = total + nt(flat(pg3c[a : a + 16]), weight)
    bgrad_ref[...] = total.reshape(TILE, TILE, 256).astype(BF16)


def local_work(scale, pos, z, up, down, lo, hi, bot_kernel, up_kernel, lvl_kernel):
    vmem = pl.BlockSpec(memory_space=pltpu.VMEM)
    return pl.pallas_call(
        functools.partial(main_kernel, scale),
        out_shape=(
            jax.ShapeDtypeStruct((2 * TILE, 2 * TILE, 128), BF16),
            jax.ShapeDtypeStruct((TILE, TILE, 256), BF16),
            jax.ShapeDtypeStruct((2, HALF, 128), BF16),
        ),
        in_specs=[pl.BlockSpec(memory_space=pltpu.SMEM)] + [vmem] * 8,
        out_specs=(vmem, vmem, vmem),
        scratch_shapes=[
            pltpu.VMEM((5, EXT, PITCH, 256), F32),
            pltpu.VMEM((EXT, PITCH, 768), BF16),
            pltpu.VMEM((18, TILE, 768), BF16),
            pltpu.VMEM((EXT, PITCH, 768), BF16),
            pltpu.VMEM((TILE * TILE, 256), BF16),
            pltpu.VMEM((18 * PITCH, 256), F32),
            pltpu.VMEM((2, EXT, PITCH, 512), BF16),
            pltpu.VMEM((2, EXT, PITCH, 512), BF16),
            pltpu.VMEM((2, EXT, TILE, 512), BF16),
            pltpu.VMEM((2, 18, TILE, 512), BF16),
            pltpu.VMEM((18, TILE, 768), BF16),
            pltpu.VMEM((TILE * TILE, 256), BF16),
            pltpu.VMEM((TILE, 2, 2 * TILE, 128), F32),
        ],
        compiler_params=pltpu.CompilerParams(vmem_limit_bytes=56 << 20),
    )(pos, z, up, down, lo, hi, bot_kernel, up_kernel, lvl_kernel)


def shifted(last, first, axis):
    count = lax.axis_size(axis)
    up = [(i, i + 1) for i in range(count - 1)]
    down = [(i + 1, i) for i in range(count - 1)]
    return lax.ppermute(last, axis, up), lax.ppermute(first, axis, down)


def spread(x, count, groups):
    return lax.all_to_all(
        jnp.broadcast_to(x[None], (count,) + x.shape), AXES, 0, 0, axis_index_groups=groups
    )


def sum_parts(x):
    return jnp.sum(x.astype(F32), axis=0).astype(BF16)


def total_over_devices(grads):
    got = lax.ppermute(grads[1], "row", CORE_SWAP)
    half = (grads[0].astype(F32) + got.astype(F32)).astype(BF16).reshape(16, HALF // 16, 128)
    part = sum_parts(lax.all_to_all(half, AXES, 0, 0, axis_index_groups=PLANE_GROUPS))
    part = jnp.pad(part.reshape(8, HALF // 128, 128), ((0, 0), (0, 8), (0, 0)))
    piece = sum_parts(lax.all_to_all(part, AXES, 0, 0, axis_index_groups=DEPTH_GROUPS))
    part = spread(piece, 8, DEPTH_GROUPS)[:, : HALF // 128].reshape(HALF // 16, 128)
    half = spread(part, 16, PLANE_GROUPS).reshape(HALF, 128)
    other = lax.ppermute(half, "row", CORE_SWAP)
    core = lax.rem(lax.axis_index("row"), 2)
    return jnp.where(core == 0, half, other), jnp.where(core == 0, other, half)


def on_device(bottom_in, skip_feat, cotangent, bot_kernel, up_kernel, lvl_kernel):
    rows, cols = lax.axis_size("row"), lax.axis_size("col")
    scale = 1.0 / float(2 * TILE * rows * 2 * TILE * cols) ** 0.5
    z = split(bottom_in, skip_feat, cotangent)
    up, down = shifted(z[:, TILE - 2 :], z[:, :2], "row")
    last = jnp.concatenate([up[:, :, -2:], z[:, :, -2:], down[:, :, -2:]], axis=1)
    first = jnp.concatenate([up[:, :, :2], z[:, :, :2], down[:, :, :2]], axis=1)
    lo, hi = shifted(last, first, "col")
    row = lax.axis_index("row")
    pos = jnp.stack(
        [row, lax.axis_index("col"), jnp.int32(TILE * rows), jnp.int32(TILE * cols), row % 2]
    ).astype(jnp.int32)
    level_out, bottom_grad, grads = local_work(
        scale, pos, z, up, down, lo, hi, bot_kernel, up_kernel, lvl_kernel
    )
    even, odd = total_over_devices(grads)
    up_grad = even[:4096].astype(F32).reshape(4, 4, 256, 128)
    lvl_grad = jnp.concatenate([even[4096:4864], odd[4608:4992]], axis=0).astype(F32)
    bot_grad = jnp.concatenate([odd[:2304], odd[2304:4608]], axis=1).astype(F32)
    return (
        level_out,
        bottom_grad,
        lvl_grad.reshape(3, 3, 128, 128),
        up_grad,
        bot_grad.reshape(3, 3, 256, 256),
    )


def solution(mesh):
    return jax.shard_map(
        on_device,
        mesh=mesh,
        in_specs=(
            P("row", "col", None),
            P("row", "col", None),
            P("row", "col", None),
            P(),
            P(),
            P(),
        ),
        out_specs=(P("row", "col", None), P("row", "col", None), P(), P(), P()),
        check_vma=False,
    )
```

```python
import functools

import jax
import jax.numpy as jnp
from jax import lax
from jax.experimental import pallas as pl
from jax.experimental.pallas import tpu as pltpu
from jax.sharding import PartitionSpec as P

AXES = ("row", "col")
F32 = jnp.float32
BF16 = jnp.bfloat16
TILE = 16
EXT = TILE + 4
PITCH = 32
CORE = 8
HALF = 5120


def place(x, y, z, core):
    row = (((y >> 1) & 1) * 4 + x % 4) * 2 + core
    col = (z % 8) * 2 + (y & 1)
    return row * 16 + col


def device_xyz(device):
    row, col = divmod(device, 16)
    return (row >> 1) & 3, ((row >> 3) << 1) | (col & 1), col >> 1, row & 1


BLOCK = 32
BLOCK_GROUPS = [
    [place(x, y, z + dz, core) for dz in range(2) for x in range(4) for y in range(4)]
    for z in range(0, 8, 2)
    for core in range(2)
]


def depth_shift(step):
    moves = []
    for device in range(256):
        x, y, z, core = device_xyz(device)
        moves.append((device, place(x, y, z + step, core)))
    return moves


CORE_SWAP = [(i, i ^ 1) for i in range(16)]


def split_kernel(
    bot_hbm, skip_hbm, cot_hbm, out_ref, last_ref, first_ref, bot, skip, cot, wide, sems
):
    copies = [
        pltpu.make_async_copy(src, dst, sems.at[i])
        for i, (src, dst) in enumerate(((cot_hbm, cot), (skip_hbm, skip), (bot_hbm, bot)))
    ]
    for copy in copies:
        copy.start()
    for plane, ref, copy in ((1, cot, copies[0]), (3, skip, copies[1])):
        copy.wait()
        wide[...] = ref[...].astype(F32)
        for col_par in range(2):
            part = wide[:, pl.ds(col_par, TILE, stride=2), :].astype(BF16)
            part = part.reshape(TILE, 2, TILE, 128)
            lanes = slice(col_par * 128, col_par * 128 + 128)
            out_ref[plane, :, :, lanes] = part[:, 0]
            out_ref[plane + 1, :, :, lanes] = part[:, 1]
    copies[2].wait()
    out_ref[0] = bot[...]
    for plane in range(3):
        last_ref[2 * plane : 2 * plane + 2] = out_ref[plane, TILE - 2 : TILE]
        first_ref[2 * plane : 2 * plane + 2] = out_ref[plane, 0:2]
    last_ref[6] = out_ref[4, TILE - 1]
    first_ref[6] = out_ref[3, 0]


def split(bottom_in, skip_feat, cotangent):
    vmem = pl.BlockSpec(memory_space=pltpu.VMEM)
    strip = jax.ShapeDtypeStruct((7, TILE, 256), BF16)
    return pl.pallas_call(
        split_kernel,
        out_shape=(jax.ShapeDtypeStruct((5, TILE, TILE, 256), BF16), strip, strip),
        in_specs=[pl.BlockSpec(memory_space=pl.ANY)] * 3,
        out_specs=(vmem, vmem, vmem),
        scratch_shapes=[
            pltpu.VMEM((TILE, TILE, 256), BF16),
            pltpu.VMEM((2 * TILE, 2 * TILE, 128), BF16),
            pltpu.VMEM((2 * TILE, 2 * TILE, 128), BF16),
            pltpu.VMEM((2 * TILE, 2 * TILE, 128), F32),
            pltpu.SemaphoreType.DMA((3,)),
        ],
        compiler_params=pltpu.CompilerParams(vmem_limit_bytes=16 << 20),
    )(bottom_in, skip_feat, cotangent)


def nn(a, b):
    return lax.dot_general(a, b, (((1,), (0,)), ((), ())), preferred_element_type=F32)


def nt(a, b):
    return lax.dot_general(a, b, (((1,), (1,)), ((), ())), preferred_element_type=F32)


def tn(a, b):
    return lax.dot_general(a, b, (((0,), (0,)), ((), ())), preferred_element_type=F32)


def flat(x):
    return x.reshape(-1, x.shape[-1])


def left(x):
    return pltpu.roll(x, 1, 0)


def right(x):
    return pltpu.roll(x, x.shape[0] - 1, 0)


def core_of(x):
    rows = x.shape[0] // PITCH
    return x.reshape(rows, PITCH, x.shape[1])[:, CORE : CORE + TILE]


def three(x):
    return (left(x), x, right(x))


def four(x):
    return (left(x[:, 128:]), x, right(x[:, :128]))


def fine_row(offset):
    return offset % 2, offset // 2


def pair_weight(taps, zero):
    first = jnp.concatenate([taps[0], taps[1], taps[2], zero], axis=0)
    second = jnp.concatenate([zero, taps[0], taps[1], taps[2]], axis=0)
    return jnp.concatenate([first, second], axis=1)


def pair_weight_back(taps, zero):
    first = jnp.concatenate([taps[0], taps[1], taps[2], zero], axis=1)
    second = jnp.concatenate([zero, taps[0], taps[1], taps[2]], axis=1)
    return jnp.concatenate([first, second], axis=0)


def main_kernel(
    scale, pos_ref, z_ref, up_ref, down_ref, lo_ref, hi_ref, bk_ref, uk_ref, lk_ref,
    mix4c, pg3c, keep_ref, send_ref,
    ext, bot3, botc, act3, actc, dsilu, cot4, mg4, mg4c, pgc, packed, sems,
):
    row0 = pos_ref[0] * TILE
    col0 = pos_ref[1] * TILE
    image_h = pos_ref[2]
    image_w = pos_ref[3]
    mine = pos_ref[4]

    core = slice(CORE, CORE + TILE)
    ext[...] = jnp.zeros_like(ext)
    ext[:, 2 : 2 + TILE, core, :] = z_ref[...].astype(F32)
    for plane in range(3):
        two = slice(2 * plane, 2 * plane + 2)
        ext[plane, 0:2, core, :] = up_ref[two].astype(F32)
        ext[plane, 2 + TILE : EXT, core, :] = down_ref[two].astype(F32)
        side = slice(EXT * plane, EXT * plane + EXT)
        ext[plane, :, CORE - 2 : CORE, :] = lo_ref[side].astype(F32)
        ext[plane, :, CORE + TILE : CORE + TILE + 2, :] = hi_ref[side].astype(F32)
    ext[4, 1, core, :] = up_ref[6].astype(F32)
    ext[3, 2 + TILE, core, :] = down_ref[6].astype(F32)
    for par in range(2):
        side = slice(3 * EXT, 3 * EXT + 18)
        ext[3 + par, 1:19, CORE - 1 : CORE, :] = lo_ref[side, par : par + 1].astype(F32)
        ext[3 + par, 1:19, CORE + TILE : CORE + TILE + 1, :] = hi_ref[
            side, par : par + 1
        ].astype(F32)

    def masked(x, first):
        rows = x.shape[0] // PITCH
        x = x.reshape(rows, PITCH, x.shape[1])
        i = lax.broadcasted_iota(jnp.int32, x.shape, 0) + (row0 + first - 2)
        w = lax.broadcasted_iota(jnp.int32, x.shape, 1)
        j = w + (col0 - CORE)
        keep = (i >= 0) & (i < image_h) & (j >= 0) & (j < image_w)
        keep = keep & (w >= CORE - 2) & (w < CORE + TILE + 2)
        return flat(jnp.where(keep, x, 0.0))

    zero = jnp.zeros((128, 128), BF16)

    for b, part in enumerate(three(flat(ext[0]))):
        lanes = slice(256 * b, 256 * b + 256)
        bot3[:, :, lanes] = part.reshape(EXT, PITCH, 256).astype(BF16)
        botc[:, :, lanes] = core_of(part)[1 : 19].astype(BF16)
    pre = jnp.zeros((18 * PITCH, 256), F32)
    for a in range(3):
        pre = pre + nn(flat(bot3[a : a + 18]), bk_ref[a].reshape(768, 256))
    sigma = jax.nn.sigmoid(pre)
    dsilu[...] = sigma * (1.0 + pre * (1.0 - sigma))
    activ = masked((pre * sigma).astype(BF16).astype(F32), 1)
    act3[0] = jnp.zeros((PITCH, 768), BF16)
    act3[EXT - 1] = jnp.zeros((PITCH, 768), BF16)
    for b, part in enumerate(three(activ)):
        act3[1:19, :, 256 * b : 256 * b + 256] = part.reshape(18, PITCH, 256).astype(BF16)
    actc[...] = flat(core_of(activ)[1:17]).astype(BF16)

    for par in range(2):
        a, b, c = four(flat(ext[1 + par]))
        cot4[par, :, :, 0:128] = a.reshape(EXT, PITCH, 128).astype(BF16)
        cot4[par, :, :, 128:384] = b.reshape(EXT, PITCH, 256).astype(BF16)
        cot4[par, :, :, 384:512] = c.reshape(EXT, PITCH, 128).astype(BF16)
    for par in range(2):
        first = 1 - par
        total = jnp.zeros((19 * PITCH, 256), F32)
        for a in range(3):
            src, shift = fine_row(par + a - 1)
            weight = pair_weight_back([lk_ref[2 - a, 2 - b] for b in range(3)], zero)
            total = total + nt(flat(cot4[src, first + shift : first + shift + 19]), weight)
        grad = masked(total.astype(BF16).astype(F32), first)
        a, b, c = four(grad)
        mg4[par, first : first + 19, :, 0:128] = a.reshape(19, PITCH, 128).astype(BF16)
        mg4[par, first : first + 19, :, 128:384] = b.reshape(19, PITCH, 256).astype(BF16)
        mg4[par, first : first + 19, :, 384:512] = c.reshape(19, PITCH, 128).astype(BF16)
        mg4c[par, first : first + 19, :, 0:128] = core_of(a).astype(BF16)
        mg4c[par, first : first + 19, :, 128:384] = core_of(b).astype(BF16)
        mg4c[par, first : first + 19, :, 384:512] = core_of(c).astype(BF16)

    def put(half, row, value):
        packed[half, row : row + value.shape[0], :] = (value * scale).astype(BF16)

    def hand_out(number, half, first, count, act):
        rows = pl.ds(first, count)
        for which in range(2):

            @pl.when(mine == which)
            def _():
                out = keep_ref if half == which else send_ref
                act(pltpu.make_async_copy(packed.at[half, rows], out.at[rows], sems.at[number]))

    parts = ((0, 0, 0, 4096), (1, 1, 0, 4608), (2, 0, 4096, HALF - 4096), (3, 1, 4608, HALF - 4608))

    act_t = actc[...].T
    for a in range(4):
        src, shift = fine_row(a - 1)
        prod = nn(act_t, flat(mg4c[src, 2 + shift : 18 + shift]))
        for b in range(4):
            put(0, (4 * a + b) * 256, prod[:, 128 * b : 128 * b + 128])
    hand_out(*parts[0], lambda copy: copy.start())

    agrad = jnp.zeros((18 * PITCH, 256), F32)
    for a in range(4):
        src, shift = fine_row(a - 1)
        weight = jnp.concatenate([uk_ref[a, b] for b in range(4)], axis=1)
        agrad = agrad + nt(flat(mg4[src, 1 + shift : 19 + shift]), weight)
    pgrad = masked((agrad * dsilu[...]).astype(BF16).astype(F32), 1)
    for b, part in enumerate(three(pgrad)):
        pg3c[:, :, 256 * b : 256 * b + 256] = core_of(part).astype(BF16)
    pgc[...] = flat(core_of(pgrad)[1:17]).astype(BF16)

    for a in range(3):
        prod = tn(flat(botc[a : a + 16]), pgc[...])
        put(1, 768 * a, prod[:, :128])
        put(1, 2304 + 768 * a, prod[:, 128:])
    hand_out(*parts[1], lambda copy: copy.start())

    for par in range(2):
        total = flat(ext[3 + par, 1:19])
        for row_k, shift in (((1, 0), (3, -1)), ((0, 1), (2, 0)))[par]:
            k = [uk_ref[row_k, b] for b in range(4)]
            none = jnp.zeros((256, 128), BF16)
            weight = jnp.concatenate(
                [
                    jnp.concatenate([k[3], k[1], none], axis=0),
                    jnp.concatenate([none, k[2], k[0]], axis=0),
                ],
                axis=1,
            )
            total = total + nn(flat(act3[1 + shift : 19 + shift]), weight)
        mixed = masked(total.astype(BF16).astype(F32), 1)
        a, b, c = four(mixed)
        mix4c[par, :, :, 0:128] = core_of(a).astype(BF16)
        mix4c[par, :, :, 128:384] = core_of(b).astype(BF16)
        mix4c[par, :, :, 384:512] = core_of(c).astype(BF16)

    for a in range(3):
        prod = jnp.zeros((512, 256), F32)
        for par in range(2):
            src, shift = fine_row(par + a - 1)
            prod = prod + tn(
                flat(mix4c[src, 1 + shift : 17 + shift]), flat(z_ref[1 + par])
            )
        for b in range(3):
            tap = prod[128 * b : 128 * b + 128, :128] + prod[128 * b + 128 : 128 * b + 256, 128:]
            if a < 2:
                put(0, 4096 + (3 * a + b) * 128, tap)
            else:
                put(1, 4608 + b * 128, tap)
    put(0, 4864, jnp.zeros((HALF - 4864, 128), F32))
    put(1, 4992, jnp.zeros((HALF - 4992, 128), F32))

    for part in parts[2:]:
        hand_out(*part, lambda copy: copy.start())
    for part in parts:
        hand_out(*part, lambda copy: copy.wait())


def rest_kernel(mix4c, pg3c, bk_ref, lk_ref, level_ref, bgrad_ref, inter):
    zero = jnp.zeros((128, 128), BF16)

    for par in range(2):
        total = jnp.zeros((TILE * TILE, 256), F32)
        for a in range(3):
            src, shift = fine_row(par + a - 1)
            weight = pair_weight([lk_ref[a, b] for b in range(3)], zero)
            total = total + nn(flat(mix4c[src, 1 + shift : 17 + shift]), weight)
        total = total.reshape(TILE, TILE, 256)
        for col_par in range(2):
            inter[:, par, pl.ds(col_par, TILE, stride=2), :] = total[
                :, :, 128 * col_par : 128 * col_par + 128
            ]
    level_ref[...] = inter[...].reshape(2 * TILE, 2 * TILE, 128).astype(BF16)

    total = jnp.zeros((TILE * TILE, 256), F32)
    for a in range(3):
        weight = jnp.concatenate([bk_ref[2 - a, 2 - b] for b in range(3)], axis=1)
        total = total + nt(flat(pg3c[a : a + 16]), weight)
    bgrad_ref[...] = total.reshape(TILE, TILE, 256).astype(BF16)


def rest_work(mix4c, pg3c, bot_kernel, lvl_kernel):
    return pl.pallas_call(
        rest_kernel,
        out_shape=(
            jax.ShapeDtypeStruct((2 * TILE, 2 * TILE, 128), BF16),
            jax.ShapeDtypeStruct((TILE, TILE, 256), BF16),
        ),
        scratch_shapes=[pltpu.VMEM((TILE, 2, 2 * TILE, 128), F32)],
        compiler_params=pltpu.CompilerParams(vmem_limit_bytes=16 << 20),
        cost_estimate=pl.CostEstimate(
            flops=1000000000, bytes_accessed=3000000, transcendentals=0
        ),
    )(mix4c, pg3c, bot_kernel, lvl_kernel)


def local_work(scale, pos, z, up, down, lo, hi, bot_kernel, up_kernel, lvl_kernel):
    vmem = pl.BlockSpec(memory_space=pltpu.VMEM)
    anywhere = pl.BlockSpec(memory_space=pl.ANY)
    return pl.pallas_call(
        functools.partial(main_kernel, scale),
        out_shape=(
            jax.ShapeDtypeStruct((2, 18, TILE, 512), BF16),
            jax.ShapeDtypeStruct((18, TILE, 768), BF16),
            jax.ShapeDtypeStruct((HALF, 128), BF16),
            jax.ShapeDtypeStruct((HALF, 128), BF16),
        ),
        in_specs=[pl.BlockSpec(memory_space=pltpu.SMEM)] + [vmem] * 8,
        out_specs=(vmem, vmem, anywhere, anywhere),
        scratch_shapes=[
            pltpu.VMEM((5, EXT, PITCH, 256), F32),
            pltpu.VMEM((EXT, PITCH, 768), BF16),
            pltpu.VMEM((18, TILE, 768), BF16),
            pltpu.VMEM((EXT, PITCH, 768), BF16),
            pltpu.VMEM((TILE * TILE, 256), BF16),
            pltpu.VMEM((18 * PITCH, 256), F32),
            pltpu.VMEM((2, EXT, PITCH, 512), BF16),
            pltpu.VMEM((2, EXT, PITCH, 512), BF16),
            pltpu.VMEM((2, EXT, TILE, 512), BF16),
            pltpu.VMEM((TILE * TILE, 256), BF16),
            pltpu.VMEM((2, HALF, 128), BF16),
            pltpu.SemaphoreType.DMA((4,)),
        ],
        compiler_params=pltpu.CompilerParams(vmem_limit_bytes=48 << 20),
    )(pos, z, up, down, lo, hi, bot_kernel, up_kernel, lvl_kernel)


def unpack_kernel(
    pos_ref, half_hbm, other_hbm, up_hbm, bot_hbm, lvl_hbm,
    half, other, up, bot, lvl, in_sems, out_sems,
):
    ins = [
        pltpu.make_async_copy(src, dst, in_sems.at[i])
        for i, (src, dst) in enumerate(((half_hbm, half), (other_hbm, other)))
    ]
    for copy in ins:
        copy.start()
    for copy in ins:
        copy.wait()
    for which in range(2):

        @pl.when(pos_ref[4] == which)
        def _():
            even, odd = (half, other) if which == 0 else (other, half)
            up[...] = even[0:4096].astype(F32)
            lvl[0:768] = even[4096:4864].astype(F32)
            lvl[768:1152] = odd[4608:4992].astype(F32)
            bot[:, 0:128] = odd[0:2304].astype(F32)
            bot[:, 128:256] = odd[2304:4608].astype(F32)

    outs = [
        pltpu.make_async_copy(src, dst, out_sems.at[i])
        for i, (src, dst) in enumerate(((up, up_hbm), (bot, bot_hbm), (lvl, lvl_hbm)))
    ]
    for copy in outs:
        copy.start()
    for copy in outs:
        copy.wait()


def unpack(pos, half, other):
    anywhere = pl.BlockSpec(memory_space=pl.ANY)
    shapes = ((4096, 128), (2304, 256), (1152, 128))
    return pl.pallas_call(
        unpack_kernel,
        out_shape=tuple(jax.ShapeDtypeStruct(shape, F32) for shape in shapes),
        in_specs=[pl.BlockSpec(memory_space=pltpu.SMEM), anywhere, anywhere],
        out_specs=(anywhere,) * 3,
        scratch_shapes=[pltpu.VMEM((HALF, 128), BF16)] * 2
        + [pltpu.VMEM(shape, F32) for shape in shapes]
        + [pltpu.SemaphoreType.DMA((2,)), pltpu.SemaphoreType.DMA((3,))],
        compiler_params=pltpu.CompilerParams(vmem_limit_bytes=16 << 20),
    )(pos, half, other)


def shifted(last, first, axis):
    count = lax.axis_size(axis)
    up = [(i, i + 1) for i in range(count - 1)]
    down = [(i + 1, i) for i in range(count - 1)]
    return lax.ppermute(last, axis, up), lax.ppermute(first, axis, down)


def exchange(x):
    return lax.all_to_all(x, AXES, 0, 0, axis_index_groups=BLOCK_GROUPS)


def total_over_devices(keep, send):
    got = lax.ppermute(send, "row", CORE_SWAP)
    half = (keep.astype(F32) + got.astype(F32)).astype(BF16)
    parts = exchange(half.reshape(BLOCK, HALF // BLOCK, 128))
    part = jnp.sum(parts.astype(F32), axis=0).astype(BF16)
    planes = [lax.ppermute(part, AXES, depth_shift(step)) for step in (2, 6, 4)]
    pair = lax.axis_index("col") // 4
    terms = [part] + planes
    places = [pair, (pair + 3) % 4, (pair + 1) % 4, (pair + 2) % 4]
    total = jnp.zeros(part.shape, F32)
    for slot in range(4):
        for term, where in zip(terms, places):
            total = total + jnp.where(where == slot, term.astype(F32), 0.0)
    total = total.astype(BF16)
    half = exchange(jnp.broadcast_to(total[None], parts.shape)).reshape(HALF, 128)
    return half, lax.ppermute(half, "row", CORE_SWAP)


def on_device(bottom_in, skip_feat, cotangent, bot_kernel, up_kernel, lvl_kernel):
    rows, cols = lax.axis_size("row"), lax.axis_size("col")
    scale = 1.0 / float(2 * TILE * rows * 2 * TILE * cols) ** 0.5
    z, last, first = split(bottom_in, skip_feat, cotangent)
    up, down = shifted(last, first, "row")

    def side(cols, skip_col):
        parts = [
            jnp.concatenate(
                [up[2 * p : 2 * p + 2, cols], z[p, :, cols], down[2 * p : 2 * p + 2, cols]], axis=0
            )
            for p in range(3)
        ]
        blank = jnp.zeros((1, 1, 256), BF16)
        even = jnp.concatenate([blank, z[3, :, skip_col], down[6:7, skip_col]], axis=0)
        odd = jnp.concatenate([up[6:7, skip_col], z[4, :, skip_col], blank], axis=0)
        return jnp.concatenate(parts + [jnp.concatenate([even, odd], axis=1)], axis=0)

    lo, hi = shifted(
        side(slice(TILE - 2, TILE), slice(TILE - 1, TILE)), side(slice(0, 2), slice(0, 1)), "col"
    )
    row = lax.axis_index("row")
    pos = jnp.stack(
        [row, lax.axis_index("col"), jnp.int32(TILE * rows), jnp.int32(TILE * cols), row % 2]
    ).astype(jnp.int32)
    mix4c, pg3c, keep, send = local_work(
        scale, pos, z, up, down, lo, hi, bot_kernel, up_kernel, lvl_kernel
    )
    level_out, bottom_grad = rest_work(mix4c, pg3c, bot_kernel, lvl_kernel)
    up_grad, bot_grad, lvl_grad = unpack(pos, *total_over_devices(keep, send))
    return (
        level_out,
        bottom_grad,
        lvl_grad.reshape(3, 3, 128, 128),
        up_grad.reshape(4, 4, 256, 128),
        bot_grad.reshape(3, 3, 256, 256),
    )


def solution(mesh):
    return jax.shard_map(
        on_device,
        mesh=mesh,
        in_specs=(
            P("row", "col", None),
            P("row", "col", None),
            P("row", "col", None),
            P(),
            P(),
            P(),
        ),
        out_specs=(P("row", "col", None), P("row", "col", None), P(), P(), P()),
        check_vma=False,
    )
```

```python
import functools

import jax
import jax.numpy as jnp
from jax import lax
from jax.experimental import pallas as pl
from jax.experimental.pallas import tpu as pltpu
from jax.sharding import PartitionSpec as P

AXES = ("row", "col")
F32 = jnp.float32
BF16 = jnp.bfloat16
TILE = 16
EXT = TILE + 4
PITCH = 32
CORE = 8
WHOLE = 62 << 20
HALF = 5120


def place(x, y, z, core):
    row = (((y >> 1) & 1) * 4 + x % 4) * 2 + core
    col = (z % 8) * 2 + (y & 1)
    return row * 16 + col


def device_xyz(device):
    row, col = divmod(device, 16)
    return (row >> 1) & 3, ((row >> 3) << 1) | (col & 1), col >> 1, row & 1


BLOCK = 32
BLOCK_GROUPS = [
    [place(x, y, z + dz, core) for dz in range(2) for x in range(4) for y in range(4)]
    for z in range(0, 8, 2)
    for core in range(2)
]


def depth_shift(step):
    moves = []
    for device in range(256):
        x, y, z, core = device_xyz(device)
        moves.append((device, place(x, y, z + step, core)))
    return moves


CORE_SWAP = [(i, i ^ 1) for i in range(16)]
INNER_PAIRS = CORE_SWAP
OUTER_PAIRS = [pair for i in range(1, 15, 2) for pair in ((i, i + 1), (i + 1, i))]


def split_kernel(
    bot_hbm, skip_hbm, cot_hbm, out_hbm, inner_hbm, outer_hbm,
    bot, skip, cot, wide, out_ref, inner_ref, outer_ref, sems, out_sems,
):
    even = lax.rem(lax.axis_index("row"), 2) == 0
    copies = [
        pltpu.make_async_copy(src, dst, sems.at[i])
        for i, (src, dst) in enumerate(((cot_hbm, cot), (skip_hbm, skip), (bot_hbm, bot)))
    ]
    for copy in copies:
        copy.start()
    for plane, ref, copy in ((1, cot, copies[0]), (3, skip, copies[1])):
        copy.wait()
        wide[...] = ref[...].astype(F32)
        for col_par in range(2):
            part = wide[:, pl.ds(col_par, TILE, stride=2), :].astype(BF16)
            part = part.reshape(TILE, 2, TILE, 128)
            lanes = slice(col_par * 128, col_par * 128 + 128)
            out_ref[plane, :, :, lanes] = part[:, 0]
            out_ref[plane + 1, :, :, lanes] = part[:, 1]
    copies[2].wait()
    out_ref[0] = bot[...]
    for plane in range(3):
        two = slice(2 * plane, 2 * plane + 2)
        last, first = out_ref[plane, TILE - 2 : TILE], out_ref[plane, 0:2]
        inner_ref[two] = jnp.where(even, last, first)
        outer_ref[two] = jnp.where(even, first, last)
    last, first = out_ref[4, TILE - 1], out_ref[3, 0]
    inner_ref[6] = jnp.where(even, last, first)
    outer_ref[6] = jnp.where(even, first, last)
    copies = [
        pltpu.make_async_copy(src, dst, out_sems.at[i])
        for i, (src, dst) in enumerate(
            ((inner_ref, inner_hbm), (outer_ref, outer_hbm), (out_ref, out_hbm))
        )
    ]
    for copy in copies:
        copy.start()
    for copy in copies:
        copy.wait()


def split(bottom_in, skip_feat, cotangent):
    anywhere = pl.BlockSpec(memory_space=pl.ANY)
    fine = (2 * TILE, 2 * TILE, 128)
    shapes = ((5, TILE, TILE, 256), (7, TILE, 256), (7, TILE, 256))
    return pl.pallas_call(
        split_kernel,
        out_shape=tuple(jax.ShapeDtypeStruct(shape, BF16) for shape in shapes),
        in_specs=[anywhere] * 3,
        out_specs=(anywhere,) * 3,
        scratch_shapes=[
            pltpu.VMEM((TILE, TILE, 256), BF16),
            pltpu.VMEM(fine, BF16),
            pltpu.VMEM(fine, BF16),
            pltpu.VMEM(fine, F32),
        ]
        + [pltpu.VMEM(shape, BF16) for shape in shapes]
        + [pltpu.SemaphoreType.DMA((3,)), pltpu.SemaphoreType.DMA((3,))],
        compiler_params=pltpu.CompilerParams(vmem_limit_bytes=WHOLE),
    )(bottom_in, skip_feat, cotangent)


def nn(a, b):
    return lax.dot_general(a, b, (((1,), (0,)), ((), ())), preferred_element_type=F32)


def nt(a, b):
    return lax.dot_general(a, b, (((1,), (1,)), ((), ())), preferred_element_type=F32)


def tn(a, b):
    return lax.dot_general(a, b, (((0,), (0,)), ((), ())), preferred_element_type=F32)


def flat(x):
    return x.reshape(-1, x.shape[-1])


def left(x):
    return pltpu.roll(x, 1, 0)


def right(x):
    return pltpu.roll(x, x.shape[0] - 1, 0)


def core_of(x):
    rows = x.shape[0] // PITCH
    return x.reshape(rows, PITCH, x.shape[1])[:, CORE : CORE + TILE]


def three(x):
    return (left(x), x, right(x))


def four(x):
    return (left(x[:, 128:]), x, right(x[:, :128]))


def fine_row(offset):
    return offset % 2, offset // 2


def pair_weight(taps, zero):
    first = jnp.concatenate([taps[0], taps[1], taps[2], zero], axis=0)
    second = jnp.concatenate([zero, taps[0], taps[1], taps[2]], axis=0)
    return jnp.concatenate([first, second], axis=1)


def pair_weight_back(taps, zero):
    first = jnp.concatenate([taps[0], taps[1], taps[2], zero], axis=1)
    second = jnp.concatenate([zero, taps[0], taps[1], taps[2]], axis=1)
    return jnp.concatenate([first, second], axis=0)


def main_kernel(
    scale, pos_ref, z_hbm, up_hbm, down_hbm, lo_hbm, hi_hbm, bk_hbm, uk_hbm, lk_hbm,
    mix4c_hbm, pg3c_hbm, keep_ref, send_ref,
    ext, bot3, botc, act3, actc, dsilu, cot4, mg4, mg4c, pgc, packed, sems,
    mix4c, pg3c, z_ref, up_ref, down_ref, lo_ref, hi_ref, bk_ref, uk_ref, lk_ref, in_sems, out_sems,
):
    loads = [
        pltpu.make_async_copy(src, dst, in_sems.at[i])
        for i, (src, dst) in enumerate(
            (
                (z_hbm, z_ref),
                (up_hbm, up_ref),
                (down_hbm, down_ref),
                (lo_hbm, lo_ref),
                (hi_hbm, hi_ref),
                (bk_hbm, bk_ref),
                (lk_hbm, lk_ref),
                (uk_hbm, uk_ref),
            )
        )
    ]
    for copy in loads:
        copy.start()
    row0 = pos_ref[0] * TILE
    col0 = pos_ref[1] * TILE
    image_h = pos_ref[2]
    image_w = pos_ref[3]
    mine = pos_ref[4]

    core = slice(CORE, CORE + TILE)
    ext[...] = jnp.zeros_like(ext)
    for copy in loads[:5]:
        copy.wait()
    ext[:, 2 : 2 + TILE, core, :] = z_ref[...].astype(F32)
    for plane in range(3):
        two = slice(2 * plane, 2 * plane + 2)
        ext[plane, 0:2, core, :] = up_ref[two].astype(F32)
        ext[plane, 2 + TILE : EXT, core, :] = down_ref[two].astype(F32)
        side = slice(EXT * plane, EXT * plane + EXT)
        ext[plane, :, CORE - 2 : CORE, :] = lo_ref[side].astype(F32)
        ext[plane, :, CORE + TILE : CORE + TILE + 2, :] = hi_ref[side].astype(F32)
    ext[4, 1, core, :] = up_ref[6].astype(F32)
    ext[3, 2 + TILE, core, :] = down_ref[6].astype(F32)
    for par in range(2):
        side = slice(3 * EXT, 3 * EXT + 18)
        ext[3 + par, 1:19, CORE - 1 : CORE, :] = lo_ref[side, par : par + 1].astype(F32)
        ext[3 + par, 1:19, CORE + TILE : CORE + TILE + 1, :] = hi_ref[
            side, par : par + 1
        ].astype(F32)

    def masked(x, first):
        rows = x.shape[0] // PITCH
        x = x.reshape(rows, PITCH, x.shape[1])
        i = lax.broadcasted_iota(jnp.int32, x.shape, 0) + (row0 + first - 2)
        w = lax.broadcasted_iota(jnp.int32, x.shape, 1)
        j = w + (col0 - CORE)
        keep = (i >= 0) & (i < image_h) & (j >= 0) & (j < image_w)
        keep = keep & (w >= CORE - 2) & (w < CORE + TILE + 2)
        return flat(jnp.where(keep, x, 0.0))

    zero = jnp.zeros((128, 128), BF16)

    for b, part in enumerate(three(flat(ext[0]))):
        lanes = slice(256 * b, 256 * b + 256)
        bot3[:, :, lanes] = part.reshape(EXT, PITCH, 256).astype(BF16)
        botc[:, :, lanes] = core_of(part)[1 : 19].astype(BF16)
    loads[5].wait()
    pre = jnp.zeros((18 * PITCH, 256), F32)
    for a in range(3):
        pre = pre + nn(flat(bot3[a : a + 18]), bk_ref[a].reshape(768, 256))
    sigma = jax.nn.sigmoid(pre)
    dsilu[...] = sigma * (1.0 + pre * (1.0 - sigma))
    activ = masked((pre * sigma).astype(BF16).astype(F32), 1)
    act3[0] = jnp.zeros((PITCH, 768), BF16)
    act3[EXT - 1] = jnp.zeros((PITCH, 768), BF16)
    for b, part in enumerate(three(activ)):
        act3[1:19, :, 256 * b : 256 * b + 256] = part.reshape(18, PITCH, 256).astype(BF16)
    actc[...] = flat(core_of(activ)[1:17]).astype(BF16)

    for par in range(2):
        a, b, c = four(flat(ext[1 + par]))
        cot4[par, :, :, 0:128] = a.reshape(EXT, PITCH, 128).astype(BF16)
        cot4[par, :, :, 128:384] = b.reshape(EXT, PITCH, 256).astype(BF16)
        cot4[par, :, :, 384:512] = c.reshape(EXT, PITCH, 128).astype(BF16)
    loads[6].wait()
    for par in range(2):
        first = 1 - par
        total = jnp.zeros((19 * PITCH, 256), F32)
        for a in range(3):
            src, shift = fine_row(par + a - 1)
            weight = pair_weight_back([lk_ref[2 - a, 2 - b] for b in range(3)], zero)
            total = total + nt(flat(cot4[src, first + shift : first + shift + 19]), weight)
        grad = masked(total.astype(BF16).astype(F32), first)
        a, b, c = four(grad)
        mg4[par, first : first + 19, :, 0:128] = a.reshape(19, PITCH, 128).astype(BF16)
        mg4[par, first : first + 19, :, 128:384] = b.reshape(19, PITCH, 256).astype(BF16)
        mg4[par, first : first + 19, :, 384:512] = c.reshape(19, PITCH, 128).astype(BF16)
        mg4c[par, first : first + 19, :, 0:128] = core_of(a).astype(BF16)
        mg4c[par, first : first + 19, :, 128:384] = core_of(b).astype(BF16)
        mg4c[par, first : first + 19, :, 384:512] = core_of(c).astype(BF16)

    def put(half, row, value):
        packed[half, row : row + value.shape[0], :] = (value * scale).astype(BF16)

    def hand_out(number, half, first, count, act):
        rows = pl.ds(first, count)
        for which in range(2):

            @pl.when(mine == which)
            def _():
                out = keep_ref if half == which else send_ref
                act(pltpu.make_async_copy(packed.at[half, rows], out.at[rows], sems.at[number]))

    parts = ((0, 0, 0, 4096), (1, 1, 0, 4608), (2, 0, 4096, HALF - 4096), (3, 1, 4608, HALF - 4608))

    act_t = actc[...].T
    for a in range(4):
        src, shift = fine_row(a - 1)
        prod = nn(act_t, flat(mg4c[src, 2 + shift : 18 + shift]))
        for b in range(4):
            put(0, (4 * a + b) * 256, prod[:, 128 * b : 128 * b + 128])
    hand_out(*parts[0], lambda copy: copy.start())

    loads[7].wait()
    agrad = jnp.zeros((18 * PITCH, 256), F32)
    for a in range(4):
        src, shift = fine_row(a - 1)
        weight = jnp.concatenate([uk_ref[a, b] for b in range(4)], axis=1)
        agrad = agrad + nt(flat(mg4[src, 1 + shift : 19 + shift]), weight)
    pgrad = masked((agrad * dsilu[...]).astype(BF16).astype(F32), 1)
    for b, part in enumerate(three(pgrad)):
        pg3c[:, :, 256 * b : 256 * b + 256] = core_of(part).astype(BF16)
    pgc[...] = flat(core_of(pgrad)[1:17]).astype(BF16)

    rest = [
        pltpu.make_async_copy(pg3c, pg3c_hbm, out_sems.at[0]),
        pltpu.make_async_copy(mix4c, mix4c_hbm, out_sems.at[1]),
    ]
    rest[0].start()

    for a in range(3):
        prod = tn(flat(botc[a : a + 16]), pgc[...])
        put(1, 768 * a, prod[:, :128])
        put(1, 2304 + 768 * a, prod[:, 128:])
    hand_out(*parts[1], lambda copy: copy.start())

    for par in range(2):
        total = flat(ext[3 + par, 1:19])
        for row_k, shift in (((1, 0), (3, -1)), ((0, 1), (2, 0)))[par]:
            k = [uk_ref[row_k, b] for b in range(4)]
            none = jnp.zeros((256, 128), BF16)
            weight = jnp.concatenate(
                [
                    jnp.concatenate([k[3], k[1], none], axis=0),
                    jnp.concatenate([none, k[2], k[0]], axis=0),
                ],
                axis=1,
            )
            total = total + nn(flat(act3[1 + shift : 19 + shift]), weight)
        mixed = masked(total.astype(BF16).astype(F32), 1)
        a, b, c = four(mixed)
        mix4c[par, :, :, 0:128] = core_of(a).astype(BF16)
        mix4c[par, :, :, 128:384] = core_of(b).astype(BF16)
        mix4c[par, :, :, 384:512] = core_of(c).astype(BF16)

    rest[1].start()

    for a in range(3):
        prod = jnp.zeros((512, 256), F32)
        for par in range(2):
            src, shift = fine_row(par + a - 1)
            prod = prod + tn(
                flat(mix4c[src, 1 + shift : 17 + shift]), flat(z_ref[1 + par])
            )
        for b in range(3):
            tap = prod[128 * b : 128 * b + 128, :128] + prod[128 * b + 128 : 128 * b + 256, 128:]
            if a < 2:
                put(0, 4096 + (3 * a + b) * 128, tap)
            else:
                put(1, 4608 + b * 128, tap)
    put(0, 4864, jnp.zeros((HALF - 4864, 128), F32))
    put(1, 4992, jnp.zeros((HALF - 4992, 128), F32))

    for part in parts[2:]:
        hand_out(*part, lambda copy: copy.start())
    for part in parts:
        hand_out(*part, lambda copy: copy.wait())
    for copy in rest:
        copy.wait()


def rest_kernel(mix4c, pg3c, bk_ref, lk_ref, level_ref, bgrad_ref, inter):
    zero = jnp.zeros((128, 128), BF16)

    for par in range(2):
        total = jnp.zeros((TILE * TILE, 256), F32)
        for a in range(3):
            src, shift = fine_row(par + a - 1)
            weight = pair_weight([lk_ref[a, b] for b in range(3)], zero)
            total = total + nn(flat(mix4c[src, 1 + shift : 17 + shift]), weight)
        total = total.reshape(TILE, TILE, 256)
        for col_par in range(2):
            inter[:, par, pl.ds(col_par, TILE, stride=2), :] = total[
                :, :, 128 * col_par : 128 * col_par + 128
            ]
    level_ref[...] = inter[...].reshape(2 * TILE, 2 * TILE, 128).astype(BF16)

    total = jnp.zeros((TILE * TILE, 256), F32)
    for a in range(3):
        weight = jnp.concatenate([bk_ref[2 - a, 2 - b] for b in range(3)], axis=1)
        total = total + nt(flat(pg3c[a : a + 16]), weight)
    bgrad_ref[...] = total.reshape(TILE, TILE, 256).astype(BF16)


def rest_work(mix4c, pg3c, bot_kernel, lvl_kernel):
    return pl.pallas_call(
        rest_kernel,
        out_shape=(
            jax.ShapeDtypeStruct((2 * TILE, 2 * TILE, 128), BF16),
            jax.ShapeDtypeStruct((TILE, TILE, 256), BF16),
        ),
        scratch_shapes=[pltpu.VMEM((TILE, 2, 2 * TILE, 128), F32)],
        compiler_params=pltpu.CompilerParams(vmem_limit_bytes=16 << 20),
        cost_estimate=pl.CostEstimate(
            flops=1000000000, bytes_accessed=3000000, transcendentals=0
        ),
    )(mix4c, pg3c, bot_kernel, lvl_kernel)


def local_work(scale, pos, z, up, down, lo, hi, bot_kernel, up_kernel, lvl_kernel):
    anywhere = pl.BlockSpec(memory_space=pl.ANY)
    operands = (z, up, down, lo, hi, bot_kernel, up_kernel, lvl_kernel)
    shapes = ((2, 18, TILE, 512), (18, TILE, 768), (HALF, 128), (HALF, 128))
    return pl.pallas_call(
        functools.partial(main_kernel, scale),
        out_shape=tuple(jax.ShapeDtypeStruct(shape, BF16) for shape in shapes),
        in_specs=[pl.BlockSpec(memory_space=pltpu.SMEM)] + [anywhere] * len(operands),
        out_specs=(anywhere,) * len(shapes),
        scratch_shapes=[
            pltpu.VMEM((5, EXT, PITCH, 256), F32),
            pltpu.VMEM((EXT, PITCH, 768), BF16),
            pltpu.VMEM((18, TILE, 768), BF16),
            pltpu.VMEM((EXT, PITCH, 768), BF16),
            pltpu.VMEM((TILE * TILE, 256), BF16),
            pltpu.VMEM((18 * PITCH, 256), F32),
            pltpu.VMEM((2, EXT, PITCH, 512), BF16),
            pltpu.VMEM((2, EXT, PITCH, 512), BF16),
            pltpu.VMEM((2, EXT, TILE, 512), BF16),
            pltpu.VMEM((TILE * TILE, 256), BF16),
            pltpu.VMEM((2, HALF, 128), BF16),
            pltpu.SemaphoreType.DMA((4,)),
        ]
        + [pltpu.VMEM(shape, BF16) for shape in shapes[:2]]
        + [pltpu.VMEM(x.shape, BF16) for x in operands]
        + [pltpu.SemaphoreType.DMA((len(operands),)), pltpu.SemaphoreType.DMA((2,))],
        compiler_params=pltpu.CompilerParams(vmem_limit_bytes=WHOLE),
    )(pos, *operands)


def unpack_kernel(
    pos_ref, half, other, up_hbm, bot_hbm, lvl_hbm, up, bot, lvl, sems
):
    copies = []

    def send(src, dst):
        copy = pltpu.make_async_copy(src, dst, sems.at[len(copies)])
        copy.start()
        copies.append(copy)

    own_even = pos_ref[4] == 0

    def rows(parity, first, count):
        at = slice(first, first + count)
        mine, theirs = (half, other) if parity == 0 else (other, half)
        return jnp.where(own_even, mine[at], theirs[at]).astype(F32)

    step = 1024
    for first in range(0, 4096, step):
        up[first : first + step] = rows(0, first, step)
        send(up.at[pl.ds(first, step)], up_hbm.at[pl.ds(first, step)])
    step = 768
    for first in range(0, 2304, step):
        bot[first : first + step, 0:128] = rows(1, first, step)
        bot[first : first + step, 128:256] = rows(1, 2304 + first, step)
        send(bot.at[pl.ds(first, step)], bot_hbm.at[pl.ds(first, step)])
    lvl[0:768] = rows(0, 4096, 768)
    lvl[768:1152] = rows(1, 4608, 384)
    send(lvl, lvl_hbm)
    for copy in copies:
        copy.wait()


def unpack(pos, half, other):
    vmem = pl.BlockSpec(memory_space=pltpu.VMEM)
    anywhere = pl.BlockSpec(memory_space=pl.ANY)
    shapes = ((4096, 128), (2304, 256), (1152, 128))
    return pl.pallas_call(
        unpack_kernel,
        out_shape=tuple(jax.ShapeDtypeStruct(shape, F32) for shape in shapes),
        in_specs=[pl.BlockSpec(memory_space=pltpu.SMEM), vmem, vmem],
        out_specs=(anywhere,) * 3,
        scratch_shapes=[pltpu.VMEM(shape, F32) for shape in shapes]
        + [pltpu.SemaphoreType.DMA((8,))],
        compiler_params=pltpu.CompilerParams(vmem_limit_bytes=16 << 20),
    )(pos, half, other)


def swapped(inner, outer, axis):
    got_inner = lax.ppermute(inner, axis, INNER_PAIRS)
    got_outer = lax.ppermute(outer, axis, OUTER_PAIRS)
    even = lax.rem(lax.axis_index(axis), 2) == 0
    return jnp.where(even, got_outer, got_inner), jnp.where(even, got_inner, got_outer)


def exchange(x):
    return lax.all_to_all(x, AXES, 0, 0, axis_index_groups=BLOCK_GROUPS)


def total_over_devices(keep, send):
    got = lax.ppermute(send, "row", CORE_SWAP)
    half = (keep.astype(F32) + got.astype(F32)).astype(BF16)
    parts = exchange(half.reshape(BLOCK, HALF // BLOCK, 128))
    part = jnp.sum(parts.astype(F32), axis=0).astype(BF16)
    planes = [lax.ppermute(part, AXES, depth_shift(step)) for step in (2, 6, 4)]
    pair = lax.axis_index("col") // 4
    terms = [part] + planes
    places = [pair, (pair + 3) % 4, (pair + 1) % 4, (pair + 2) % 4]
    total = jnp.zeros(part.shape, F32)
    for slot in range(4):
        for term, where in zip(terms, places):
            total = total + jnp.where(where == slot, term.astype(F32), 0.0)
    total = total.astype(BF16)
    half = exchange(jnp.broadcast_to(total[None], parts.shape)).reshape(HALF, 128)
    return half, lax.ppermute(half, "row", CORE_SWAP)


def on_device(bottom_in, skip_feat, cotangent, bot_kernel, up_kernel, lvl_kernel):
    rows, cols = lax.axis_size("row"), lax.axis_size("col")
    scale = 1.0 / float(2 * TILE * rows * 2 * TILE * cols) ** 0.5
    z, inner, outer = split(bottom_in, skip_feat, cotangent)
    up, down = swapped(inner, outer, "row")

    def side(cols, skip_col):
        parts = [
            jnp.concatenate(
                [up[2 * p : 2 * p + 2, cols], z[p, :, cols], down[2 * p : 2 * p + 2, cols]], axis=0
            )
            for p in range(3)
        ]
        blank = jnp.zeros((1, 1, 256), BF16)
        even = jnp.concatenate([blank, z[3, :, skip_col], down[6:7, skip_col]], axis=0)
        odd = jnp.concatenate([up[6:7, skip_col], z[4, :, skip_col], blank], axis=0)
        return jnp.concatenate(parts + [jnp.concatenate([even, odd], axis=1)], axis=0)

    last = side(slice(TILE - 2, TILE), slice(TILE - 1, TILE))
    first = side(slice(0, 2), slice(0, 1))
    even = lax.rem(lax.axis_index("col"), 2) == 0
    lo, hi = swapped(jnp.where(even, last, first), jnp.where(even, first, last), "col")
    row = lax.axis_index("row")
    pos = jnp.stack(
        [row, lax.axis_index("col"), jnp.int32(TILE * rows), jnp.int32(TILE * cols), row % 2]
    ).astype(jnp.int32)
    mix4c, pg3c, keep, send = local_work(
        scale, pos, z, up, down, lo, hi, bot_kernel, up_kernel, lvl_kernel
    )
    level_out, bottom_grad = rest_work(mix4c, pg3c, bot_kernel, lvl_kernel)
    up_grad, bot_grad, lvl_grad = unpack(pos, *total_over_devices(keep, send))
    return (
        level_out,
        bottom_grad,
        lvl_grad.reshape(3, 3, 128, 128),
        up_grad.reshape(4, 4, 256, 128),
        bot_grad.reshape(3, 3, 256, 256),
    )


def solution(mesh):
    return jax.shard_map(
        on_device,
        mesh=mesh,
        in_specs=(
            P("row", "col", None),
            P("row", "col", None),
            P("row", "col", None),
            P(),
            P(),
            P(),
        ),
        out_specs=(P("row", "col", None), P("row", "col", None), P(), P(), P()),
        check_vma=False,
    )
```

```python
import functools

import jax
import jax.numpy as jnp
from jax import lax
from jax.experimental import pallas as pl
from jax.experimental.pallas import tpu as pltpu
from jax.sharding import PartitionSpec as P

AXES = ("row", "col")
F32 = jnp.float32
BF16 = jnp.bfloat16
TILE = 16
EXT = TILE + 4
PITCH = 32
CORE = 8
MAIN_LIMIT = 40 << 20
HALF = 5120


def place(x, y, z, core):
    row = (((y >> 1) & 1) * 4 + x % 4) * 2 + core
    col = (z % 8) * 2 + (y & 1)
    return row * 16 + col


def device_xyz(device):
    row, col = divmod(device, 16)
    return (row >> 1) & 3, ((row >> 3) << 1) | (col & 1), col >> 1, row & 1


BLOCK = 32
BLOCK_GROUPS = [
    [place(x, y, z + dz, core) for dz in range(2) for x in range(4) for y in range(4)]
    for z in range(0, 8, 2)
    for core in range(2)
]


def depth_shift(step):
    moves = []
    for device in range(256):
        x, y, z, core = device_xyz(device)
        moves.append((device, place(x, y, z + step, core)))
    return moves


CORE_SWAP = [(i, i ^ 1) for i in range(16)]
INNER_PAIRS = CORE_SWAP
OUTER_PAIRS = [pair for i in range(1, 15, 2) for pair in ((i, i + 1), (i + 1, i))]


def split_kernel(bot, skip, cot, out_ref, inner_ref, outer_ref, wide):
    even = lax.rem(lax.axis_index("row"), 2) == 0
    for plane, ref in ((1, cot), (3, skip)):
        wide[...] = ref[...].astype(F32)
        for col_par in range(2):
            part = wide[:, pl.ds(col_par, TILE, stride=2), :].astype(BF16)
            part = part.reshape(TILE, 2, TILE, 128)
            lanes = slice(col_par * 128, col_par * 128 + 128)
            out_ref[plane, :, :, lanes] = part[:, 0]
            out_ref[plane + 1, :, :, lanes] = part[:, 1]
    out_ref[0] = bot[...]
    for plane in range(3):
        two = slice(2 * plane, 2 * plane + 2)
        last, first = out_ref[plane, TILE - 2 : TILE], out_ref[plane, 0:2]
        inner_ref[two] = jnp.where(even, last, first)
        outer_ref[two] = jnp.where(even, first, last)
    last, first = out_ref[4, TILE - 1], out_ref[3, 0]
    inner_ref[6] = jnp.where(even, last, first)
    outer_ref[6] = jnp.where(even, first, last)


def split(bottom_in, skip_feat, cotangent):
    vmem = pl.BlockSpec(memory_space=pltpu.VMEM)
    shapes = ((5, TILE, TILE, 256), (7, TILE, 256), (7, TILE, 256))
    return pl.pallas_call(
        split_kernel,
        out_shape=tuple(jax.ShapeDtypeStruct(shape, BF16) for shape in shapes),
        in_specs=[vmem] * 3,
        out_specs=(vmem,) * 3,
        scratch_shapes=[pltpu.VMEM((2 * TILE, 2 * TILE, 128), F32)],
        compiler_params=pltpu.CompilerParams(vmem_limit_bytes=16 << 20),
    )(bottom_in, skip_feat, cotangent)


def nn(a, b):
    return lax.dot_general(a, b, (((1,), (0,)), ((), ())), preferred_element_type=F32)


def nt(a, b):
    return lax.dot_general(a, b, (((1,), (1,)), ((), ())), preferred_element_type=F32)


def tn(a, b):
    return lax.dot_general(a, b, (((0,), (0,)), ((), ())), preferred_element_type=F32)


def flat(x):
    return x.reshape(-1, x.shape[-1])


def left(x):
    return pltpu.roll(x, 1, 0)


def right(x):
    return pltpu.roll(x, x.shape[0] - 1, 0)


def core_of(x):
    rows = x.shape[0] // PITCH
    return x.reshape(rows, PITCH, x.shape[1])[:, CORE : CORE + TILE]


def three(x):
    return (left(x), x, right(x))


def four(x):
    return (left(x[:, 128:]), x, right(x[:, :128]))


def fine_row(offset):
    return offset % 2, offset // 2


def pair_weight(taps, zero):
    first = jnp.concatenate([taps[0], taps[1], taps[2], zero], axis=0)
    second = jnp.concatenate([zero, taps[0], taps[1], taps[2]], axis=0)
    return jnp.concatenate([first, second], axis=1)


def pair_weight_back(taps, zero):
    first = jnp.concatenate([taps[0], taps[1], taps[2], zero], axis=1)
    second = jnp.concatenate([zero, taps[0], taps[1], taps[2]], axis=1)
    return jnp.concatenate([first, second], axis=0)


def main_kernel(
    scale, pos_ref, z_ref, up_ref, down_ref, lo_ref, hi_ref, bk_ref, uk_ref, flip_ref,
    mix4c, pg3c, keep_ref, send_ref,
    ext, bot3, botc, act3, actc, dsilu, cot4, mg4, mg4c, pgc, packed, sems,
):
    row0 = pos_ref[0] * TILE
    col0 = pos_ref[1] * TILE
    image_h = pos_ref[2]
    image_w = pos_ref[3]
    mine = pos_ref[4]

    core = slice(CORE, CORE + TILE)
    ext[...] = jnp.zeros_like(ext)
    ext[:, 2 : 2 + TILE, core, :] = z_ref[...].astype(F32)
    for plane in range(3):
        two = slice(2 * plane, 2 * plane + 2)
        ext[plane, 0:2, core, :] = up_ref[two].astype(F32)
        ext[plane, 2 + TILE : EXT, core, :] = down_ref[two].astype(F32)
        side = slice(EXT * plane, EXT * plane + EXT)
        ext[plane, :, CORE - 2 : CORE, :] = lo_ref[side].astype(F32)
        ext[plane, :, CORE + TILE : CORE + TILE + 2, :] = hi_ref[side].astype(F32)
    ext[4, 1, core, :] = up_ref[6].astype(F32)
    ext[3, 2 + TILE, core, :] = down_ref[6].astype(F32)
    for par in range(2):
        side = slice(3 * EXT, 3 * EXT + 18)
        ext[3 + par, 1:19, CORE - 1 : CORE, :] = lo_ref[side, par : par + 1].astype(F32)
        ext[3 + par, 1:19, CORE + TILE : CORE + TILE + 1, :] = hi_ref[
            side, par : par + 1
        ].astype(F32)

    def masked(x, first):
        rows = x.shape[0] // PITCH
        x = x.reshape(rows, PITCH, x.shape[1])
        i = lax.broadcasted_iota(jnp.int32, x.shape, 0) + (row0 + first - 2)
        w = lax.broadcasted_iota(jnp.int32, x.shape, 1)
        j = w + (col0 - CORE)
        keep = (i >= 0) & (i < image_h) & (j >= 0) & (j < image_w)
        keep = keep & (w >= CORE - 2) & (w < CORE + TILE + 2)
        return flat(jnp.where(keep, x, 0.0))

    zero = jnp.zeros((128, 128), BF16)

    for b, part in enumerate(three(flat(ext[0]))):
        lanes = slice(256 * b, 256 * b + 256)
        bot3[:, :, lanes] = part.reshape(EXT, PITCH, 256).astype(BF16)
        botc[:, :, lanes] = core_of(part)[1 : 19].astype(BF16)
    pre = jnp.zeros((18 * PITCH, 256), F32)
    for a in range(3):
        pre = pre + nn(flat(bot3[a : a + 18]), bk_ref[a].reshape(768, 256))
    sigma = jax.nn.sigmoid(pre)
    dsilu[...] = sigma * (1.0 + pre * (1.0 - sigma))
    activ = masked((pre * sigma).astype(BF16).astype(F32), 1)
    act3[0] = jnp.zeros((PITCH, 768), BF16)
    act3[EXT - 1] = jnp.zeros((PITCH, 768), BF16)
    for b, part in enumerate(three(activ)):
        act3[1:19, :, 256 * b : 256 * b + 256] = part.reshape(18, PITCH, 256).astype(BF16)
    actc[...] = flat(core_of(activ)[1:17]).astype(BF16)

    for par in range(2):
        a, b, c = four(flat(ext[1 + par]))
        cot4[par, :, :, 0:128] = a.reshape(EXT, PITCH, 128).astype(BF16)
        cot4[par, :, :, 128:384] = b.reshape(EXT, PITCH, 256).astype(BF16)
        cot4[par, :, :, 384:512] = c.reshape(EXT, PITCH, 128).astype(BF16)
    for par in range(2):
        first = 1 - par
        total = jnp.zeros((19 * PITCH, 256), F32)
        for a in range(3):
            src, shift = fine_row(par + a - 1)
            weight = pair_weight_back([flip_ref[a, b] for b in range(3)], zero)
            total = total + nt(flat(cot4[src, first + shift : first + shift + 19]), weight)
        grad = masked(total.astype(BF16).astype(F32), first)
        a, b, c = four(grad)
        mg4[par, first : first + 19, :, 0:128] = a.reshape(19, PITCH, 128).astype(BF16)
        mg4[par, first : first + 19, :, 128:384] = b.reshape(19, PITCH, 256).astype(BF16)
        mg4[par, first : first + 19, :, 384:512] = c.reshape(19, PITCH, 128).astype(BF16)
        mg4c[par, first : first + 19, :, 0:128] = core_of(a).astype(BF16)
        mg4c[par, first : first + 19, :, 128:384] = core_of(b).astype(BF16)
        mg4c[par, first : first + 19, :, 384:512] = core_of(c).astype(BF16)

    def put(half, row, value):
        packed[half, row : row + value.shape[0], :] = (value * scale).astype(BF16)

    def hand_out(number, half, first, count, act):
        rows = pl.ds(first, count)
        for which in range(2):

            @pl.when(mine == which)
            def _():
                out = keep_ref if half == which else send_ref
                act(pltpu.make_async_copy(packed.at[half, rows], out.at[rows], sems.at[number]))

    parts = ((0, 0, 0, 4096), (1, 1, 0, 4608), (2, 0, 4096, HALF - 4096), (3, 1, 4608, HALF - 4608))

    act_t = actc[...].T
    for a in range(4):
        src, shift = fine_row(a - 1)
        prod = nn(act_t, flat(mg4c[src, 2 + shift : 18 + shift]))
        for b in range(4):
            put(0, (4 * a + b) * 256, prod[:, 128 * b : 128 * b + 128])
    hand_out(*parts[0], lambda copy: copy.start())

    agrad = jnp.zeros((18 * PITCH, 256), F32)
    for a in range(4):
        src, shift = fine_row(a - 1)
        weight = jnp.concatenate([uk_ref[a, b] for b in range(4)], axis=1)
        agrad = agrad + nt(flat(mg4[src, 1 + shift : 19 + shift]), weight)
    pgrad = masked((agrad * dsilu[...]).astype(BF16).astype(F32), 1)
    for b, part in enumerate(three(pgrad)):
        pg3c[:, :, 256 * b : 256 * b + 256] = core_of(part).astype(BF16)
    pgc[...] = flat(core_of(pgrad)[1:17]).astype(BF16)

    for a in range(3):
        prod = tn(flat(botc[a : a + 16]), pgc[...])
        put(1, 768 * a, prod[:, :128])
        put(1, 2304 + 768 * a, prod[:, 128:])
    hand_out(*parts[1], lambda copy: copy.start())

    for par in range(2):
        total = flat(ext[3 + par, 1:19])
        for row_k, shift in (((1, 0), (3, -1)), ((0, 1), (2, 0)))[par]:
            k = [uk_ref[row_k, b] for b in range(4)]
            none = jnp.zeros((256, 128), BF16)
            weight = jnp.concatenate(
                [
                    jnp.concatenate([k[3], k[1], none], axis=0),
                    jnp.concatenate([none, k[2], k[0]], axis=0),
                ],
                axis=1,
            )
            total = total + nn(flat(act3[1 + shift : 19 + shift]), weight)
        mixed = masked(total.astype(BF16).astype(F32), 1)
        a, b, c = four(mixed)
        mix4c[par, :, :, 0:128] = core_of(a).astype(BF16)
        mix4c[par, :, :, 128:384] = core_of(b).astype(BF16)
        mix4c[par, :, :, 384:512] = core_of(c).astype(BF16)

    for a in range(3):
        prod = jnp.zeros((512, 256), F32)
        for par in range(2):
            src, shift = fine_row(par + a - 1)
            prod = prod + tn(
                flat(mix4c[src, 1 + shift : 17 + shift]), flat(z_ref[1 + par])
            )
        for b in range(3):
            tap = prod[128 * b : 128 * b + 128, :128] + prod[128 * b + 128 : 128 * b + 256, 128:]
            if a < 2:
                put(0, 4096 + (3 * a + b) * 128, tap)
            else:
                put(1, 4608 + b * 128, tap)
    put(0, 4864, jnp.zeros((HALF - 4864, 128), F32))
    put(1, 4992, jnp.zeros((HALF - 4992, 128), F32))

    for part in parts[2:]:
        hand_out(*part, lambda copy: copy.start())
    for part in parts:
        hand_out(*part, lambda copy: copy.wait())


def rest_kernel(mix4c, pg3c, bk_ref, lk_ref, level_ref, bgrad_ref, inter):
    zero = jnp.zeros((128, 128), BF16)

    for par in range(2):
        total = jnp.zeros((TILE * TILE, 256), F32)
        for a in range(3):
            src, shift = fine_row(par + a - 1)
            weight = pair_weight([lk_ref[a, b] for b in range(3)], zero)
            total = total + nn(flat(mix4c[src, 1 + shift : 17 + shift]), weight)
        total = total.reshape(TILE, TILE, 256)
        for col_par in range(2):
            inter[:, par, pl.ds(col_par, TILE, stride=2), :] = total[
                :, :, 128 * col_par : 128 * col_par + 128
            ]
    level_ref[...] = inter[...].reshape(2 * TILE, 2 * TILE, 128).astype(BF16)

    total = jnp.zeros((TILE * TILE, 256), F32)
    for a in range(3):
        weight = jnp.concatenate([bk_ref[2 - a, 2 - b] for b in range(3)], axis=1)
        total = total + nt(flat(pg3c[a : a + 16]), weight)
    bgrad_ref[...] = total.reshape(TILE, TILE, 256).astype(BF16)


def rest_work(mix4c, pg3c, bot_kernel, lvl_kernel):
    return pl.pallas_call(
        rest_kernel,
        out_shape=(
            jax.ShapeDtypeStruct((2 * TILE, 2 * TILE, 128), BF16),
            jax.ShapeDtypeStruct((TILE, TILE, 256), BF16),
        ),
        scratch_shapes=[pltpu.VMEM((TILE, 2, 2 * TILE, 128), F32)],
        compiler_params=pltpu.CompilerParams(vmem_limit_bytes=16 << 20),
        cost_estimate=pl.CostEstimate(
            flops=1000000000, bytes_accessed=3000000, transcendentals=0
        ),
    )(mix4c, pg3c, bot_kernel, lvl_kernel)


def local_work(scale, pos, *operands):
    vmem = pl.BlockSpec(memory_space=pltpu.VMEM)
    anywhere = pl.BlockSpec(memory_space=pl.ANY)
    shapes = ((2, 18, TILE, 512), (18, TILE, 768), (HALF, 128), (HALF, 128))
    return pl.pallas_call(
        functools.partial(main_kernel, scale),
        out_shape=tuple(jax.ShapeDtypeStruct(shape, BF16) for shape in shapes),
        in_specs=[pl.BlockSpec(memory_space=pltpu.SMEM)] + [vmem] * len(operands),
        out_specs=(vmem, vmem, anywhere, anywhere),
        scratch_shapes=[
            pltpu.VMEM((5, EXT, PITCH, 256), F32),
            pltpu.VMEM((EXT, PITCH, 768), BF16),
            pltpu.VMEM((18, TILE, 768), BF16),
            pltpu.VMEM((EXT, PITCH, 768), BF16),
            pltpu.VMEM((TILE * TILE, 256), BF16),
            pltpu.VMEM((18 * PITCH, 256), F32),
            pltpu.VMEM((2, EXT, PITCH, 512), BF16),
            pltpu.VMEM((2, EXT, PITCH, 512), BF16),
            pltpu.VMEM((2, EXT, TILE, 512), BF16),
            pltpu.VMEM((TILE * TILE, 256), BF16),
            pltpu.VMEM((2, HALF, 128), BF16),
            pltpu.SemaphoreType.DMA((4,)),
        ],
        compiler_params=pltpu.CompilerParams(vmem_limit_bytes=MAIN_LIMIT),
    )(pos, *operands)


def unpack_kernel(half_of, pos_ref, half, *refs):
    up_hbm, bot_hbm, lvl_hbm, up, bot, lvl, sems = refs[-7:]

    @pl.when(pos_ref[4] == half_of)
    def _():
        copies = []
        for i in range(4):
            rows = pl.ds(1024 * i, 1024)
            up[rows] = half[rows].astype(F32)
            copies.append(pltpu.make_async_copy(up.at[rows], up_hbm.at[rows], sems.at[i]))
            copies[-1].start()
        rows = pl.ds(0, 768)
        lvl[rows] = half[4096:4864].astype(F32)
        copies.append(pltpu.make_async_copy(lvl.at[rows], lvl_hbm.at[rows], sems.at[4]))
        copies[-1].start()
        for copy in copies:
            copy.wait()

    @pl.when(pos_ref[4] != half_of)
    def _():
        copies = []
        for i in range(3):
            rows = pl.ds(768 * i, 768)
            bot[rows, 0:128] = half[768 * i : 768 * i + 768].astype(F32)
            bot[rows, 128:256] = half[2304 + 768 * i : 3072 + 768 * i].astype(F32)
            copies.append(pltpu.make_async_copy(bot.at[rows], bot_hbm.at[rows], sems.at[i]))
            copies[-1].start()
        rows = pl.ds(768, 384)
        lvl[rows] = half[4608:4992].astype(F32)
        copies.append(pltpu.make_async_copy(lvl.at[rows], lvl_hbm.at[rows], sems.at[3]))
        copies[-1].start()
        for copy in copies:
            copy.wait()


def unpack(pos, half, begun=()):
    vmem = pl.BlockSpec(memory_space=pltpu.VMEM)
    anywhere = pl.BlockSpec(memory_space=pl.ANY)
    shapes = ((4096, 128), (2304, 256), (1152, 128))
    return pl.pallas_call(
        functools.partial(unpack_kernel, 1 if begun else 0),
        out_shape=tuple(jax.ShapeDtypeStruct(shape, F32) for shape in shapes),
        in_specs=[pl.BlockSpec(memory_space=pltpu.SMEM), vmem] + [anywhere] * len(begun),
        out_specs=(anywhere,) * 3,
        scratch_shapes=[pltpu.VMEM(shape, F32) for shape in shapes]
        + [pltpu.SemaphoreType.DMA((5,))],
        input_output_aliases={2 + i: i for i in range(len(begun))},
        compiler_params=pltpu.CompilerParams(vmem_limit_bytes=16 << 20),
        cost_estimate=pl.CostEstimate(flops=0, bytes_accessed=4000000, transcendentals=0),
    )(pos, half, *begun)


def swapped(inner, outer, axis):
    got_inner = lax.ppermute(inner, axis, INNER_PAIRS)
    got_outer = lax.ppermute(outer, axis, OUTER_PAIRS)
    even = lax.rem(lax.axis_index(axis), 2) == 0
    return jnp.where(even, got_outer, got_inner), jnp.where(even, got_inner, got_outer)


def exchange(x):
    return lax.all_to_all(x, AXES, 0, 0, axis_index_groups=BLOCK_GROUPS)


def total_over_devices(keep, send, rest):
    got = lax.ppermute(send, "row", CORE_SWAP)
    half = (keep.astype(F32) + got.astype(F32)).astype(BF16)
    parts = exchange(half.reshape(BLOCK, HALF // BLOCK, 128))
    part = jnp.sum(parts.astype(F32), axis=0).astype(BF16)
    part, rest = lax.optimization_barrier((part, rest))
    planes = [lax.ppermute(part, AXES, depth_shift(step)) for step in (2, 6, 4)]
    pair = lax.axis_index("col") // 4
    terms = [part] + planes
    places = [pair, (pair + 3) % 4, (pair + 1) % 4, (pair + 2) % 4]
    total = jnp.zeros(part.shape, F32)
    for slot in range(4):
        for term, where in zip(terms, places):
            total = total + jnp.where(where == slot, term.astype(F32), 0.0)
    total = total.astype(BF16)
    half = exchange(jnp.broadcast_to(total[None], parts.shape)).reshape(HALF, 128)
    return half, lax.ppermute(half, "row", CORE_SWAP), rest


def on_device(bottom_in, skip_feat, cotangent, bot_kernel, up_kernel, lvl_kernel):
    rows, cols = lax.axis_size("row"), lax.axis_size("col")
    scale = 1.0 / float(2 * TILE * rows * 2 * TILE * cols) ** 0.5
    z, inner, outer = split(bottom_in, skip_feat, cotangent)
    up, down = swapped(inner, outer, "row")

    def side(cols, skip_col):
        parts = [
            jnp.concatenate(
                [up[2 * p : 2 * p + 2, cols], z[p, :, cols], down[2 * p : 2 * p + 2, cols]], axis=0
            )
            for p in range(3)
        ]
        blank = jnp.zeros((1, 1, 256), BF16)
        even = jnp.concatenate([blank, z[3, :, skip_col], down[6:7, skip_col]], axis=0)
        odd = jnp.concatenate([up[6:7, skip_col], z[4, :, skip_col], blank], axis=0)
        return jnp.concatenate(parts + [jnp.concatenate([even, odd], axis=1)], axis=0)

    last = side(slice(TILE - 2, TILE), slice(TILE - 1, TILE))
    first = side(slice(0, 2), slice(0, 1))
    even = lax.rem(lax.axis_index("col"), 2) == 0
    lo, hi = swapped(jnp.where(even, last, first), jnp.where(even, first, last), "col")
    row = lax.axis_index("row")
    pos = jnp.stack(
        [row, lax.axis_index("col"), jnp.int32(TILE * rows), jnp.int32(TILE * cols), row % 2]
    ).astype(jnp.int32)
    flip = lvl_kernel[::-1, ::-1]
    mix4c, pg3c, keep, send = local_work(
        scale, pos, z, up, down, lo, hi, bot_kernel, up_kernel, flip
    )
    rest = rest_work(mix4c, pg3c, bot_kernel, lvl_kernel)
    half, other, (level_out, bottom_grad) = total_over_devices(keep, send, rest)
    up_grad, bot_grad, lvl_grad = unpack(pos, other, unpack(pos, half))
    return (
        level_out,
        bottom_grad,
        lvl_grad.reshape(3, 3, 128, 128),
        up_grad.reshape(4, 4, 256, 128),
        bot_grad.reshape(3, 3, 256, 256),
    )


def solution(mesh):
    return jax.shard_map(
        on_device,
        mesh=mesh,
        in_specs=(
            P("row", "col", None),
            P("row", "col", None),
            P("row", "col", None),
            P(),
            P(),
            P(),
        ),
        out_specs=(P("row", "col", None), P("row", "col", None), P(), P(), P()),
        check_vma=False,
    )
```

```python
import functools

import jax
import jax.numpy as jnp
from jax import lax
from jax.experimental import pallas as pl
from jax.experimental.pallas import tpu as pltpu
from jax.sharding import PartitionSpec as P

AXES = ("row", "col")
F32 = jnp.float32
BF16 = jnp.bfloat16
TILE = 16
EXT = TILE + 4
PITCH = 32
CORE = 8
MAIN_LIMIT = 40 << 20
EDGE_LIMIT = 56 << 20
HALF = 5120


def place(x, y, z, core):
    row = (((y >> 1) & 1) * 4 + x % 4) * 2 + core
    col = (z % 8) * 2 + (y & 1)
    return row * 16 + col


BLOCK = 32
BLOCK_GROUPS = [
    [place(x, y, z + dz, core) for dz in range(2) for x in range(4) for y in range(4)]
    for z in range(0, 8, 2)
    for core in range(2)
]


PAIR_GROUPS = [
    [place(x, y, z + dz, core) for z in range(0, 8, 2)]
    for dz in range(2)
    for x in range(4)
    for y in range(4)
    for core in range(2)
]
CORE_SWAP = [(i, i ^ 1) for i in range(16)]
INNER_PAIRS = CORE_SWAP
OUTER_PAIRS = [pair for i in range(1, 15, 2) for pair in ((i, i + 1), (i + 1, i))]


def edge_kernel(
    bot_hbm, skip_hbm, cot_hbm, inner_ref, outer_ref, bot, fine, wide, sems
):
    copies = [
        pltpu.make_async_copy(src, dst, sems.at[i])
        for i, (src, dst) in enumerate(
            (
                (cot_hbm.at[pl.ds(0, 4)], fine.at[pl.ds(0, 4)]),
                (cot_hbm.at[pl.ds(2 * TILE - 4, 4)], fine.at[pl.ds(4, 4)]),
                (skip_hbm.at[pl.ds(0, 1)], fine.at[pl.ds(8, 1)]),
                (skip_hbm.at[pl.ds(2 * TILE - 1, 1)], fine.at[pl.ds(9, 1)]),
                (bot_hbm.at[pl.ds(0, 2)], bot.at[pl.ds(0, 2)]),
                (bot_hbm.at[pl.ds(TILE - 2, 2)], bot.at[pl.ds(2, 2)]),
            )
        )
    ]
    for copy in copies:
        copy.start()
    even = lax.rem(lax.axis_index("row"), 2) == 0

    def put(at, lanes, first, last):
        inner_ref[at, :, lanes] = jnp.where(even, last, first)
        outer_ref[at, :, lanes] = jnp.where(even, first, last)

    for copy in copies:
        copy.wait()
    put(slice(0, 2), slice(0, 256), bot[0:2], bot[2:4])
    wide[...] = fine[...].astype(F32)
    for col_par in range(2):
        lanes = slice(col_par * 128, col_par * 128 + 128)
        part = wide[:, pl.ds(col_par, TILE, stride=2), :].astype(BF16)
        for par in range(2):
            for step in range(2):
                row = 2 * step + par
                put(2 + 2 * par + step, lanes, part[row], part[4 + row])
        put(6, lanes, part[8], part[9])


def edges(bottom_in, skip_feat, cotangent):
    vmem = pl.BlockSpec(memory_space=pltpu.VMEM)
    strip = jax.ShapeDtypeStruct((7, TILE, 256), BF16)
    return pl.pallas_call(
        edge_kernel,
        out_shape=(strip, strip),
        in_specs=[pl.BlockSpec(memory_space=pl.ANY)] * 3,
        out_specs=(vmem, vmem),
        scratch_shapes=[
            pltpu.VMEM((4, TILE, 256), BF16),
            pltpu.VMEM((10, 2 * TILE, 128), BF16),
            pltpu.VMEM((10, 2 * TILE, 128), F32),
            pltpu.SemaphoreType.DMA((6,)),
        ],
        compiler_params=pltpu.CompilerParams(vmem_limit_bytes=EDGE_LIMIT),
    )(bottom_in, skip_feat, cotangent)


def split_kernel(bot, skip, cot, out_ref, wide):
    for plane, ref in ((1, cot), (3, skip)):
        wide[...] = ref[...].astype(F32)
        for col_par in range(2):
            part = wide[:, pl.ds(col_par, TILE, stride=2), :].astype(BF16)
            part = part.reshape(TILE, 2, TILE, 128)
            lanes = slice(col_par * 128, col_par * 128 + 128)
            out_ref[plane, :, :, lanes] = part[:, 0]
            out_ref[plane + 1, :, :, lanes] = part[:, 1]
    out_ref[0] = bot[...]


def split(bottom_in, skip_feat, cotangent):
    vmem = pl.BlockSpec(memory_space=pltpu.VMEM)
    return pl.pallas_call(
        split_kernel,
        out_shape=jax.ShapeDtypeStruct((5, TILE, TILE, 256), BF16),
        in_specs=[vmem] * 3,
        out_specs=vmem,
        scratch_shapes=[pltpu.VMEM((2 * TILE, 2 * TILE, 128), F32)],
        compiler_params=pltpu.CompilerParams(vmem_limit_bytes=16 << 20),
    )(bottom_in, skip_feat, cotangent)


def nn(a, b):
    return lax.dot_general(a, b, (((1,), (0,)), ((), ())), preferred_element_type=F32)


def nt(a, b):
    return lax.dot_general(a, b, (((1,), (1,)), ((), ())), preferred_element_type=F32)


def tn(a, b):
    return lax.dot_general(a, b, (((0,), (0,)), ((), ())), preferred_element_type=F32)


def flat(x):
    return x.reshape(-1, x.shape[-1])


def left(x):
    return pltpu.roll(x, 1, 0)


def right(x):
    return pltpu.roll(x, x.shape[0] - 1, 0)


def core_of(x):
    rows = x.shape[0] // PITCH
    return x.reshape(rows, PITCH, x.shape[1])[:, CORE : CORE + TILE]


def three(x):
    return (left(x), x, right(x))


def four(x):
    return (left(x[:, 128:]), x, right(x[:, :128]))


def fine_row(offset):
    return offset % 2, offset // 2


def pair_weight(taps, zero):
    first = jnp.concatenate([taps[0], taps[1], taps[2], zero], axis=0)
    second = jnp.concatenate([zero, taps[0], taps[1], taps[2]], axis=0)
    return jnp.concatenate([first, second], axis=1)


def pair_weight_back(taps, zero):
    first = jnp.concatenate([taps[0], taps[1], taps[2], zero], axis=1)
    second = jnp.concatenate([zero, taps[0], taps[1], taps[2]], axis=1)
    return jnp.concatenate([first, second], axis=0)


def main_kernel(
    scale, pos_ref, z_ref, up_ref, down_ref, lo_ref, hi_ref, bk_ref, uk_ref, flip_ref,
    mix4c, pg3c, keep_ref, send_ref,
    ext, bot3, botc, act3, actc, dsilu, cot4, mg4, mg4c, pgc, packed, sems,
):
    row0 = pos_ref[0] * TILE
    col0 = pos_ref[1] * TILE
    image_h = pos_ref[2]
    image_w = pos_ref[3]
    mine = pos_ref[4]

    core = slice(CORE, CORE + TILE)
    ext[...] = jnp.zeros_like(ext)
    ext[:, 2 : 2 + TILE, core, :] = z_ref[...].astype(F32)
    for plane in range(3):
        two = slice(2 * plane, 2 * plane + 2)
        ext[plane, 0:2, core, :] = up_ref[two].astype(F32)
        ext[plane, 2 + TILE : EXT, core, :] = down_ref[two].astype(F32)
        side = slice(EXT * plane, EXT * plane + EXT)
        ext[plane, :, CORE - 2 : CORE, :] = lo_ref[side].astype(F32)
        ext[plane, :, CORE + TILE : CORE + TILE + 2, :] = hi_ref[side].astype(F32)
    ext[4, 1, core, :] = up_ref[6].astype(F32)
    ext[3, 2 + TILE, core, :] = down_ref[6].astype(F32)
    for par in range(2):
        side = slice(3 * EXT, 3 * EXT + 18)
        ext[3 + par, 1:19, CORE - 1 : CORE, :] = lo_ref[side, par : par + 1].astype(F32)
        ext[3 + par, 1:19, CORE + TILE : CORE + TILE + 1, :] = hi_ref[
            side, par : par + 1
        ].astype(F32)

    def masked(x, first):
        rows = x.shape[0] // PITCH
        x = x.reshape(rows, PITCH, x.shape[1])
        i = lax.broadcasted_iota(jnp.int32, x.shape, 0) + (row0 + first - 2)
        w = lax.broadcasted_iota(jnp.int32, x.shape, 1)
        j = w + (col0 - CORE)
        keep = (i >= 0) & (i < image_h) & (j >= 0) & (j < image_w)
        keep = keep & (w >= CORE - 2) & (w < CORE + TILE + 2)
        return flat(jnp.where(keep, x, 0.0))

    zero = jnp.zeros((128, 128), BF16)

    for b, part in enumerate(three(flat(ext[0]))):
        lanes = slice(256 * b, 256 * b + 256)
        bot3[:, :, lanes] = part.reshape(EXT, PITCH, 256).astype(BF16)
        botc[:, :, lanes] = core_of(part)[1 : 19].astype(BF16)
    pre = jnp.zeros((18 * PITCH, 256), F32)
    for a in range(3):
        pre = pre + nn(flat(bot3[a : a + 18]), bk_ref[a].reshape(768, 256))
    sigma = jax.nn.sigmoid(pre)
    dsilu[...] = sigma * (1.0 + pre * (1.0 - sigma))
    activ = masked((pre * sigma).astype(BF16).astype(F32), 1)
    act3[0] = jnp.zeros((PITCH, 768), BF16)
    act3[EXT - 1] = jnp.zeros((PITCH, 768), BF16)
    for b, part in enumerate(three(activ)):
        act3[1:19, :, 256 * b : 256 * b + 256] = part.reshape(18, PITCH, 256).astype(BF16)
    actc[...] = flat(core_of(activ)[1:17]).astype(BF16)

    for par in range(2):
        a, b, c = four(flat(ext[1 + par]))
        cot4[par, :, :, 0:128] = a.reshape(EXT, PITCH, 128).astype(BF16)
        cot4[par, :, :, 128:384] = b.reshape(EXT, PITCH, 256).astype(BF16)
        cot4[par, :, :, 384:512] = c.reshape(EXT, PITCH, 128).astype(BF16)
    for par in range(2):
        first = 1 - par
        total = jnp.zeros((19 * PITCH, 256), F32)
        for a in range(3):
            src, shift = fine_row(par + a - 1)
            weight = pair_weight_back([flip_ref[a, b] for b in range(3)], zero)
            total = total + nt(flat(cot4[src, first + shift : first + shift + 19]), weight)
        grad = masked(total.astype(BF16).astype(F32), first)
        a, b, c = four(grad)
        mg4[par, first : first + 19, :, 0:128] = a.reshape(19, PITCH, 128).astype(BF16)
        mg4[par, first : first + 19, :, 128:384] = b.reshape(19, PITCH, 256).astype(BF16)
        mg4[par, first : first + 19, :, 384:512] = c.reshape(19, PITCH, 128).astype(BF16)
        mg4c[par, first : first + 19, :, 0:128] = core_of(a).astype(BF16)
        mg4c[par, first : first + 19, :, 128:384] = core_of(b).astype(BF16)
        mg4c[par, first : first + 19, :, 384:512] = core_of(c).astype(BF16)

    def put(half, row, value):
        packed[half, row : row + value.shape[0], :] = (value * scale).astype(BF16)

    def hand_out(number, half, first, count, act):
        rows = pl.ds(first, count)
        for which in range(2):

            @pl.when(mine == which)
            def _():
                out = keep_ref if half == which else send_ref
                act(pltpu.make_async_copy(packed.at[half, rows], out.at[rows], sems.at[number]))

    parts = ((0, 0, 0, 4096), (1, 1, 0, 4608), (2, 0, 4096, HALF - 4096), (3, 1, 4608, HALF - 4608))

    act_t = actc[...].T
    for a in range(4):
        src, shift = fine_row(a - 1)
        prod = nn(act_t, flat(mg4c[src, 2 + shift : 18 + shift]))
        for b in range(4):
            put(0, (4 * a + b) * 256, prod[:, 128 * b : 128 * b + 128])
    hand_out(*parts[0], lambda copy: copy.start())

    agrad = jnp.zeros((18 * PITCH, 256), F32)
    for a in range(4):
        src, shift = fine_row(a - 1)
        weight = jnp.concatenate([uk_ref[a, b] for b in range(4)], axis=1)
        agrad = agrad + nt(flat(mg4[src, 1 + shift : 19 + shift]), weight)
    pgrad = masked((agrad * dsilu[...]).astype(BF16).astype(F32), 1)
    for b, part in enumerate(three(pgrad)):
        pg3c[:, :, 256 * b : 256 * b + 256] = core_of(part).astype(BF16)
    pgc[...] = flat(core_of(pgrad)[1:17]).astype(BF16)

    for a in range(3):
        prod = tn(flat(botc[a : a + 16]), pgc[...])
        put(1, 768 * a, prod[:, :128])
        put(1, 2304 + 768 * a, prod[:, 128:])
    hand_out(*parts[1], lambda copy: copy.start())

    for par in range(2):
        total = flat(ext[3 + par, 1:19])
        for row_k, shift in (((1, 0), (3, -1)), ((0, 1), (2, 0)))[par]:
            k = [uk_ref[row_k, b] for b in range(4)]
            none = jnp.zeros((256, 128), BF16)
            weight = jnp.concatenate(
                [
                    jnp.concatenate([k[3], k[1], none], axis=0),
                    jnp.concatenate([none, k[2], k[0]], axis=0),
                ],
                axis=1,
            )
            total = total + nn(flat(act3[1 + shift : 19 + shift]), weight)
        mixed = masked(total.astype(BF16).astype(F32), 1)
        a, b, c = four(mixed)
        mix4c[par, :, :, 0:128] = core_of(a).astype(BF16)
        mix4c[par, :, :, 128:384] = core_of(b).astype(BF16)
        mix4c[par, :, :, 384:512] = core_of(c).astype(BF16)

    for a in range(3):
        prod = jnp.zeros((512, 256), F32)
        for par in range(2):
            src, shift = fine_row(par + a - 1)
            prod = prod + tn(
                flat(mix4c[src, 1 + shift : 17 + shift]), flat(z_ref[1 + par])
            )
        for b in range(3):
            tap = prod[128 * b : 128 * b + 128, :128] + prod[128 * b + 128 : 128 * b + 256, 128:]
            if a < 2:
                put(0, 4096 + (3 * a + b) * 128, tap)
            else:
                put(1, 4608 + b * 128, tap)
    put(0, 4864, jnp.zeros((HALF - 4864, 128), F32))
    put(1, 4992, jnp.zeros((HALF - 4992, 128), F32))

    for part in parts[2:]:
        hand_out(*part, lambda copy: copy.start())
    for part in parts:
        hand_out(*part, lambda copy: copy.wait())


def rest_kernel(mix4c, pg3c, bk_ref, lk_ref, level_ref, bgrad_ref, inter):
    zero = jnp.zeros((128, 128), BF16)

    for par in range(2):
        total = jnp.zeros((TILE * TILE, 256), F32)
        for a in range(3):
            src, shift = fine_row(par + a - 1)
            weight = pair_weight([lk_ref[a, b] for b in range(3)], zero)
            total = total + nn(flat(mix4c[src, 1 + shift : 17 + shift]), weight)
        total = total.reshape(TILE, TILE, 256)
        for col_par in range(2):
            inter[:, par, pl.ds(col_par, TILE, stride=2), :] = total[
                :, :, 128 * col_par : 128 * col_par + 128
            ]
    level_ref[...] = inter[...].reshape(2 * TILE, 2 * TILE, 128).astype(BF16)

    total = jnp.zeros((TILE * TILE, 256), F32)
    for a in range(3):
        weight = jnp.concatenate([bk_ref[2 - a, 2 - b] for b in range(3)], axis=1)
        total = total + nt(flat(pg3c[a : a + 16]), weight)
    bgrad_ref[...] = total.reshape(TILE, TILE, 256).astype(BF16)


def rest_work(mix4c, pg3c, bot_kernel, lvl_kernel):
    return pl.pallas_call(
        rest_kernel,
        out_shape=(
            jax.ShapeDtypeStruct((2 * TILE, 2 * TILE, 128), BF16),
            jax.ShapeDtypeStruct((TILE, TILE, 256), BF16),
        ),
        scratch_shapes=[pltpu.VMEM((TILE, 2, 2 * TILE, 128), F32)],
        compiler_params=pltpu.CompilerParams(vmem_limit_bytes=16 << 20),
        cost_estimate=pl.CostEstimate(
            flops=1000000000, bytes_accessed=3000000, transcendentals=0
        ),
    )(mix4c, pg3c, bot_kernel, lvl_kernel)


def local_work(scale, pos, *operands):
    vmem = pl.BlockSpec(memory_space=pltpu.VMEM)
    anywhere = pl.BlockSpec(memory_space=pl.ANY)
    shapes = ((2, 18, TILE, 512), (18, TILE, 768), (HALF, 128), (HALF, 128))
    return pl.pallas_call(
        functools.partial(main_kernel, scale),
        out_shape=tuple(jax.ShapeDtypeStruct(shape, BF16) for shape in shapes),
        in_specs=[pl.BlockSpec(memory_space=pltpu.SMEM)] + [vmem] * len(operands),
        out_specs=(vmem, vmem, anywhere, anywhere),
        scratch_shapes=[
            pltpu.VMEM((5, EXT, PITCH, 256), F32),
            pltpu.VMEM((EXT, PITCH, 768), BF16),
            pltpu.VMEM((18, TILE, 768), BF16),
            pltpu.VMEM((EXT, PITCH, 768), BF16),
            pltpu.VMEM((TILE * TILE, 256), BF16),
            pltpu.VMEM((18 * PITCH, 256), F32),
            pltpu.VMEM((2, EXT, PITCH, 512), BF16),
            pltpu.VMEM((2, EXT, PITCH, 512), BF16),
            pltpu.VMEM((2, EXT, TILE, 512), BF16),
            pltpu.VMEM((TILE * TILE, 256), BF16),
            pltpu.VMEM((2, HALF, 128), BF16),
            pltpu.SemaphoreType.DMA((4,)),
        ],
        compiler_params=pltpu.CompilerParams(vmem_limit_bytes=MAIN_LIMIT),
    )(pos, *operands)


def unpack_kernel(half_of, pos_ref, half, *refs):
    up_hbm, bot_hbm, lvl_hbm, up, bot, lvl, sems = refs[-7:]

    @pl.when(pos_ref[4] == half_of)
    def _():
        copies = []
        for i in range(4):
            rows = pl.ds(1024 * i, 1024)
            up[rows] = half[rows].astype(F32)
            copies.append(pltpu.make_async_copy(up.at[rows], up_hbm.at[rows], sems.at[i]))
            copies[-1].start()
        rows = pl.ds(0, 768)
        lvl[rows] = half[4096:4864].astype(F32)
        copies.append(pltpu.make_async_copy(lvl.at[rows], lvl_hbm.at[rows], sems.at[4]))
        copies[-1].start()
        for copy in copies:
            copy.wait()

    @pl.when(pos_ref[4] != half_of)
    def _():
        copies = []
        for i in range(3):
            rows = pl.ds(768 * i, 768)
            bot[rows, 0:128] = half[768 * i : 768 * i + 768].astype(F32)
            bot[rows, 128:256] = half[2304 + 768 * i : 3072 + 768 * i].astype(F32)
            copies.append(pltpu.make_async_copy(bot.at[rows], bot_hbm.at[rows], sems.at[i]))
            copies[-1].start()
        rows = pl.ds(768, 384)
        lvl[rows] = half[4608:4992].astype(F32)
        copies.append(pltpu.make_async_copy(lvl.at[rows], lvl_hbm.at[rows], sems.at[3]))
        copies[-1].start()
        for copy in copies:
            copy.wait()


def unpack(pos, half, begun=()):
    vmem = pl.BlockSpec(memory_space=pltpu.VMEM)
    anywhere = pl.BlockSpec(memory_space=pl.ANY)
    shapes = ((4096, 128), (2304, 256), (1152, 128))
    return pl.pallas_call(
        functools.partial(unpack_kernel, 1 if begun else 0),
        out_shape=tuple(jax.ShapeDtypeStruct(shape, F32) for shape in shapes),
        in_specs=[pl.BlockSpec(memory_space=pltpu.SMEM), vmem] + [anywhere] * len(begun),
        out_specs=(anywhere,) * 3,
        scratch_shapes=[pltpu.VMEM(shape, F32) for shape in shapes]
        + [pltpu.SemaphoreType.DMA((5,))],
        input_output_aliases={2 + i: i for i in range(len(begun))},
        compiler_params=pltpu.CompilerParams(vmem_limit_bytes=16 << 20),
        cost_estimate=pl.CostEstimate(flops=0, bytes_accessed=4000000, transcendentals=0),
    )(pos, half, *begun)


def swapped(inner, outer, axis):
    got_inner = lax.ppermute(inner, axis, INNER_PAIRS)
    got_outer = lax.ppermute(outer, axis, OUTER_PAIRS)
    even = lax.rem(lax.axis_index(axis), 2) == 0
    return jnp.where(even, got_outer, got_inner), jnp.where(even, got_inner, got_outer)


def exchange(x, groups):
    return lax.all_to_all(x, AXES, 0, 0, axis_index_groups=groups)


def total_over_devices(keep, send, rest):
    got, rest = lax.optimization_barrier((lax.ppermute(send, "row", CORE_SWAP), rest))
    half = (keep.astype(F32) + got.astype(F32)).astype(BF16)
    parts = exchange(half.reshape(BLOCK, HALF // BLOCK, 128), BLOCK_GROUPS)
    part = jnp.sum(parts.astype(F32), axis=0).astype(BF16)
    pairs = exchange(jnp.broadcast_to(part[None], (4,) + part.shape), PAIR_GROUPS)
    total = jnp.sum(pairs.astype(F32), axis=0).astype(BF16)
    half = exchange(jnp.broadcast_to(total[None], parts.shape), BLOCK_GROUPS).reshape(HALF, 128)
    return half, lax.ppermute(half, "row", CORE_SWAP), rest


def on_device(bottom_in, skip_feat, cotangent, bot_kernel, up_kernel, lvl_kernel):
    rows, cols = lax.axis_size("row"), lax.axis_size("col")
    scale = 1.0 / float(2 * TILE * rows * 2 * TILE * cols) ** 0.5
    inner, outer = edges(bottom_in, skip_feat, cotangent)
    inner, outer, *fields = lax.optimization_barrier(
        (inner, outer, bottom_in, skip_feat, cotangent)
    )
    z = split(*fields)
    up, down = swapped(inner, outer, "row")

    def side(cols, skip_col):
        parts = [
            jnp.concatenate(
                [up[2 * p : 2 * p + 2, cols], z[p, :, cols], down[2 * p : 2 * p + 2, cols]], axis=0
            )
            for p in range(3)
        ]
        blank = jnp.zeros((1, 1, 256), BF16)
        even = jnp.concatenate([blank, z[3, :, skip_col], down[6:7, skip_col]], axis=0)
        odd = jnp.concatenate([up[6:7, skip_col], z[4, :, skip_col], blank], axis=0)
        return jnp.concatenate(parts + [jnp.concatenate([even, odd], axis=1)], axis=0)

    last = side(slice(TILE - 2, TILE), slice(TILE - 1, TILE))
    first = side(slice(0, 2), slice(0, 1))
    even = lax.rem(lax.axis_index("col"), 2) == 0
    lo, hi = swapped(jnp.where(even, last, first), jnp.where(even, first, last), "col")
    row = lax.axis_index("row")
    pos = jnp.stack(
        [row, lax.axis_index("col"), jnp.int32(TILE * rows), jnp.int32(TILE * cols), row % 2]
    ).astype(jnp.int32)
    flip = lvl_kernel[::-1, ::-1]
    mix4c, pg3c, keep, send = local_work(
        scale, pos, z, up, down, lo, hi, bot_kernel, up_kernel, flip
    )
    rest = rest_work(mix4c, pg3c, bot_kernel, lvl_kernel)
    half, other, (level_out, bottom_grad) = total_over_devices(keep, send, rest)
    up_grad, bot_grad, lvl_grad = unpack(pos, other, unpack(pos, half))
    return (
        level_out,
        bottom_grad,
        lvl_grad.reshape(3, 3, 128, 128),
        up_grad.reshape(4, 4, 256, 128),
        bot_grad.reshape(3, 3, 256, 256),
    )


def solution(mesh):
    return jax.shard_map(
        on_device,
        mesh=mesh,
        in_specs=(
            P("row", "col", None),
            P("row", "col", None),
            P("row", "col", None),
            P(),
            P(),
            P(),
        ),
        out_specs=(P("row", "col", None), P("row", "col", None), P(), P(), P()),
        check_vma=False,
    )
```

```python
import functools

import jax
import jax.numpy as jnp
from jax import lax
from jax.experimental import pallas as pl
from jax.experimental.pallas import tpu as pltpu
from jax.sharding import PartitionSpec as P

AXES = ("row", "col")
F32 = jnp.float32
BF16 = jnp.bfloat16
TILE = 16
EXT = TILE + 4
PITCH = 32
CORE = 8
MAIN_LIMIT = 40 << 20
FIRST_LIMIT = 56 << 20
HALF = 5120


def place(x, y, z, core):
    row = (((y >> 1) & 1) * 4 + x % 4) * 2 + core
    col = (z % 8) * 2 + (y & 1)
    return row * 16 + col


BLOCK = 32
BLOCK_GROUPS = [
    [place(x, y, z + dz, core) for dz in range(2) for x in range(4) for y in range(4)]
    for z in range(0, 8, 2)
    for core in range(2)
]


PAIR_GROUPS = [
    [place(x, y, z + dz, core) for z in range(0, 8, 2)]
    for dz in range(2)
    for x in range(4)
    for y in range(4)
    for core in range(2)
]
CORE_SWAP = [(i, i ^ 1) for i in range(16)]
INNER_PAIRS = CORE_SWAP
OUTER_PAIRS = [pair for i in range(1, 15, 2) for pair in ((i, i + 1), (i + 1, i))]


COLUMNS = 3 * EXT + 18


def is_even(axis):
    return lax.rem(lax.axis_index(axis), 2) == 0


def both(even, first, last):
    return jnp.where(even, last, first).astype(BF16), jnp.where(even, first, last).astype(BF16)


def pair_of(first, second):
    shape = (first.shape[0], 2, 256)
    odd = lax.broadcasted_iota(jnp.int32, shape, 1) == 1
    return jnp.where(odd, jnp.broadcast_to(second, shape), jnp.broadcast_to(first, shape))


def split_kernel(
    bot_hbm, skip_hbm, cot_hbm, z_hbm, inner_hbm, outer_hbm, own_hbm,
    bot, skip, cot, wide, z, inner, outer, own, sems, out_sems,
):
    copies = [
        pltpu.make_async_copy(src, dst, sems.at[i])
        for i, (src, dst) in enumerate(((cot_hbm, cot), (skip_hbm, skip), (bot_hbm, bot)))
    ]
    for copy in copies:
        copy.start()
    for plane, ref, copy in ((1, cot, copies[0]), (3, skip, copies[1])):
        copy.wait()
        wide[...] = ref[...].astype(F32)
        for col_par in range(2):
            part = wide[:, pl.ds(col_par, TILE, stride=2), :].astype(BF16)
            part = part.reshape(TILE, 2, TILE, 128)
            lanes = slice(col_par * 128, col_par * 128 + 128)
            z[plane, :, :, lanes] = part[:, 0]
            z[plane + 1, :, :, lanes] = part[:, 1]
    copies[2].wait()
    z[0] = bot[...]

    even = is_even("row")
    for plane in range(3):
        two = slice(2 * plane, 2 * plane + 2)
        inner[two], outer[two] = both(even, z[plane, 0:2], z[plane, TILE - 2 : TILE])
    inner[6], outer[6] = both(even, z[3, 0], z[4, TILE - 1])
    outs = [
        pltpu.make_async_copy(src, dst, out_sems.at[i])
        for i, (src, dst) in enumerate(
            (
                (inner, inner_hbm),
                (outer, outer_hbm),
                (z, z_hbm),
                (own, own_hbm),
            )
        )
    ]
    for copy in outs[:3]:
        copy.start()

    even = is_even("col")
    own[...] = jnp.zeros((2, COLUMNS, 2, 256), BF16)
    for plane in range(3):
        rows = slice(EXT * plane + 2, EXT * plane + 2 + TILE)
        x = z[plane].astype(F32)
        own[0, rows], own[1, rows] = both(even, x[:, 0:2], x[:, TILE - 2 : TILE])
    x, y = z[3].astype(F32), z[4].astype(F32)
    rows = slice(3 * EXT + 1, 3 * EXT + 1 + TILE)
    own[0, rows], own[1, rows] = both(
        even, pair_of(x[:, 0:1], y[:, 0:1]), pair_of(x[:, TILE - 1 : TILE], y[:, TILE - 1 : TILE])
    )
    for copy in outs[3:]:
        copy.start()
    for copy in outs:
        copy.wait()


def split(bottom_in, skip_feat, cotangent):
    anywhere = pl.BlockSpec(memory_space=pl.ANY)
    fine = (2 * TILE, 2 * TILE, 128)
    shapes = ((5, TILE, TILE, 256),) + ((7, TILE, 256),) * 2 + ((2, COLUMNS, 2, 256),)
    return pl.pallas_call(
        split_kernel,
        out_shape=tuple(jax.ShapeDtypeStruct(shape, BF16) for shape in shapes),
        in_specs=[anywhere] * 3,
        out_specs=(anywhere,) * len(shapes),
        scratch_shapes=[
            pltpu.VMEM((TILE, TILE, 256), BF16),
            pltpu.VMEM(fine, BF16),
            pltpu.VMEM(fine, BF16),
            pltpu.VMEM(fine, F32),
        ]
        + [pltpu.VMEM(shape, BF16) for shape in shapes]
        + [pltpu.SemaphoreType.DMA((3,)), pltpu.SemaphoreType.DMA((len(shapes),))],
        compiler_params=pltpu.CompilerParams(vmem_limit_bytes=FIRST_LIMIT),
    )(bottom_in, skip_feat, cotangent)


def ends_kernel(own, got_inner, got_outer, inner_ref, outer_ref):
    inner_ref[...] = own[1]
    outer_ref[...] = own[0]
    got = got_inner[...].astype(F32), got_outer[...].astype(F32)
    even = is_even("row")
    up, down = jnp.where(even, got[1], got[0]), jnp.where(even, got[0], got[1])
    even = is_even("col")
    for plane in range(3):
        for x, at in ((up, EXT * plane), (down, EXT * plane + 2 + TILE)):
            x = x[2 * plane : 2 * plane + 2]
            inner_ref[at : at + 2], outer_ref[at : at + 2] = both(
                even, x[:, 0:2], x[:, TILE - 2 : TILE]
            )
    zero = jnp.zeros((1, 1, 256), F32)
    x, at = up[6:7], slice(3 * EXT, 3 * EXT + 1)
    inner_ref[at], outer_ref[at] = both(
        even, pair_of(zero, x[:, 0:1]), pair_of(zero, x[:, TILE - 1 : TILE])
    )
    x, at = down[6:7], slice(3 * EXT + 17, 3 * EXT + 18)
    inner_ref[at], outer_ref[at] = both(
        even, pair_of(x[:, 0:1], zero), pair_of(x[:, TILE - 1 : TILE], zero)
    )


def with_ends(*strips):
    vmem = pl.BlockSpec(memory_space=pltpu.VMEM)
    shape = jax.ShapeDtypeStruct((COLUMNS, 2, 256), BF16)
    return pl.pallas_call(
        ends_kernel,
        out_shape=(shape, shape),
        in_specs=[vmem] * 3,
        out_specs=(vmem, vmem),
        compiler_params=pltpu.CompilerParams(vmem_limit_bytes=8 << 20),
        cost_estimate=pl.CostEstimate(flops=0, bytes_accessed=20000000, transcendentals=0),
    )(*strips)


def nn(a, b):
    return lax.dot_general(a, b, (((1,), (0,)), ((), ())), preferred_element_type=F32)


def nt(a, b):
    return lax.dot_general(a, b, (((1,), (1,)), ((), ())), preferred_element_type=F32)


def tn(a, b):
    return lax.dot_general(a, b, (((0,), (0,)), ((), ())), preferred_element_type=F32)


def flat(x):
    return x.reshape(-1, x.shape[-1])


def left(x):
    return pltpu.roll(x, 1, 0)


def right(x):
    return pltpu.roll(x, x.shape[0] - 1, 0)


def core_of(x):
    rows = x.shape[0] // PITCH
    return x.reshape(rows, PITCH, x.shape[1])[:, CORE : CORE + TILE]


def three(x):
    return (left(x), x, right(x))


def four(x):
    return (left(x[:, 128:]), x, right(x[:, :128]))


def fine_row(offset):
    return offset % 2, offset // 2


def pair_weight(taps, zero):
    first = jnp.concatenate([taps[0], taps[1], taps[2], zero], axis=0)
    second = jnp.concatenate([zero, taps[0], taps[1], taps[2]], axis=0)
    return jnp.concatenate([first, second], axis=1)


def pair_weight_back(taps, zero):
    first = jnp.concatenate([taps[0], taps[1], taps[2], zero], axis=1)
    second = jnp.concatenate([zero, taps[0], taps[1], taps[2]], axis=1)
    return jnp.concatenate([first, second], axis=0)


def main_kernel(
    scale, pos_ref, z_ref, row_in, row_out, col_in, col_out, bk_ref, uk_ref, flip_ref,
    mix4c, pg3c, keep_ref, send_ref,
    ext, bot3, botc, act3, actc, dsilu, cot4, mg4, mg4c, pgc, packed, sems,
):
    row0 = pos_ref[0] * TILE
    col0 = pos_ref[1] * TILE
    image_h = pos_ref[2]
    image_w = pos_ref[3]
    mine = pos_ref[4]

    def before_behind(inner, outer, even):
        inner, outer = inner.astype(F32), outer.astype(F32)
        return jnp.where(even, outer, inner), jnp.where(even, inner, outer)

    core = slice(CORE, CORE + TILE)
    low, high = slice(CORE - 2, CORE), slice(CORE + TILE, CORE + TILE + 2)
    even_row, even_col = is_even("row"), is_even("col")
    ext[...] = jnp.zeros_like(ext)
    for plane in range(5):
        ext[plane, 2 : 2 + TILE, core, :] = z_ref[4 - plane].astype(F32)
    for plane in range(3):
        two = slice(2 * plane, 2 * plane + 2)
        ext[plane, 0:2, core, :], ext[plane, 2 + TILE : EXT, core, :] = before_behind(
            row_in[two], row_out[two], even_row
        )
        side = slice(EXT * plane, EXT * plane + EXT)
        ext[plane, :, low, :], ext[plane, :, high, :] = before_behind(
            col_in[side], col_out[side], even_col
        )
    ext[4, 1, core, :], ext[3, 2 + TILE, core, :] = before_behind(row_in[6], row_out[6], even_row)
    low, high = slice(CORE - 1, CORE), slice(CORE + TILE, CORE + TILE + 1)
    for par in range(2):
        side = slice(3 * EXT, 3 * EXT + 18)
        ext[3 + par, 1:19, low, :], ext[3 + par, 1:19, high, :] = before_behind(
            col_in[side, par : par + 1], col_out[side, par : par + 1], even_col
        )

    def masked(x, first):
        rows = x.shape[0] // PITCH
        x = x.reshape(rows, PITCH, x.shape[1])
        i = lax.broadcasted_iota(jnp.int32, x.shape, 0) + (row0 + first - 2)
        w = lax.broadcasted_iota(jnp.int32, x.shape, 1)
        j = w + (col0 - CORE)
        keep = (i >= 0) & (i < image_h) & (j >= 0) & (j < image_w)
        keep = keep & (w >= CORE - 2) & (w < CORE + TILE + 2)
        return flat(jnp.where(keep, x, 0.0))

    zero = jnp.zeros((128, 128), BF16)

    for b, part in enumerate(three(flat(ext[0]))):
        lanes = slice(256 * b, 256 * b + 256)
        bot3[:, :, lanes] = part.reshape(EXT, PITCH, 256).astype(BF16)
        botc[:, :, lanes] = core_of(part)[1 : 19].astype(BF16)
    pre = jnp.zeros((18 * PITCH, 256), F32)
    for a in range(3):
        pre = pre + nn(flat(bot3[a : a + 18]), bk_ref[a].reshape(768, 256))
    sigma = jax.nn.sigmoid(pre)
    dsilu[...] = sigma * (1.0 + pre * (1.0 - sigma))
    activ = masked((pre * sigma).astype(BF16).astype(F32), 1)
    act3[0] = jnp.zeros((PITCH, 768), BF16)
    act3[EXT - 1] = jnp.zeros((PITCH, 768), BF16)
    for b, part in enumerate(three(activ)):
        act3[1:19, :, 256 * b : 256 * b + 256] = part.reshape(18, PITCH, 256).astype(BF16)
    actc[...] = flat(core_of(activ)[1:17]).astype(BF16)

    for par in range(2):
        a, b, c = four(flat(ext[1 + par]))
        cot4[par, :, :, 0:128] = a.reshape(EXT, PITCH, 128).astype(BF16)
        cot4[par, :, :, 128:384] = b.reshape(EXT, PITCH, 256).astype(BF16)
        cot4[par, :, :, 384:512] = c.reshape(EXT, PITCH, 128).astype(BF16)
    for par in range(2):
        first = 1 - par
        total = jnp.zeros((19 * PITCH, 256), F32)
        for a in range(3):
            src, shift = fine_row(par + a - 1)
            weight = pair_weight_back([flip_ref[a, b] for b in range(3)], zero)
            total = total + nt(flat(cot4[src, first + shift : first + shift + 19]), weight)
        grad = masked(total.astype(BF16).astype(F32), first)
        a, b, c = four(grad)
        mg4[par, first : first + 19, :, 0:128] = a.reshape(19, PITCH, 128).astype(BF16)
        mg4[par, first : first + 19, :, 128:384] = b.reshape(19, PITCH, 256).astype(BF16)
        mg4[par, first : first + 19, :, 384:512] = c.reshape(19, PITCH, 128).astype(BF16)
        mg4c[par, first : first + 19, :, 0:128] = core_of(a).astype(BF16)
        mg4c[par, first : first + 19, :, 128:384] = core_of(b).astype(BF16)
        mg4c[par, first : first + 19, :, 384:512] = core_of(c).astype(BF16)

    def put(half, row, value):
        packed[half, row : row + value.shape[0], :] = (value * scale).astype(BF16)

    def hand_out(number, half, first, count, act):
        rows = pl.ds(first, count)
        for which in range(2):

            @pl.when(mine == which)
            def _():
                out = keep_ref if half == which else send_ref
                act(pltpu.make_async_copy(packed.at[half, rows], out.at[rows], sems.at[number]))

    parts = ((0, 0, 0, 4096), (1, 1, 0, 4608), (2, 0, 4096, HALF - 4096), (3, 1, 4608, HALF - 4608))

    act_t = actc[...].T
    for a in range(4):
        src, shift = fine_row(a - 1)
        prod = nn(act_t, flat(mg4c[src, 2 + shift : 18 + shift]))
        for b in range(4):
            put(0, (4 * a + b) * 256, prod[:, 128 * b : 128 * b + 128])
    hand_out(*parts[0], lambda copy: copy.start())

    agrad = jnp.zeros((18 * PITCH, 256), F32)
    for a in range(4):
        src, shift = fine_row(a - 1)
        weight = jnp.concatenate([uk_ref[a, 3 - b] for b in range(4)], axis=1)
        agrad = agrad + nt(flat(mg4[src, 1 + shift : 19 + shift]), weight)
    pgrad = masked((agrad * dsilu[...]).astype(BF16).astype(F32), 1)
    for b, part in enumerate(three(pgrad)):
        pg3c[:, :, 256 * b : 256 * b + 256] = core_of(part).astype(BF16)
    pgc[...] = flat(core_of(pgrad)[1:17]).astype(BF16)

    for a in range(3):
        prod = tn(flat(botc[a : a + 16]), pgc[...])
        put(1, 768 * a, prod[:, :128])
        put(1, 2304 + 768 * a, prod[:, 128:])
    hand_out(*parts[1], lambda copy: copy.start())

    for par in range(2):
        total = flat(ext[3 + par, 1:19])
        for row_k, shift in (((1, 0), (3, -1)), ((0, 1), (2, 0)))[par]:
            k = [uk_ref[row_k, 3 - b] for b in range(4)]
            none = jnp.zeros((256, 128), BF16)
            weight = jnp.concatenate(
                [
                    jnp.concatenate([k[3], k[1], none], axis=0),
                    jnp.concatenate([none, k[2], k[0]], axis=0),
                ],
                axis=1,
            )
            total = total + nn(flat(act3[1 + shift : 19 + shift]), weight)
        mixed = masked(total.astype(BF16).astype(F32), 1)
        a, b, c = four(mixed)
        mix4c[par, :, :, 0:128] = core_of(a).astype(BF16)
        mix4c[par, :, :, 128:384] = core_of(b).astype(BF16)
        mix4c[par, :, :, 384:512] = core_of(c).astype(BF16)

    for a in range(3):
        prod = jnp.zeros((512, 256), F32)
        for par in range(2):
            src, shift = fine_row(par + a - 1)
            prod = prod + tn(
                flat(mix4c[src, 1 + shift : 17 + shift]), flat(z_ref[3 - par])
            )
        for b in range(3):
            tap = prod[128 * b : 128 * b + 128, :128] + prod[128 * b + 128 : 128 * b + 256, 128:]
            if a < 2:
                put(0, 4096 + (3 * a + b) * 128, tap)
            else:
                put(1, 4608 + b * 128, tap)
    put(0, 4864, jnp.zeros((HALF - 4864, 128), F32))
    put(1, 4992, jnp.zeros((HALF - 4992, 128), F32))

    for part in parts[2:]:
        hand_out(*part, lambda copy: copy.start())
    for part in parts:
        hand_out(*part, lambda copy: copy.wait())


def rest_kernel(mix4c, pg3c, bk_ref, lk_ref, level_ref, bgrad_ref, inter):
    zero = jnp.zeros((128, 128), BF16)

    for par in range(2):
        total = jnp.zeros((TILE * TILE, 256), F32)
        for a in range(3):
            src, shift = fine_row(par + a - 1)
            weight = pair_weight([lk_ref[a, b] for b in range(3)], zero)
            total = total + nn(flat(mix4c[src, 1 + shift : 17 + shift]), weight)
        total = total.reshape(TILE, TILE, 256)
        for col_par in range(2):
            inter[:, par, pl.ds(col_par, TILE, stride=2), :] = total[
                :, :, 128 * col_par : 128 * col_par + 128
            ]
    level_ref[...] = inter[...].reshape(2 * TILE, 2 * TILE, 128).astype(BF16)

    total = jnp.zeros((TILE * TILE, 256), F32)
    for a in range(3):
        weight = jnp.concatenate([bk_ref[2 - a, 2 - b] for b in range(3)], axis=1)
        total = total + nt(flat(pg3c[a : a + 16]), weight)
    bgrad_ref[...] = total.reshape(TILE, TILE, 256).astype(BF16)


def rest_work(mix4c, pg3c, bot_kernel, lvl_kernel):
    return pl.pallas_call(
        rest_kernel,
        out_shape=(
            jax.ShapeDtypeStruct((2 * TILE, 2 * TILE, 128), BF16),
            jax.ShapeDtypeStruct((TILE, TILE, 256), BF16),
        ),
        scratch_shapes=[pltpu.VMEM((TILE, 2, 2 * TILE, 128), F32)],
        compiler_params=pltpu.CompilerParams(vmem_limit_bytes=16 << 20),
        cost_estimate=pl.CostEstimate(
            flops=1000000000, bytes_accessed=3000000, transcendentals=0
        ),
    )(mix4c, pg3c, bot_kernel, lvl_kernel)


def local_work(scale, pos, *operands):
    vmem = pl.BlockSpec(memory_space=pltpu.VMEM)
    anywhere = pl.BlockSpec(memory_space=pl.ANY)
    shapes = ((2, 18, TILE, 512), (18, TILE, 768), (HALF, 128), (HALF, 128))
    return pl.pallas_call(
        functools.partial(main_kernel, scale),
        out_shape=tuple(jax.ShapeDtypeStruct(shape, BF16) for shape in shapes),
        in_specs=[pl.BlockSpec(memory_space=pltpu.SMEM)] + [vmem] * len(operands),
        out_specs=(vmem, vmem, anywhere, anywhere),
        scratch_shapes=[
            pltpu.VMEM((5, EXT, PITCH, 256), F32),
            pltpu.VMEM((EXT, PITCH, 768), BF16),
            pltpu.VMEM((18, TILE, 768), BF16),
            pltpu.VMEM((EXT, PITCH, 768), BF16),
            pltpu.VMEM((TILE * TILE, 256), BF16),
            pltpu.VMEM((18 * PITCH, 256), F32),
            pltpu.VMEM((2, EXT, PITCH, 512), BF16),
            pltpu.VMEM((2, EXT, PITCH, 512), BF16),
            pltpu.VMEM((2, EXT, TILE, 512), BF16),
            pltpu.VMEM((TILE * TILE, 256), BF16),
            pltpu.VMEM((2, HALF, 128), BF16),
            pltpu.SemaphoreType.DMA((4,)),
        ],
        compiler_params=pltpu.CompilerParams(vmem_limit_bytes=MAIN_LIMIT),
    )(pos, *operands)


def unpack_kernel(half_of, pos_ref, half, *refs):
    up_hbm, bot_hbm, lvl_hbm, up, bot, lvl, sems = refs[-7:]

    @pl.when(pos_ref[4] == half_of)
    def _():
        copies = []
        for i in range(4):
            rows = pl.ds(1024 * i, 1024)
            up[rows] = half[rows].astype(F32)
            copies.append(pltpu.make_async_copy(up.at[rows], up_hbm.at[rows], sems.at[i]))
            copies[-1].start()
        rows = pl.ds(0, 768)
        lvl[rows] = half[4096:4864].astype(F32)
        copies.append(pltpu.make_async_copy(lvl.at[rows], lvl_hbm.at[rows], sems.at[4]))
        copies[-1].start()
        for copy in copies:
            copy.wait()

    @pl.when(pos_ref[4] != half_of)
    def _():
        copies = []
        for i in range(3):
            rows = pl.ds(768 * i, 768)
            bot[rows, 0:128] = half[768 * i : 768 * i + 768].astype(F32)
            bot[rows, 128:256] = half[2304 + 768 * i : 3072 + 768 * i].astype(F32)
            copies.append(pltpu.make_async_copy(bot.at[rows], bot_hbm.at[rows], sems.at[i]))
            copies[-1].start()
        rows = pl.ds(768, 384)
        lvl[rows] = half[4608:4992].astype(F32)
        copies.append(pltpu.make_async_copy(lvl.at[rows], lvl_hbm.at[rows], sems.at[3]))
        copies[-1].start()
        for copy in copies:
            copy.wait()


def unpack(pos, half, begun=()):
    vmem = pl.BlockSpec(memory_space=pltpu.VMEM)
    anywhere = pl.BlockSpec(memory_space=pl.ANY)
    shapes = ((4096, 128), (2304, 256), (1152, 128))
    return pl.pallas_call(
        functools.partial(unpack_kernel, 1 if begun else 0),
        out_shape=tuple(jax.ShapeDtypeStruct(shape, F32) for shape in shapes),
        in_specs=[pl.BlockSpec(memory_space=pltpu.SMEM), vmem] + [anywhere] * len(begun),
        out_specs=(anywhere,) * 3,
        scratch_shapes=[pltpu.VMEM(shape, F32) for shape in shapes]
        + [pltpu.SemaphoreType.DMA((5,))],
        input_output_aliases={2 + i: i for i in range(len(begun))},
        compiler_params=pltpu.CompilerParams(vmem_limit_bytes=16 << 20),
        cost_estimate=pl.CostEstimate(flops=0, bytes_accessed=4000000, transcendentals=0),
    )(pos, half, *begun)


def swapped(inner, outer, axis):
    return lax.ppermute(inner, axis, INNER_PAIRS), lax.ppermute(outer, axis, OUTER_PAIRS)


def exchange(x, groups):
    return lax.all_to_all(x, AXES, 0, 0, axis_index_groups=groups)


def total_over_devices(keep, send, rest):
    got, rest = lax.optimization_barrier((lax.ppermute(send, "row", CORE_SWAP), rest))
    half = (keep.astype(F32) + got.astype(F32)).astype(BF16)
    parts = exchange(half.reshape(BLOCK, HALF // BLOCK, 128), BLOCK_GROUPS)
    part = jnp.sum(parts.astype(F32), axis=0).astype(BF16)
    pairs = exchange(jnp.broadcast_to(part[None], (4,) + part.shape), PAIR_GROUPS)
    total = jnp.sum(pairs.astype(F32), axis=0).astype(BF16)
    half = exchange(jnp.broadcast_to(total[None], parts.shape), BLOCK_GROUPS).reshape(HALF, 128)
    return half, lax.ppermute(half, "row", CORE_SWAP), rest


def on_device(bottom_in, skip_feat, cotangent, bot_kernel, up_kernel, lvl_kernel):
    rows, cols = lax.axis_size("row"), lax.axis_size("col")
    scale = 1.0 / float(2 * TILE * rows * 2 * TILE * cols) ** 0.5
    z, inner, outer, own = split(bottom_in, skip_feat, cotangent)
    row_strips = swapped(inner, outer, "row")
    row_strips, z, turned = lax.optimization_barrier((row_strips, z, up_kernel))
    z, turned = z[::-1], turned[:, ::-1]
    col_strips = swapped(*with_ends(own[::-1], *row_strips), "col")
    row = lax.axis_index("row")
    pos = jnp.stack(
        [row, lax.axis_index("col"), jnp.int32(TILE * rows), jnp.int32(TILE * cols), row % 2]
    ).astype(jnp.int32)
    flip = lvl_kernel[::-1, ::-1]
    mix4c, pg3c, keep, send = local_work(
        scale, pos, z, *row_strips, *col_strips, bot_kernel, turned, flip
    )
    rest = rest_work(mix4c, pg3c, bot_kernel, lvl_kernel)
    half, other, (level_out, bottom_grad) = total_over_devices(keep, send, rest)
    up_grad, bot_grad, lvl_grad = unpack(pos, other, unpack(pos, half))
    return (
        level_out,
        bottom_grad,
        lvl_grad.reshape(3, 3, 128, 128),
        up_grad.reshape(4, 4, 256, 128),
        bot_grad.reshape(3, 3, 256, 256),
    )


def solution(mesh):
    return jax.shard_map(
        on_device,
        mesh=mesh,
        in_specs=(
            P("row", "col", None),
            P("row", "col", None),
            P("row", "col", None),
            P(),
            P(),
            P(),
        ),
        out_specs=(P("row", "col", None), P("row", "col", None), P(), P(), P()),
        check_vma=False,
    )
```

```python
import functools

import jax
import jax.numpy as jnp
from jax import lax
from jax.experimental import pallas as pl
from jax.experimental.pallas import tpu as pltpu
from jax.sharding import PartitionSpec as P

AXES = ("row", "col")
F32 = jnp.float32
BF16 = jnp.bfloat16
TILE = 16
EXT = TILE + 4
PITCH = 32
CORE = 8
MAIN_LIMIT = 40 << 20
FIRST_LIMIT = 56 << 20
HALF = 5120


def place(x, y, z, core):
    row = (((y >> 1) & 1) * 4 + x % 4) * 2 + core
    col = (z % 8) * 2 + (y & 1)
    return row * 16 + col


LINE = 4
LINE_GROUPS = [[place(x, y, z, 0) for x in range(4)] for y in range(4) for z in range(8)]
LINE_GROUPS += [[place(x, y, z, 1) for y in range(4)] for x in range(4) for z in range(8)]
SHEET = 32
SHEET_GROUPS = [[place(x, y, z, 0) for y in range(4) for z in range(8)] for x in range(4)]
SHEET_GROUPS += [[place(x, y, z, 1) for x in range(4) for z in range(8)] for y in range(4)]
CORE_SWAP = [(i, i ^ 1) for i in range(16)]
INNER_PAIRS = CORE_SWAP
OUTER_PAIRS = [pair for i in range(1, 15, 2) for pair in ((i, i + 1), (i + 1, i))]


COLUMNS = 3 * EXT + 18


def is_even(axis):
    return lax.rem(lax.axis_index(axis), 2) == 0


def both(even, first, last):
    return jnp.where(even, last, first).astype(BF16), jnp.where(even, first, last).astype(BF16)


def pair_of(first, second):
    shape = (first.shape[0], 2, 256)
    odd = lax.broadcasted_iota(jnp.int32, shape, 1) == 1
    return jnp.where(odd, jnp.broadcast_to(second, shape), jnp.broadcast_to(first, shape))


def split_kernel(
    bot_hbm, skip_hbm, cot_hbm, z_hbm, inner_hbm, outer_hbm, own_hbm,
    bot, skip, cot, wide, z, inner, outer, own, sems, out_sems,
):
    copies = [
        pltpu.make_async_copy(src, dst, sems.at[i])
        for i, (src, dst) in enumerate(((cot_hbm, cot), (skip_hbm, skip), (bot_hbm, bot)))
    ]
    for copy in copies:
        copy.start()
    for plane, ref, copy in ((1, cot, copies[0]), (3, skip, copies[1])):
        copy.wait()
        wide[...] = ref[...].astype(F32)
        for col_par in range(2):
            part = wide[:, pl.ds(col_par, TILE, stride=2), :].astype(BF16)
            part = part.reshape(TILE, 2, TILE, 128)
            lanes = slice(col_par * 128, col_par * 128 + 128)
            z[plane, :, :, lanes] = part[:, 0]
            z[plane + 1, :, :, lanes] = part[:, 1]
    copies[2].wait()
    z[0] = bot[...]

    even = is_even("row")
    for plane in range(3):
        two = slice(2 * plane, 2 * plane + 2)
        inner[two], outer[two] = both(even, z[plane, 0:2], z[plane, TILE - 2 : TILE])
    inner[6], outer[6] = both(even, z[3, 0], z[4, TILE - 1])
    outs = [
        pltpu.make_async_copy(src, dst, out_sems.at[i])
        for i, (src, dst) in enumerate(
            (
                (inner, inner_hbm),
                (outer, outer_hbm),
                (z, z_hbm),
                (own, own_hbm),
            )
        )
    ]
    for copy in outs[:3]:
        copy.start()

    even = is_even("col")
    own[...] = jnp.zeros((2, COLUMNS, 2, 256), BF16)
    for plane in range(3):
        rows = slice(EXT * plane + 2, EXT * plane + 2 + TILE)
        x = z[plane].astype(F32)
        own[0, rows], own[1, rows] = both(even, x[:, 0:2], x[:, TILE - 2 : TILE])
    x, y = z[3].astype(F32), z[4].astype(F32)
    rows = slice(3 * EXT + 1, 3 * EXT + 1 + TILE)
    own[0, rows], own[1, rows] = both(
        even, pair_of(x[:, 0:1], y[:, 0:1]), pair_of(x[:, TILE - 1 : TILE], y[:, TILE - 1 : TILE])
    )
    for copy in outs[3:]:
        copy.start()
    for copy in outs:
        copy.wait()


def split(bottom_in, skip_feat, cotangent):
    anywhere = pl.BlockSpec(memory_space=pl.ANY)
    fine = (2 * TILE, 2 * TILE, 128)
    shapes = ((5, TILE, TILE, 256),) + ((7, TILE, 256),) * 2 + ((2, COLUMNS, 2, 256),)
    return pl.pallas_call(
        split_kernel,
        out_shape=tuple(jax.ShapeDtypeStruct(shape, BF16) for shape in shapes),
        in_specs=[anywhere] * 3,
        out_specs=(anywhere,) * len(shapes),
        scratch_shapes=[
            pltpu.VMEM((TILE, TILE, 256), BF16),
            pltpu.VMEM(fine, BF16),
            pltpu.VMEM(fine, BF16),
            pltpu.VMEM(fine, F32),
        ]
        + [pltpu.VMEM(shape, BF16) for shape in shapes]
        + [pltpu.SemaphoreType.DMA((3,)), pltpu.SemaphoreType.DMA((len(shapes),))],
        compiler_params=pltpu.CompilerParams(vmem_limit_bytes=FIRST_LIMIT),
    )(bottom_in, skip_feat, cotangent)


def ends_kernel(own, got_inner, got_outer, inner_ref, outer_ref):
    inner_ref[...] = own[1]
    outer_ref[...] = own[0]
    got = got_inner[...].astype(F32), got_outer[...].astype(F32)
    even = is_even("row")
    up, down = jnp.where(even, got[1], got[0]), jnp.where(even, got[0], got[1])
    even = is_even("col")
    for plane in range(3):
        for x, at in ((up, EXT * plane), (down, EXT * plane + 2 + TILE)):
            x = x[2 * plane : 2 * plane + 2]
            inner_ref[at : at + 2], outer_ref[at : at + 2] = both(
                even, x[:, 0:2], x[:, TILE - 2 : TILE]
            )
    zero = jnp.zeros((1, 1, 256), F32)
    x, at = up[6:7], slice(3 * EXT, 3 * EXT + 1)
    inner_ref[at], outer_ref[at] = both(
        even, pair_of(zero, x[:, 0:1]), pair_of(zero, x[:, TILE - 1 : TILE])
    )
    x, at = down[6:7], slice(3 * EXT + 17, 3 * EXT + 18)
    inner_ref[at], outer_ref[at] = both(
        even, pair_of(x[:, 0:1], zero), pair_of(x[:, TILE - 1 : TILE], zero)
    )


def with_ends(*strips):
    vmem = pl.BlockSpec(memory_space=pltpu.VMEM)
    shape = jax.ShapeDtypeStruct((COLUMNS, 2, 256), BF16)
    return pl.pallas_call(
        ends_kernel,
        out_shape=(shape, shape),
        in_specs=[vmem] * 3,
        out_specs=(vmem, vmem),
        compiler_params=pltpu.CompilerParams(vmem_limit_bytes=8 << 20),
        cost_estimate=pl.CostEstimate(flops=0, bytes_accessed=20000000, transcendentals=0),
    )(*strips)


def nn(a, b):
    return lax.dot_general(a, b, (((1,), (0,)), ((), ())), preferred_element_type=F32)


def nt(a, b):
    return lax.dot_general(a, b, (((1,), (1,)), ((), ())), preferred_element_type=F32)


def tn(a, b):
    return lax.dot_general(a, b, (((0,), (0,)), ((), ())), preferred_element_type=F32)


def flat(x):
    return x.reshape(-1, x.shape[-1])


def left(x):
    return pltpu.roll(x, 1, 0)


def right(x):
    return pltpu.roll(x, x.shape[0] - 1, 0)


def core_of(x):
    rows = x.shape[0] // PITCH
    return x.reshape(rows, PITCH, x.shape[1])[:, CORE : CORE + TILE]


def three(x):
    return (left(x), x, right(x))


def four(x):
    return (left(x[:, 128:]), x, right(x[:, :128]))


def fine_row(offset):
    return offset % 2, offset // 2


def pair_weight(taps, zero):
    first = jnp.concatenate([taps[0], taps[1], taps[2], zero], axis=0)
    second = jnp.concatenate([zero, taps[0], taps[1], taps[2]], axis=0)
    return jnp.concatenate([first, second], axis=1)


def pair_weight_back(taps, zero):
    first = jnp.concatenate([taps[0], taps[1], taps[2], zero], axis=1)
    second = jnp.concatenate([zero, taps[0], taps[1], taps[2]], axis=1)
    return jnp.concatenate([first, second], axis=0)


def main_kernel(
    scale, pos_ref, z_ref, row_in, row_out, col_in, col_out, bk_ref, uk_ref, flip_ref,
    mix4c, pg3c, keep_ref, send_ref,
    ext, bot3, botc, act3, actc, dsilu, cot4, mg4, mg4c, pgc, packed, sems,
):
    row0 = pos_ref[0] * TILE
    col0 = pos_ref[1] * TILE
    image_h = pos_ref[2]
    image_w = pos_ref[3]
    mine = pos_ref[4]

    def before_behind(inner, outer, even):
        inner, outer = inner.astype(F32), outer.astype(F32)
        return jnp.where(even, outer, inner), jnp.where(even, inner, outer)

    core = slice(CORE, CORE + TILE)
    low, high = slice(CORE - 2, CORE), slice(CORE + TILE, CORE + TILE + 2)
    even_row, even_col = is_even("row"), is_even("col")
    ext[...] = jnp.zeros_like(ext)
    for plane in range(5):
        ext[plane, 2 : 2 + TILE, core, :] = z_ref[4 - plane].astype(F32)
    for plane in range(3):
        two = slice(2 * plane, 2 * plane + 2)
        ext[plane, 0:2, core, :], ext[plane, 2 + TILE : EXT, core, :] = before_behind(
            row_in[two], row_out[two], even_row
        )
        side = slice(EXT * plane, EXT * plane + EXT)
        ext[plane, :, low, :], ext[plane, :, high, :] = before_behind(
            col_in[side], col_out[side], even_col
        )
    ext[4, 1, core, :], ext[3, 2 + TILE, core, :] = before_behind(row_in[6], row_out[6], even_row)
    low, high = slice(CORE - 1, CORE), slice(CORE + TILE, CORE + TILE + 1)
    for par in range(2):
        side = slice(3 * EXT, 3 * EXT + 18)
        ext[3 + par, 1:19, low, :], ext[3 + par, 1:19, high, :] = before_behind(
            col_in[side, par : par + 1], col_out[side, par : par + 1], even_col
        )

    def masked(x, first):
        rows = x.shape[0] // PITCH
        x = x.reshape(rows, PITCH, x.shape[1])
        i = lax.broadcasted_iota(jnp.int32, x.shape, 0) + (row0 + first - 2)
        w = lax.broadcasted_iota(jnp.int32, x.shape, 1)
        j = w + (col0 - CORE)
        keep = (i >= 0) & (i < image_h) & (j >= 0) & (j < image_w)
        keep = keep & (w >= CORE - 2) & (w < CORE + TILE + 2)
        return flat(jnp.where(keep, x, 0.0))

    zero = jnp.zeros((128, 128), BF16)

    for b, part in enumerate(three(flat(ext[0]))):
        lanes = slice(256 * b, 256 * b + 256)
        bot3[:, :, lanes] = part.reshape(EXT, PITCH, 256).astype(BF16)
        botc[:, :, lanes] = core_of(part)[1 : 19].astype(BF16)
    pre = jnp.zeros((18 * PITCH, 256), F32)
    for a in range(3):
        pre = pre + nn(flat(bot3[a : a + 18]), bk_ref[a].reshape(768, 256))
    sigma = jax.nn.sigmoid(pre)
    dsilu[...] = sigma * (1.0 + pre * (1.0 - sigma))
    activ = masked((pre * sigma).astype(BF16).astype(F32), 1)
    act3[0] = jnp.zeros((PITCH, 768), BF16)
    act3[EXT - 1] = jnp.zeros((PITCH, 768), BF16)
    for b, part in enumerate(three(activ)):
        act3[1:19, :, 256 * b : 256 * b + 256] = part.reshape(18, PITCH, 256).astype(BF16)
    actc[...] = flat(core_of(activ)[1:17]).astype(BF16)

    for par in range(2):
        a, b, c = four(flat(ext[1 + par]))
        cot4[par, :, :, 0:128] = a.reshape(EXT, PITCH, 128).astype(BF16)
        cot4[par, :, :, 128:384] = b.reshape(EXT, PITCH, 256).astype(BF16)
        cot4[par, :, :, 384:512] = c.reshape(EXT, PITCH, 128).astype(BF16)
    for par in range(2):
        first = 1 - par
        total = jnp.zeros((19 * PITCH, 256), F32)
        for a in range(3):
            src, shift = fine_row(par + a - 1)
            weight = pair_weight_back([flip_ref[a, b] for b in range(3)], zero)
            total = total + nt(flat(cot4[src, first + shift : first + shift + 19]), weight)
        grad = masked(total.astype(BF16).astype(F32), first)
        a, b, c = four(grad)
        mg4[par, first : first + 19, :, 0:128] = a.reshape(19, PITCH, 128).astype(BF16)
        mg4[par, first : first + 19, :, 128:384] = b.reshape(19, PITCH, 256).astype(BF16)
        mg4[par, first : first + 19, :, 384:512] = c.reshape(19, PITCH, 128).astype(BF16)
        mg4c[par, first : first + 19, :, 0:128] = core_of(a).astype(BF16)
        mg4c[par, first : first + 19, :, 128:384] = core_of(b).astype(BF16)
        mg4c[par, first : first + 19, :, 384:512] = core_of(c).astype(BF16)

    def put(half, row, value):
        packed[half, row : row + value.shape[0], :] = (value * scale).astype(BF16)

    def hand_out(number, half, first, count, act):
        rows = pl.ds(first, count)
        for which in range(2):

            @pl.when(mine == which)
            def _():
                out = keep_ref if half == which else send_ref
                act(pltpu.make_async_copy(packed.at[half, rows], out.at[rows], sems.at[number]))

    parts = ((0, 0, 0, 4096), (1, 1, 0, 4608), (2, 0, 4096, HALF - 4096), (3, 1, 4608, HALF - 4608))

    act_t = actc[...].T
    for a in range(4):
        src, shift = fine_row(a - 1)
        prod = nn(act_t, flat(mg4c[src, 2 + shift : 18 + shift]))
        for b in range(4):
            put(0, (4 * a + b) * 256, prod[:, 128 * b : 128 * b + 128])
    hand_out(*parts[0], lambda copy: copy.start())

    agrad = jnp.zeros((18 * PITCH, 256), F32)
    for a in range(4):
        src, shift = fine_row(a - 1)
        weight = jnp.concatenate([uk_ref[a, 3 - b] for b in range(4)], axis=1)
        agrad = agrad + nt(flat(mg4[src, 1 + shift : 19 + shift]), weight)
    pgrad = masked((agrad * dsilu[...]).astype(BF16).astype(F32), 1)
    for b, part in enumerate(three(pgrad)):
        pg3c[:, :, 256 * b : 256 * b + 256] = core_of(part).astype(BF16)
    pgc[...] = flat(core_of(pgrad)[1:17]).astype(BF16)

    for a in range(3):
        prod = tn(flat(botc[a : a + 16]), pgc[...])
        put(1, 768 * a, prod[:, :128])
        put(1, 2304 + 768 * a, prod[:, 128:])
    hand_out(*parts[1], lambda copy: copy.start())

    for par in range(2):
        total = flat(ext[3 + par, 1:19])
        for row_k, shift in (((1, 0), (3, -1)), ((0, 1), (2, 0)))[par]:
            k = [uk_ref[row_k, 3 - b] for b in range(4)]
            none = jnp.zeros((256, 128), BF16)
            weight = jnp.concatenate(
                [
                    jnp.concatenate([k[3], k[1], none], axis=0),
                    jnp.concatenate([none, k[2], k[0]], axis=0),
                ],
                axis=1,
            )
            total = total + nn(flat(act3[1 + shift : 19 + shift]), weight)
        mixed = masked(total.astype(BF16).astype(F32), 1)
        a, b, c = four(mixed)
        mix4c[par, :, :, 0:128] = core_of(a).astype(BF16)
        mix4c[par, :, :, 128:384] = core_of(b).astype(BF16)
        mix4c[par, :, :, 384:512] = core_of(c).astype(BF16)

    for a in range(3):
        prod = jnp.zeros((512, 256), F32)
        for par in range(2):
            src, shift = fine_row(par + a - 1)
            prod = prod + tn(
                flat(mix4c[src, 1 + shift : 17 + shift]), flat(z_ref[3 - par])
            )
        for b in range(3):
            tap = prod[128 * b : 128 * b + 128, :128] + prod[128 * b + 128 : 128 * b + 256, 128:]
            if a < 2:
                put(0, 4096 + (3 * a + b) * 128, tap)
            else:
                put(1, 4608 + b * 128, tap)
    put(0, 4864, jnp.zeros((HALF - 4864, 128), F32))
    put(1, 4992, jnp.zeros((HALF - 4992, 128), F32))

    for part in parts[2:]:
        hand_out(*part, lambda copy: copy.start())
    for part in parts:
        hand_out(*part, lambda copy: copy.wait())


def rest_kernel(mix4c, pg3c, bk_ref, lk_ref, level_ref, bgrad_ref, inter):
    zero = jnp.zeros((128, 128), BF16)

    for par in range(2):
        total = jnp.zeros((TILE * TILE, 256), F32)
        for a in range(3):
            src, shift = fine_row(par + a - 1)
            weight = pair_weight([lk_ref[a, b] for b in range(3)], zero)
            total = total + nn(flat(mix4c[src, 1 + shift : 17 + shift]), weight)
        total = total.reshape(TILE, TILE, 256)
        for col_par in range(2):
            inter[:, par, pl.ds(col_par, TILE, stride=2), :] = total[
                :, :, 128 * col_par : 128 * col_par + 128
            ]
    level_ref[...] = inter[...].reshape(2 * TILE, 2 * TILE, 128).astype(BF16)

    total = jnp.zeros((TILE * TILE, 256), F32)
    for a in range(3):
        weight = jnp.concatenate([bk_ref[2 - a, 2 - b] for b in range(3)], axis=1)
        total = total + nt(flat(pg3c[a : a + 16]), weight)
    bgrad_ref[...] = total.reshape(TILE, TILE, 256).astype(BF16)


def rest_work(mix4c, pg3c, bot_kernel, lvl_kernel):
    return pl.pallas_call(
        rest_kernel,
        out_shape=(
            jax.ShapeDtypeStruct((2 * TILE, 2 * TILE, 128), BF16),
            jax.ShapeDtypeStruct((TILE, TILE, 256), BF16),
        ),
        scratch_shapes=[pltpu.VMEM((TILE, 2, 2 * TILE, 128), F32)],
        compiler_params=pltpu.CompilerParams(vmem_limit_bytes=16 << 20),
        cost_estimate=pl.CostEstimate(
            flops=1000000000, bytes_accessed=3000000, transcendentals=0
        ),
    )(mix4c, pg3c, bot_kernel, lvl_kernel)


def local_work(scale, pos, *operands):
    vmem = pl.BlockSpec(memory_space=pltpu.VMEM)
    anywhere = pl.BlockSpec(memory_space=pl.ANY)
    shapes = ((2, 18, TILE, 512), (18, TILE, 768), (HALF, 128), (HALF, 128))
    return pl.pallas_call(
        functools.partial(main_kernel, scale),
        out_shape=tuple(jax.ShapeDtypeStruct(shape, BF16) for shape in shapes),
        in_specs=[pl.BlockSpec(memory_space=pltpu.SMEM)] + [vmem] * len(operands),
        out_specs=(vmem, vmem, anywhere, anywhere),
        scratch_shapes=[
            pltpu.VMEM((5, EXT, PITCH, 256), F32),
            pltpu.VMEM((EXT, PITCH, 768), BF16),
            pltpu.VMEM((18, TILE, 768), BF16),
            pltpu.VMEM((EXT, PITCH, 768), BF16),
            pltpu.VMEM((TILE * TILE, 256), BF16),
            pltpu.VMEM((18 * PITCH, 256), F32),
            pltpu.VMEM((2, EXT, PITCH, 512), BF16),
            pltpu.VMEM((2, EXT, PITCH, 512), BF16),
            pltpu.VMEM((2, EXT, TILE, 512), BF16),
            pltpu.VMEM((TILE * TILE, 256), BF16),
            pltpu.VMEM((2, HALF, 128), BF16),
            pltpu.SemaphoreType.DMA((4,)),
        ],
        compiler_params=pltpu.CompilerParams(vmem_limit_bytes=MAIN_LIMIT),
    )(pos, *operands)


def unpack_kernel(half_of, pos_ref, half, *refs):
    up_hbm, bot_hbm, lvl_hbm, up, bot, lvl, sems = refs[-7:]

    @pl.when(pos_ref[4] == half_of)
    def _():
        copies = []
        for i in range(4):
            rows = pl.ds(1024 * i, 1024)
            up[rows] = half[rows].astype(F32)
            copies.append(pltpu.make_async_copy(up.at[rows], up_hbm.at[rows], sems.at[i]))
            copies[-1].start()
        rows = pl.ds(0, 768)
        lvl[rows] = half[4096:4864].astype(F32)
        copies.append(pltpu.make_async_copy(lvl.at[rows], lvl_hbm.at[rows], sems.at[4]))
        copies[-1].start()
        for copy in copies:
            copy.wait()

    @pl.when(pos_ref[4] != half_of)
    def _():
        copies = []
        for i in range(3):
            rows = pl.ds(768 * i, 768)
            bot[rows, 0:128] = half[768 * i : 768 * i + 768].astype(F32)
            bot[rows, 128:256] = half[2304 + 768 * i : 3072 + 768 * i].astype(F32)
            copies.append(pltpu.make_async_copy(bot.at[rows], bot_hbm.at[rows], sems.at[i]))
            copies[-1].start()
        rows = pl.ds(768, 384)
        lvl[rows] = half[4608:4992].astype(F32)
        copies.append(pltpu.make_async_copy(lvl.at[rows], lvl_hbm.at[rows], sems.at[3]))
        copies[-1].start()
        for copy in copies:
            copy.wait()


def unpack(pos, half, begun=()):
    vmem = pl.BlockSpec(memory_space=pltpu.VMEM)
    anywhere = pl.BlockSpec(memory_space=pl.ANY)
    shapes = ((4096, 128), (2304, 256), (1152, 128))
    return pl.pallas_call(
        functools.partial(unpack_kernel, 1 if begun else 0),
        out_shape=tuple(jax.ShapeDtypeStruct(shape, F32) for shape in shapes),
        in_specs=[pl.BlockSpec(memory_space=pltpu.SMEM), vmem] + [anywhere] * len(begun),
        out_specs=(anywhere,) * 3,
        scratch_shapes=[pltpu.VMEM(shape, F32) for shape in shapes]
        + [pltpu.SemaphoreType.DMA((5,))],
        input_output_aliases={2 + i: i for i in range(len(begun))},
        compiler_params=pltpu.CompilerParams(vmem_limit_bytes=16 << 20),
        cost_estimate=pl.CostEstimate(flops=0, bytes_accessed=4000000, transcendentals=0),
    )(pos, half, *begun)


def swapped(inner, outer, axis):
    return lax.ppermute(inner, axis, INNER_PAIRS), lax.ppermute(outer, axis, OUTER_PAIRS)


def exchange(x, groups):
    return lax.all_to_all(x, AXES, 0, 0, axis_index_groups=groups)


def total_over_devices(keep, send, rest):
    got, rest = lax.optimization_barrier((lax.ppermute(send, "row", CORE_SWAP), rest))
    half = (keep.astype(F32) + got.astype(F32)).astype(BF16)
    for groups, count in ((LINE_GROUPS, LINE), (SHEET_GROUPS, SHEET)):
        parts = exchange(half.reshape(count, -1, 128), groups)
        half = jnp.sum(parts.astype(F32), axis=0).astype(BF16)
    for groups, count in ((SHEET_GROUPS, SHEET), (LINE_GROUPS, LINE)):
        copies = jnp.broadcast_to(half[None], (count,) + half.shape)
        half = exchange(copies, groups).reshape(-1, 128)
    return half, lax.ppermute(half, "row", CORE_SWAP), rest


def on_device(bottom_in, skip_feat, cotangent, bot_kernel, up_kernel, lvl_kernel):
    rows, cols = lax.axis_size("row"), lax.axis_size("col")
    scale = 1.0 / float(2 * TILE * rows * 2 * TILE * cols) ** 0.5
    z, inner, outer, own = split(bottom_in, skip_feat, cotangent)
    row_strips = swapped(inner, outer, "row")
    row_strips, z, turned = lax.optimization_barrier((row_strips, z, up_kernel))
    z, turned = z[::-1], turned[:, ::-1]
    col_strips = swapped(*with_ends(own[::-1], *row_strips), "col")
    row = lax.axis_index("row")
    pos = jnp.stack(
        [row, lax.axis_index("col"), jnp.int32(TILE * rows), jnp.int32(TILE * cols), row % 2]
    ).astype(jnp.int32)
    flip = lvl_kernel[::-1, ::-1]
    mix4c, pg3c, keep, send = local_work(
        scale, pos, z, *row_strips, *col_strips, bot_kernel, turned, flip
    )
    rest = rest_work(mix4c, pg3c, bot_kernel, lvl_kernel)
    half, other, (level_out, bottom_grad) = total_over_devices(keep, send, rest)
    up_grad, bot_grad, lvl_grad = unpack(pos, other, unpack(pos, half))
    return (
        level_out,
        bottom_grad,
        lvl_grad.reshape(3, 3, 128, 128),
        up_grad.reshape(4, 4, 256, 128),
        bot_grad.reshape(3, 3, 256, 256),
    )


def solution(mesh):
    return jax.shard_map(
        on_device,
        mesh=mesh,
        in_specs=(
            P("row", "col", None),
            P("row", "col", None),
            P("row", "col", None),
            P(),
            P(),
            P(),
        ),
        out_specs=(P("row", "col", None), P("row", "col", None), P(), P(), P()),
        check_vma=False,
    )
```

```python
import functools

import jax
import jax.numpy as jnp
from jax import lax
from jax.experimental import pallas as pl
from jax.experimental.pallas import tpu as pltpu
from jax.sharding import PartitionSpec as P

AXES = ("row", "col")
F32 = jnp.float32
BF16 = jnp.bfloat16
TILE = 16
EXT = TILE + 4
PITCH = 32
CORE = 8
MAIN_LIMIT = 40 << 20
FIRST_LIMIT = 56 << 20
HALF = 5120


def place(x, y, z, core):
    row = (((y >> 1) & 1) * 4 + x % 4) * 2 + core
    col = (z % 8) * 2 + (y & 1)
    return row * 16 + col


BLOCK = 32
BLOCK_GROUPS = [
    [place(x, y, z + dz, core) for dz in range(2) for x in range(4) for y in range(4)]
    for z in range(0, 8, 2)
    for core in range(2)
]


def depth_shift(step):
    return [
        (place(x, y, z, core), place(x, y, z + step, core))
        for x in range(4)
        for y in range(4)
        for z in range(8)
        for core in range(2)
    ]


CORE_SWAP = [(i, i ^ 1) for i in range(16)]
INNER_PAIRS = CORE_SWAP
OUTER_PAIRS = [pair for i in range(1, 15, 2) for pair in ((i, i + 1), (i + 1, i))]


COLUMNS = 3 * EXT + 18


def is_even(axis):
    return lax.rem(lax.axis_index(axis), 2) == 0


def both(even, first, last):
    return jnp.where(even, last, first).astype(BF16), jnp.where(even, first, last).astype(BF16)


def pair_of(first, second):
    shape = (first.shape[0], 2, 256)
    odd = lax.broadcasted_iota(jnp.int32, shape, 1) == 1
    return jnp.where(odd, jnp.broadcast_to(second, shape), jnp.broadcast_to(first, shape))


def split_kernel(
    bot_hbm, skip_hbm, cot_hbm, z_hbm, inner_hbm, outer_hbm, own_hbm,
    bot, skip, cot, wide, z, inner, outer, own, sems, out_sems,
):
    copies = [
        pltpu.make_async_copy(src, dst, sems.at[i])
        for i, (src, dst) in enumerate(((cot_hbm, cot), (skip_hbm, skip), (bot_hbm, bot)))
    ]
    for copy in copies:
        copy.start()
    for plane, ref, copy in ((1, cot, copies[0]), (3, skip, copies[1])):
        copy.wait()
        wide[...] = ref[...].astype(F32)
        for col_par in range(2):
            part = wide[:, pl.ds(col_par, TILE, stride=2), :].astype(BF16)
            part = part.reshape(TILE, 2, TILE, 128)
            lanes = slice(col_par * 128, col_par * 128 + 128)
            z[plane, :, :, lanes] = part[:, 0]
            z[plane + 1, :, :, lanes] = part[:, 1]
    copies[2].wait()
    z[0] = bot[...]

    even = is_even("row")
    for plane in range(3):
        two = slice(2 * plane, 2 * plane + 2)
        inner[two], outer[two] = both(even, z[plane, 0:2], z[plane, TILE - 2 : TILE])
    inner[6], outer[6] = both(even, z[3, 0], z[4, TILE - 1])
    outs = [
        pltpu.make_async_copy(src, dst, out_sems.at[i])
        for i, (src, dst) in enumerate(
            (
                (inner, inner_hbm),
                (outer, outer_hbm),
                (z, z_hbm),
                (own, own_hbm),
            )
        )
    ]
    for copy in outs[:3]:
        copy.start()

    even = is_even("col")
    own[...] = jnp.zeros((2, COLUMNS, 2, 256), BF16)
    for plane in range(3):
        rows = slice(EXT * plane + 2, EXT * plane + 2 + TILE)
        x = z[plane].astype(F32)
        own[0, rows], own[1, rows] = both(even, x[:, 0:2], x[:, TILE - 2 : TILE])
    x, y = z[3].astype(F32), z[4].astype(F32)
    rows = slice(3 * EXT + 1, 3 * EXT + 1 + TILE)
    own[0, rows], own[1, rows] = both(
        even, pair_of(x[:, 0:1], y[:, 0:1]), pair_of(x[:, TILE - 1 : TILE], y[:, TILE - 1 : TILE])
    )
    for copy in outs[3:]:
        copy.start()
    for copy in outs:
        copy.wait()


def split(bottom_in, skip_feat, cotangent):
    anywhere = pl.BlockSpec(memory_space=pl.ANY)
    fine = (2 * TILE, 2 * TILE, 128)
    shapes = ((5, TILE, TILE, 256),) + ((7, TILE, 256),) * 2 + ((2, COLUMNS, 2, 256),)
    return pl.pallas_call(
        split_kernel,
        out_shape=tuple(jax.ShapeDtypeStruct(shape, BF16) for shape in shapes),
        in_specs=[anywhere] * 3,
        out_specs=(anywhere,) * len(shapes),
        scratch_shapes=[
            pltpu.VMEM((TILE, TILE, 256), BF16),
            pltpu.VMEM(fine, BF16),
            pltpu.VMEM(fine, BF16),
            pltpu.VMEM(fine, F32),
        ]
        + [pltpu.VMEM(shape, BF16) for shape in shapes]
        + [pltpu.SemaphoreType.DMA((3,)), pltpu.SemaphoreType.DMA((len(shapes),))],
        compiler_params=pltpu.CompilerParams(vmem_limit_bytes=FIRST_LIMIT),
    )(bottom_in, skip_feat, cotangent)


def ends_kernel(own, got_inner, got_outer, inner_ref, outer_ref):
    inner_ref[...] = own[1]
    outer_ref[...] = own[0]
    got = got_inner[...].astype(F32), got_outer[...].astype(F32)
    even = is_even("row")
    up, down = jnp.where(even, got[1], got[0]), jnp.where(even, got[0], got[1])
    even = is_even("col")
    for plane in range(3):
        for x, at in ((up, EXT * plane), (down, EXT * plane + 2 + TILE)):
            x = x[2 * plane : 2 * plane + 2]
            inner_ref[at : at + 2], outer_ref[at : at + 2] = both(
                even, x[:, 0:2], x[:, TILE - 2 : TILE]
            )
    zero = jnp.zeros((1, 1, 256), F32)
    x, at = up[6:7], slice(3 * EXT, 3 * EXT + 1)
    inner_ref[at], outer_ref[at] = both(
        even, pair_of(zero, x[:, 0:1]), pair_of(zero, x[:, TILE - 1 : TILE])
    )
    x, at = down[6:7], slice(3 * EXT + 17, 3 * EXT + 18)
    inner_ref[at], outer_ref[at] = both(
        even, pair_of(x[:, 0:1], zero), pair_of(x[:, TILE - 1 : TILE], zero)
    )


def with_ends(*strips):
    vmem = pl.BlockSpec(memory_space=pltpu.VMEM)
    shape = jax.ShapeDtypeStruct((COLUMNS, 2, 256), BF16)
    return pl.pallas_call(
        ends_kernel,
        out_shape=(shape, shape),
        in_specs=[vmem] * 3,
        out_specs=(vmem, vmem),
        compiler_params=pltpu.CompilerParams(vmem_limit_bytes=8 << 20),
        cost_estimate=pl.CostEstimate(flops=0, bytes_accessed=20000000, transcendentals=0),
    )(*strips)


def nn(a, b):
    return lax.dot_general(a, b, (((1,), (0,)), ((), ())), preferred_element_type=F32)


def nt(a, b):
    return lax.dot_general(a, b, (((1,), (1,)), ((), ())), preferred_element_type=F32)


def tn(a, b):
    return lax.dot_general(a, b, (((0,), (0,)), ((), ())), preferred_element_type=F32)


def flat(x):
    return x.reshape(-1, x.shape[-1])


def left(x):
    return pltpu.roll(x, 1, 0)


def right(x):
    return pltpu.roll(x, x.shape[0] - 1, 0)


def core_of(x):
    rows = x.shape[0] // PITCH
    return x.reshape(rows, PITCH, x.shape[1])[:, CORE : CORE + TILE]


def three(x):
    return (left(x), x, right(x))


def four(x):
    return (left(x[:, 128:]), x, right(x[:, :128]))


def fine_row(offset):
    return offset % 2, offset // 2


def pair_weight(taps, zero):
    first = jnp.concatenate([taps[0], taps[1], taps[2], zero], axis=0)
    second = jnp.concatenate([zero, taps[0], taps[1], taps[2]], axis=0)
    return jnp.concatenate([first, second], axis=1)


def pair_weight_back(taps, zero):
    first = jnp.concatenate([taps[0], taps[1], taps[2], zero], axis=1)
    second = jnp.concatenate([zero, taps[0], taps[1], taps[2]], axis=1)
    return jnp.concatenate([first, second], axis=0)


def main_kernel(
    scale, pos_ref, z_ref, row_in, row_out, col_in, col_out, bk_ref, uk_ref, flip_ref,
    mix4c, pg3c, keep_ref, send_ref,
    ext, bot3, botc, act3, actc, dsilu, cot4, mg4, mg4c, pgc, packed, inside, sems,
):
    row0 = pos_ref[0] * TILE
    col0 = pos_ref[1] * TILE
    image_h = pos_ref[2]
    image_w = pos_ref[3]
    mine = pos_ref[4]

    def before_behind(inner, outer, even):
        inner, outer = inner.astype(F32), outer.astype(F32)
        return jnp.where(even, outer, inner), jnp.where(even, inner, outer)

    core = slice(CORE, CORE + TILE)
    low, high = slice(CORE - 2, CORE), slice(CORE + TILE, CORE + TILE + 2)
    even_row, even_col = is_even("row"), is_even("col")
    ext[:, :, 0:CORE, :] = jnp.zeros((5, EXT, CORE, 256), F32)
    ext[:, :, CORE + TILE : PITCH, :] = jnp.zeros((5, EXT, PITCH - CORE - TILE, 256), F32)
    for end in (0, EXT - 2):
        ext[3:5, end : end + 2, core, :] = jnp.zeros((2, 2, TILE, 256), F32)
    for plane in range(5):
        ext[plane, 2 : 2 + TILE, core, :] = z_ref[4 - plane].astype(F32)
    for plane in range(3):
        two = slice(2 * plane, 2 * plane + 2)
        ext[plane, 0:2, core, :], ext[plane, 2 + TILE : EXT, core, :] = before_behind(
            row_in[two], row_out[two], even_row
        )
        side = slice(EXT * plane, EXT * plane + EXT)
        ext[plane, :, low, :], ext[plane, :, high, :] = before_behind(
            col_in[side], col_out[side], even_col
        )
    ext[4, 1, core, :], ext[3, 2 + TILE, core, :] = before_behind(row_in[6], row_out[6], even_row)
    low, high = slice(CORE - 1, CORE), slice(CORE + TILE, CORE + TILE + 1)
    for par in range(2):
        side = slice(3 * EXT, 3 * EXT + 18)
        ext[3 + par, 1:19, low, :], ext[3 + par, 1:19, high, :] = before_behind(
            col_in[side, par : par + 1], col_out[side, par : par + 1], even_col
        )

    shape = (EXT, PITCH, 128)
    i = lax.broadcasted_iota(jnp.int32, shape, 0) + (row0 - 2)
    w = lax.broadcasted_iota(jnp.int32, shape, 1)
    j = w + (col0 - CORE)
    keep = (i >= 0) & (i < image_h) & (j >= 0) & (j < image_w)
    keep = keep & (w >= CORE - 2) & (w < CORE + TILE + 2)
    inside[...] = flat(jnp.where(keep, 1.0, 0.0))

    def masked(x, first):
        rows = inside[first * PITCH : first * PITCH + x.shape[0]]
        return x * jnp.concatenate([rows, rows], axis=1)

    zero = jnp.zeros((128, 128), BF16)

    for b, part in enumerate(three(flat(ext[0]))):
        lanes = slice(256 * b, 256 * b + 256)
        bot3[:, :, lanes] = part.reshape(EXT, PITCH, 256).astype(BF16)
        botc[:, :, lanes] = core_of(part)[1 : 19].astype(BF16)
    pre = jnp.zeros((18 * PITCH, 256), F32)
    for a in range(3):
        pre = pre + nn(flat(bot3[a : a + 18]), bk_ref[a].reshape(768, 256))
    sigma = jax.nn.sigmoid(pre)
    dsilu[...] = sigma * (1.0 + pre * (1.0 - sigma))
    activ = masked((pre * sigma).astype(BF16).astype(F32), 1)
    act3[0] = jnp.zeros((PITCH, 768), BF16)
    act3[EXT - 1] = jnp.zeros((PITCH, 768), BF16)
    for b, part in enumerate(three(activ)):
        act3[1:19, :, 256 * b : 256 * b + 256] = part.reshape(18, PITCH, 256).astype(BF16)
    actc[...] = flat(core_of(activ)[1:17]).astype(BF16)

    for par in range(2):
        a, b, c = four(flat(ext[1 + par]))
        cot4[par, :, :, 0:128] = a.reshape(EXT, PITCH, 128).astype(BF16)
        cot4[par, :, :, 128:384] = b.reshape(EXT, PITCH, 256).astype(BF16)
        cot4[par, :, :, 384:512] = c.reshape(EXT, PITCH, 128).astype(BF16)
    for par in range(2):
        first = 1 - par
        total = jnp.zeros((19 * PITCH, 256), F32)
        for a in range(3):
            src, shift = fine_row(par + a - 1)
            weight = pair_weight_back([flip_ref[a, b] for b in range(3)], zero)
            total = total + nt(flat(cot4[src, first + shift : first + shift + 19]), weight)
        grad = masked(total.astype(BF16).astype(F32), first)
        a, b, c = four(grad)
        mg4[par, first : first + 19, :, 0:128] = a.reshape(19, PITCH, 128).astype(BF16)
        mg4[par, first : first + 19, :, 128:384] = b.reshape(19, PITCH, 256).astype(BF16)
        mg4[par, first : first + 19, :, 384:512] = c.reshape(19, PITCH, 128).astype(BF16)
        mg4c[par, first : first + 19, :, 0:128] = core_of(a).astype(BF16)
        mg4c[par, first : first + 19, :, 128:384] = core_of(b).astype(BF16)
        mg4c[par, first : first + 19, :, 384:512] = core_of(c).astype(BF16)

    def put(half, row, value):
        packed[half, row : row + value.shape[0], :] = (value * scale).astype(BF16)

    def hand_out(number, half, first, count, act):
        rows = pl.ds(first, count)
        for which in range(2):

            @pl.when(mine == which)
            def _():
                out = keep_ref if half == which else send_ref
                act(pltpu.make_async_copy(packed.at[half, rows], out.at[rows], sems.at[number]))

    parts = ((0, 0, 0, 4096), (1, 1, 0, 4608), (2, 0, 4096, HALF - 4096), (3, 1, 4608, HALF - 4608))

    act_t = actc[...].T
    for a in range(4):
        src, shift = fine_row(a - 1)
        prod = nn(act_t, flat(mg4c[src, 2 + shift : 18 + shift]))
        for b in range(4):
            put(0, (4 * a + b) * 256, prod[:, 128 * b : 128 * b + 128])
    hand_out(*parts[0], lambda copy: copy.start())

    agrad = jnp.zeros((18 * PITCH, 256), F32)
    for a in range(4):
        src, shift = fine_row(a - 1)
        weight = jnp.concatenate([uk_ref[a, 3 - b] for b in range(4)], axis=1)
        agrad = agrad + nt(flat(mg4[src, 1 + shift : 19 + shift]), weight)
    pgrad = masked((agrad * dsilu[...]).astype(BF16).astype(F32), 1)
    for b, part in enumerate(three(pgrad)):
        pg3c[:, :, 256 * b : 256 * b + 256] = core_of(part).astype(BF16)
    pgc[...] = flat(core_of(pgrad)[1:17]).astype(BF16)

    for a in range(3):
        prod = tn(flat(botc[a : a + 16]), pgc[...])
        put(1, 768 * a, prod[:, :128])
        put(1, 2304 + 768 * a, prod[:, 128:])
    hand_out(*parts[1], lambda copy: copy.start())

    for par in range(2):
        total = flat(ext[3 + par, 1:19])
        for row_k, shift in (((1, 0), (3, -1)), ((0, 1), (2, 0)))[par]:
            k = [uk_ref[row_k, 3 - b] for b in range(4)]
            none = jnp.zeros((256, 128), BF16)
            weight = jnp.concatenate(
                [
                    jnp.concatenate([k[3], k[1], none], axis=0),
                    jnp.concatenate([none, k[2], k[0]], axis=0),
                ],
                axis=1,
            )
            total = total + nn(flat(act3[1 + shift : 19 + shift]), weight)
        mixed = masked(total.astype(BF16).astype(F32), 1)
        a, b, c = four(mixed)
        mix4c[par, :, :, 0:128] = core_of(a).astype(BF16)
        mix4c[par, :, :, 128:384] = core_of(b).astype(BF16)
        mix4c[par, :, :, 384:512] = core_of(c).astype(BF16)

    for a in range(3):
        prod = jnp.zeros((512, 256), F32)
        for par in range(2):
            src, shift = fine_row(par + a - 1)
            prod = prod + tn(
                flat(mix4c[src, 1 + shift : 17 + shift]), flat(z_ref[3 - par])
            )
        for b in range(3):
            tap = prod[128 * b : 128 * b + 128, :128] + prod[128 * b + 128 : 128 * b + 256, 128:]
            if a < 2:
                put(0, 4096 + (3 * a + b) * 128, tap)
            else:
                put(1, 4608 + b * 128, tap)
    put(0, 4864, jnp.zeros((HALF - 4864, 128), F32))
    put(1, 4992, jnp.zeros((HALF - 4992, 128), F32))

    for part in parts[2:]:
        hand_out(*part, lambda copy: copy.start())
    for part in parts:
        hand_out(*part, lambda copy: copy.wait())


def rest_kernel(mix4c, pg3c, bk_ref, lk_ref, level_ref, bgrad_ref, inter):
    zero = jnp.zeros((128, 128), BF16)

    for par in range(2):
        total = jnp.zeros((TILE * TILE, 256), F32)
        for a in range(3):
            src, shift = fine_row(par + a - 1)
            weight = pair_weight([lk_ref[a, b] for b in range(3)], zero)
            total = total + nn(flat(mix4c[src, 1 + shift : 17 + shift]), weight)
        total = total.reshape(TILE, TILE, 256)
        for col_par in range(2):
            inter[:, par, pl.ds(col_par, TILE, stride=2), :] = total[
                :, :, 128 * col_par : 128 * col_par + 128
            ]
    level_ref[...] = inter[...].reshape(2 * TILE, 2 * TILE, 128).astype(BF16)

    total = jnp.zeros((TILE * TILE, 256), F32)
    for a in range(3):
        weight = jnp.concatenate([bk_ref[2 - a, 2 - b] for b in range(3)], axis=1)
        total = total + nt(flat(pg3c[a : a + 16]), weight)
    bgrad_ref[...] = total.reshape(TILE, TILE, 256).astype(BF16)


def rest_work(mix4c, pg3c, bot_kernel, lvl_kernel):
    return pl.pallas_call(
        rest_kernel,
        out_shape=(
            jax.ShapeDtypeStruct((2 * TILE, 2 * TILE, 128), BF16),
            jax.ShapeDtypeStruct((TILE, TILE, 256), BF16),
        ),
        scratch_shapes=[pltpu.VMEM((TILE, 2, 2 * TILE, 128), F32)],
        compiler_params=pltpu.CompilerParams(vmem_limit_bytes=16 << 20),
        cost_estimate=pl.CostEstimate(
            flops=1000000000, bytes_accessed=3000000, transcendentals=0
        ),
    )(mix4c, pg3c, bot_kernel, lvl_kernel)


def local_work(scale, pos, *operands):
    vmem = pl.BlockSpec(memory_space=pltpu.VMEM)
    anywhere = pl.BlockSpec(memory_space=pl.ANY)
    shapes = ((2, 18, TILE, 512), (18, TILE, 768), (HALF, 128), (HALF, 128))
    return pl.pallas_call(
        functools.partial(main_kernel, scale),
        out_shape=tuple(jax.ShapeDtypeStruct(shape, BF16) for shape in shapes),
        in_specs=[pl.BlockSpec(memory_space=pltpu.SMEM)] + [vmem] * len(operands),
        out_specs=(vmem, vmem, anywhere, anywhere),
        scratch_shapes=[
            pltpu.VMEM((5, EXT, PITCH, 256), F32),
            pltpu.VMEM((EXT, PITCH, 768), BF16),
            pltpu.VMEM((18, TILE, 768), BF16),
            pltpu.VMEM((EXT, PITCH, 768), BF16),
            pltpu.VMEM((TILE * TILE, 256), BF16),
            pltpu.VMEM((18 * PITCH, 256), F32),
            pltpu.VMEM((2, EXT, PITCH, 512), BF16),
            pltpu.VMEM((2, EXT, PITCH, 512), BF16),
            pltpu.VMEM((2, EXT, TILE, 512), BF16),
            pltpu.VMEM((TILE * TILE, 256), BF16),
            pltpu.VMEM((2, HALF, 128), BF16),
            pltpu.VMEM((EXT * PITCH, 128), F32),
            pltpu.SemaphoreType.DMA((4,)),
        ],
        compiler_params=pltpu.CompilerParams(vmem_limit_bytes=MAIN_LIMIT),
    )(pos, *operands)


def unpack_kernel(half_of, pos_ref, half, *refs):
    up_hbm, bot_hbm, lvl_hbm, up, bot, lvl, sems = refs[-7:]

    @pl.when(pos_ref[4] == half_of)
    def _():
        copies = []
        for i in range(4):
            rows = pl.ds(1024 * i, 1024)
            up[rows] = half[rows].astype(F32)
            copies.append(pltpu.make_async_copy(up.at[rows], up_hbm.at[rows], sems.at[i]))
            copies[-1].start()
        rows = pl.ds(0, 768)
        lvl[rows] = half[4096:4864].astype(F32)
        copies.append(pltpu.make_async_copy(lvl.at[rows], lvl_hbm.at[rows], sems.at[4]))
        copies[-1].start()
        for copy in copies:
            copy.wait()

    @pl.when(pos_ref[4] != half_of)
    def _():
        copies = []
        for i in range(3):
            rows = pl.ds(768 * i, 768)
            bot[rows, 0:128] = half[768 * i : 768 * i + 768].astype(F32)
            bot[rows, 128:256] = half[2304 + 768 * i : 3072 + 768 * i].astype(F32)
            copies.append(pltpu.make_async_copy(bot.at[rows], bot_hbm.at[rows], sems.at[i]))
            copies[-1].start()
        rows = pl.ds(768, 384)
        lvl[rows] = half[4608:4992].astype(F32)
        copies.append(pltpu.make_async_copy(lvl.at[rows], lvl_hbm.at[rows], sems.at[3]))
        copies[-1].start()
        for copy in copies:
            copy.wait()


def unpack(pos, half, begun=()):
    vmem = pl.BlockSpec(memory_space=pltpu.VMEM)
    anywhere = pl.BlockSpec(memory_space=pl.ANY)
    shapes = ((4096, 128), (2304, 256), (1152, 128))
    return pl.pallas_call(
        functools.partial(unpack_kernel, 1 if begun else 0),
        out_shape=tuple(jax.ShapeDtypeStruct(shape, F32) for shape in shapes),
        in_specs=[pl.BlockSpec(memory_space=pltpu.SMEM), vmem] + [anywhere] * len(begun),
        out_specs=(anywhere,) * 3,
        scratch_shapes=[pltpu.VMEM(shape, F32) for shape in shapes]
        + [pltpu.SemaphoreType.DMA((5,))],
        input_output_aliases={2 + i: i for i in range(len(begun))},
        compiler_params=pltpu.CompilerParams(vmem_limit_bytes=16 << 20),
        cost_estimate=pl.CostEstimate(flops=0, bytes_accessed=4000000, transcendentals=0),
    )(pos, half, *begun)


def swapped(inner, outer, axis):
    return lax.ppermute(inner, axis, INNER_PAIRS), lax.ppermute(outer, axis, OUTER_PAIRS)


def exchange(x, groups):
    return lax.all_to_all(x, AXES, 0, 0, axis_index_groups=groups)


def total_over_devices(keep, send, rest):
    got, rest = lax.optimization_barrier((lax.ppermute(send, "row", CORE_SWAP), rest))
    half = (keep.astype(F32) + got.astype(F32)).astype(BF16)
    parts = exchange(half.reshape(BLOCK, HALF // BLOCK, 128), BLOCK_GROUPS)
    part = jnp.sum(parts.astype(F32), axis=0).astype(BF16)
    near = [lax.ppermute(part, AXES, depth_shift(step)).astype(F32) for step in (2, 6)]
    far = lax.ppermute(part, AXES, depth_shift(4)).astype(F32)
    total = ((part.astype(F32) + far) + (near[0] + near[1])).astype(BF16)
    half = exchange(jnp.broadcast_to(total[None], parts.shape), BLOCK_GROUPS).reshape(HALF, 128)
    return half, lax.ppermute(half, "row", CORE_SWAP), rest


def on_device(bottom_in, skip_feat, cotangent, bot_kernel, up_kernel, lvl_kernel):
    rows, cols = lax.axis_size("row"), lax.axis_size("col")
    scale = 1.0 / float(2 * TILE * rows * 2 * TILE * cols) ** 0.5
    z, inner, outer, own = split(bottom_in, skip_feat, cotangent)
    row_strips = swapped(inner, outer, "row")
    row_strips, z, turned = lax.optimization_barrier((row_strips, z, up_kernel))
    z, turned = z[::-1], turned[:, ::-1]
    col_strips = swapped(*with_ends(own[::-1], *row_strips), "col")
    row = lax.axis_index("row")
    pos = jnp.stack(
        [row, lax.axis_index("col"), jnp.int32(TILE * rows), jnp.int32(TILE * cols), row % 2]
    ).astype(jnp.int32)
    flip = lvl_kernel[::-1, ::-1]
    mix4c, pg3c, keep, send = local_work(
        scale, pos, z, *row_strips, *col_strips, bot_kernel, turned, flip
    )
    rest = rest_work(mix4c, pg3c, bot_kernel, lvl_kernel)
    half, other, (level_out, bottom_grad) = total_over_devices(keep, send, rest)
    up_grad, bot_grad, lvl_grad = unpack(pos, other, unpack(pos, half))
    return (
        level_out,
        bottom_grad,
        lvl_grad.reshape(3, 3, 128, 128),
        up_grad.reshape(4, 4, 256, 128),
        bot_grad.reshape(3, 3, 256, 256),
    )


def solution(mesh):
    return jax.shard_map(
        on_device,
        mesh=mesh,
        in_specs=(
            P("row", "col", None),
            P("row", "col", None),
            P("row", "col", None),
            P(),
            P(),
            P(),
        ),
        out_specs=(P("row", "col", None), P("row", "col", None), P(), P(), P()),
        check_vma=False,
    )
```

```python
import functools

import jax
import jax.numpy as jnp
from jax import lax
from jax.experimental import pallas as pl
from jax.experimental.pallas import tpu as pltpu
from jax.sharding import PartitionSpec as P

AXES = ("row", "col")
F32 = jnp.float32
BF16 = jnp.bfloat16
TILE = 16
EXT = TILE + 4
PITCH = 32
CORE = 8
MAIN_LIMIT = 40 << 20
FIRST_LIMIT = 56 << 20
HALF = 5120


def place(x, y, z, core):
    row = (((y >> 1) & 1) * 4 + x % 4) * 2 + core
    col = (z % 8) * 2 + (y & 1)
    return row * 16 + col


BLOCK = 32
BLOCK_GROUPS = [
    [place(x, y, z + dz, core) for dz in range(2) for x in range(4) for y in range(4)]
    for z in range(0, 8, 2)
    for core in range(2)
]


def depth_shift(step):
    return [
        (place(x, y, z, core), place(x, y, z + step, core))
        for x in range(4)
        for y in range(4)
        for z in range(8)
        for core in range(2)
    ]


CORE_SWAP = [(i, i ^ 1) for i in range(16)]
INNER_PAIRS = CORE_SWAP
OUTER_PAIRS = [pair for i in range(1, 15, 2) for pair in ((i, i + 1), (i + 1, i))]


COLUMNS = 3 * EXT + 18


def is_even(axis):
    return lax.rem(lax.axis_index(axis), 2) == 0


def both(even, first, last):
    return jnp.where(even, last, first).astype(BF16), jnp.where(even, first, last).astype(BF16)


def pair_of(first, second):
    shape = (first.shape[0], 2, 256)
    odd = lax.broadcasted_iota(jnp.int32, shape, 1) == 1
    return jnp.where(odd, jnp.broadcast_to(second, shape), jnp.broadcast_to(first, shape))


def split_kernel(
    bot_hbm, skip_hbm, cot_hbm, z_hbm, inner_hbm, outer_hbm, own_hbm,
    bot, skip, cot, wide, z, inner, outer, own, sems, out_sems,
):
    copies = [
        pltpu.make_async_copy(src, dst, sems.at[i])
        for i, (src, dst) in enumerate(((cot_hbm, cot), (skip_hbm, skip), (bot_hbm, bot)))
    ]
    for copy in copies:
        copy.start()
    for plane, ref, copy in ((1, cot, copies[0]), (3, skip, copies[1])):
        copy.wait()
        wide[...] = ref[...].astype(F32)
        for col_par in range(2):
            part = wide[:, pl.ds(col_par, TILE, stride=2), :].astype(BF16)
            part = part.reshape(TILE, 2, TILE, 128)
            lanes = slice(col_par * 128, col_par * 128 + 128)
            z[plane, :, :, lanes] = part[:, 0]
            z[plane + 1, :, :, lanes] = part[:, 1]
    copies[2].wait()
    z[0] = bot[...]

    even = is_even("row")
    for plane in range(3):
        two = slice(2 * plane, 2 * plane + 2)
        inner[two], outer[two] = both(even, z[plane, 0:2], z[plane, TILE - 2 : TILE])
    inner[6], outer[6] = both(even, z[3, 0], z[4, TILE - 1])
    outs = [
        pltpu.make_async_copy(src, dst, out_sems.at[i])
        for i, (src, dst) in enumerate(
            (
                (inner, inner_hbm),
                (outer, outer_hbm),
                (z, z_hbm),
                (own, own_hbm),
            )
        )
    ]
    for copy in outs[:3]:
        copy.start()

    even = is_even("col")
    own[...] = jnp.zeros((2, COLUMNS, 2, 256), BF16)
    for plane in range(3):
        rows = slice(EXT * plane + 2, EXT * plane + 2 + TILE)
        x = z[plane].astype(F32)
        own[0, rows], own[1, rows] = both(even, x[:, 0:2], x[:, TILE - 2 : TILE])
    x, y = z[3].astype(F32), z[4].astype(F32)
    rows = slice(3 * EXT + 1, 3 * EXT + 1 + TILE)
    own[0, rows], own[1, rows] = both(
        even, pair_of(x[:, 0:1], y[:, 0:1]), pair_of(x[:, TILE - 1 : TILE], y[:, TILE - 1 : TILE])
    )
    for copy in outs[3:]:
        copy.start()
    for copy in outs:
        copy.wait()


def split(bottom_in, skip_feat, cotangent):
    anywhere = pl.BlockSpec(memory_space=pl.ANY)
    fine = (2 * TILE, 2 * TILE, 128)
    shapes = ((5, TILE, TILE, 256),) + ((7, TILE, 256),) * 2 + ((2, COLUMNS, 2, 256),)
    return pl.pallas_call(
        split_kernel,
        out_shape=tuple(jax.ShapeDtypeStruct(shape, BF16) for shape in shapes),
        in_specs=[anywhere] * 3,
        out_specs=(anywhere,) * len(shapes),
        scratch_shapes=[
            pltpu.VMEM((TILE, TILE, 256), BF16),
            pltpu.VMEM(fine, BF16),
            pltpu.VMEM(fine, BF16),
            pltpu.VMEM(fine, F32),
        ]
        + [pltpu.VMEM(shape, BF16) for shape in shapes]
        + [pltpu.SemaphoreType.DMA((3,)), pltpu.SemaphoreType.DMA((len(shapes),))],
        compiler_params=pltpu.CompilerParams(vmem_limit_bytes=FIRST_LIMIT),
    )(bottom_in, skip_feat, cotangent)


def ends_kernel(own, got_inner, got_outer, inner_ref, outer_ref):
    inner_ref[...] = own[1]
    outer_ref[...] = own[0]
    got = got_inner[...].astype(F32), got_outer[...].astype(F32)
    even = is_even("row")
    up, down = jnp.where(even, got[1], got[0]), jnp.where(even, got[0], got[1])
    even = is_even("col")
    for plane in range(3):
        for x, at in ((up, EXT * plane), (down, EXT * plane + 2 + TILE)):
            x = x[2 * plane : 2 * plane + 2]
            inner_ref[at : at + 2], outer_ref[at : at + 2] = both(
                even, x[:, 0:2], x[:, TILE - 2 : TILE]
            )
    zero = jnp.zeros((1, 1, 256), F32)
    x, at = up[6:7], slice(3 * EXT, 3 * EXT + 1)
    inner_ref[at], outer_ref[at] = both(
        even, pair_of(zero, x[:, 0:1]), pair_of(zero, x[:, TILE - 1 : TILE])
    )
    x, at = down[6:7], slice(3 * EXT + 17, 3 * EXT + 18)
    inner_ref[at], outer_ref[at] = both(
        even, pair_of(x[:, 0:1], zero), pair_of(x[:, TILE - 1 : TILE], zero)
    )


def with_ends(*strips):
    vmem = pl.BlockSpec(memory_space=pltpu.VMEM)
    shape = jax.ShapeDtypeStruct((COLUMNS, 2, 256), BF16)
    return pl.pallas_call(
        ends_kernel,
        out_shape=(shape, shape),
        in_specs=[vmem] * 3,
        out_specs=(vmem, vmem),
        compiler_params=pltpu.CompilerParams(vmem_limit_bytes=8 << 20),
        cost_estimate=pl.CostEstimate(flops=0, bytes_accessed=20000000, transcendentals=0),
    )(*strips)


def nn(a, b):
    return lax.dot_general(a, b, (((1,), (0,)), ((), ())), preferred_element_type=F32)


def nt(a, b):
    return lax.dot_general(a, b, (((1,), (1,)), ((), ())), preferred_element_type=F32)


def tn(a, b):
    return lax.dot_general(a, b, (((0,), (0,)), ((), ())), preferred_element_type=F32)


def flat(x):
    return x.reshape(-1, x.shape[-1])


def left(x):
    return pltpu.roll(x, 1, 0)


def right(x):
    return pltpu.roll(x, x.shape[0] - 1, 0)


def core_of(x):
    rows = x.shape[0] // PITCH
    return x.reshape(rows, PITCH, x.shape[1])[:, CORE : CORE + TILE]


def three(x):
    return (left(x), x, right(x))


def four(x):
    return (left(x[:, 128:]), x, right(x[:, :128]))


def fine_row(offset):
    return offset % 2, offset // 2


def pair_weight(taps, zero):
    first = jnp.concatenate([taps[0], taps[1], taps[2], zero], axis=0)
    second = jnp.concatenate([zero, taps[0], taps[1], taps[2]], axis=0)
    return jnp.concatenate([first, second], axis=1)


def pair_weight_back(taps, zero):
    first = jnp.concatenate([taps[0], taps[1], taps[2], zero], axis=1)
    second = jnp.concatenate([zero, taps[0], taps[1], taps[2]], axis=1)
    return jnp.concatenate([first, second], axis=0)


def main_kernel(
    scale, pos_ref, z_ref, row_in, row_out, col_in, col_out, bk_ref, uk_ref, flip_ref,
    mix4c, pg3c, keep_ref, send_ref,
    ext, bot3, botc, act3, actc, dsilu, cot4, mg4, mg4c, pgc, packed, inside, sems,
):
    row0 = pos_ref[0] * TILE
    col0 = pos_ref[1] * TILE
    image_h = pos_ref[2]
    image_w = pos_ref[3]
    mine = pos_ref[4]

    def before_behind(inner, outer, even):
        inner, outer = inner.astype(F32), outer.astype(F32)
        return jnp.where(even, outer, inner), jnp.where(even, inner, outer)

    core = slice(CORE, CORE + TILE)
    low, high = slice(CORE - 2, CORE), slice(CORE + TILE, CORE + TILE + 2)
    even_row, even_col = is_even("row"), is_even("col")
    ext[:, :, 0:CORE, :] = jnp.zeros((5, EXT, CORE, 256), F32)
    ext[:, :, CORE + TILE : PITCH, :] = jnp.zeros((5, EXT, PITCH - CORE - TILE, 256), F32)
    for end in (0, EXT - 2):
        ext[3:5, end : end + 2, core, :] = jnp.zeros((2, 2, TILE, 256), F32)
    for plane in range(5):
        ext[plane, 2 : 2 + TILE, core, :] = z_ref[4 - plane].astype(F32)
    for plane in range(3):
        two = slice(2 * plane, 2 * plane + 2)
        ext[plane, 0:2, core, :], ext[plane, 2 + TILE : EXT, core, :] = before_behind(
            row_in[two], row_out[two], even_row
        )
        side = slice(EXT * plane, EXT * plane + EXT)
        ext[plane, :, low, :], ext[plane, :, high, :] = before_behind(
            col_in[side], col_out[side], even_col
        )
    ext[4, 1, core, :], ext[3, 2 + TILE, core, :] = before_behind(row_in[6], row_out[6], even_row)
    low, high = slice(CORE - 1, CORE), slice(CORE + TILE, CORE + TILE + 1)
    for par in range(2):
        side = slice(3 * EXT, 3 * EXT + 18)
        ext[3 + par, 1:19, low, :], ext[3 + par, 1:19, high, :] = before_behind(
            col_in[side, par : par + 1], col_out[side, par : par + 1], even_col
        )

    shape = (EXT, PITCH, 128)
    i = lax.broadcasted_iota(jnp.int32, shape, 0) + (row0 - 2)
    w = lax.broadcasted_iota(jnp.int32, shape, 1)
    j = w + (col0 - CORE)
    keep = (i >= 0) & (i < image_h) & (j >= 0) & (j < image_w)
    keep = keep & (w >= CORE - 2) & (w < CORE + TILE + 2)
    inside[...] = flat(jnp.where(keep, 1.0, 0.0))

    def masked(x, first):
        rows = inside[first * PITCH : first * PITCH + x.shape[0]]
        return x * jnp.concatenate([rows, rows], axis=1)

    zero = jnp.zeros((128, 128), BF16)

    for b, part in enumerate(three(flat(ext[0]))):
        lanes = slice(256 * b, 256 * b + 256)
        bot3[:, :, lanes] = part.reshape(EXT, PITCH, 256).astype(BF16)
        botc[:, :, lanes] = core_of(part)[1 : 19].astype(BF16)
    pre = jnp.zeros((18 * PITCH, 256), F32)
    for a in range(3):
        pre = pre + nn(flat(bot3[a : a + 18]), bk_ref[a].reshape(768, 256))
    sigma = jax.nn.sigmoid(pre)
    dsilu[...] = sigma * (1.0 + pre * (1.0 - sigma))
    activ = masked((pre * sigma).astype(BF16).astype(F32), 1)
    act3[0] = jnp.zeros((PITCH, 768), BF16)
    act3[EXT - 1] = jnp.zeros((PITCH, 768), BF16)
    for b, part in enumerate(three(activ)):
        act3[1:19, :, 256 * b : 256 * b + 256] = part.reshape(18, PITCH, 256).astype(BF16)
    actc[...] = flat(core_of(activ)[1:17]).astype(BF16)

    for par in range(2):
        a, b, c = four(flat(ext[1 + par]))
        cot4[par, :, :, 0:128] = a.reshape(EXT, PITCH, 128).astype(BF16)
        cot4[par, :, :, 128:384] = b.reshape(EXT, PITCH, 256).astype(BF16)
        cot4[par, :, :, 384:512] = c.reshape(EXT, PITCH, 128).astype(BF16)
    for par in range(2):
        first = 1 - par
        total = jnp.zeros((19 * PITCH, 256), F32)
        for a in range(3):
            src, shift = fine_row(par + a - 1)
            weight = pair_weight_back([flip_ref[a, b] for b in range(3)], zero)
            total = total + nt(flat(cot4[src, first + shift : first + shift + 19]), weight)
        grad = masked(total.astype(BF16).astype(F32), first)
        a, b, c = four(grad)
        mg4[par, first : first + 19, :, 0:128] = a.reshape(19, PITCH, 128).astype(BF16)
        mg4[par, first : first + 19, :, 128:384] = b.reshape(19, PITCH, 256).astype(BF16)
        mg4[par, first : first + 19, :, 384:512] = c.reshape(19, PITCH, 128).astype(BF16)
        mg4c[par, first : first + 19, :, 0:128] = core_of(a).astype(BF16)
        mg4c[par, first : first + 19, :, 128:384] = core_of(b).astype(BF16)
        mg4c[par, first : first + 19, :, 384:512] = core_of(c).astype(BF16)

    def put(half, row, value):
        packed[half, row : row + value.shape[0], :] = (value * scale).astype(BF16)

    def hand_out(number, half, first, count, act):
        rows = pl.ds(first, count)
        for which in range(2):

            @pl.when(mine == which)
            def _():
                out = keep_ref if half == which else send_ref
                act(pltpu.make_async_copy(packed.at[half, rows], out.at[rows], sems.at[number]))

    parts = ((0, 0, 0, 4096), (1, 1, 0, 4608), (2, 0, 4096, HALF - 4096), (3, 1, 4608, HALF - 4608))

    act_t = actc[...].T
    for a in range(4):
        src, shift = fine_row(a - 1)
        prod = nn(act_t, flat(mg4c[src, 2 + shift : 18 + shift]))
        for b in range(4):
            put(0, (4 * a + b) * 256, prod[:, 128 * b : 128 * b + 128])
    hand_out(*parts[0], lambda copy: copy.start())

    agrad = jnp.zeros((18 * PITCH, 256), F32)
    for a in range(4):
        src, shift = fine_row(a - 1)
        weight = jnp.concatenate([uk_ref[a, 3 - b] for b in range(4)], axis=1)
        agrad = agrad + nt(flat(mg4[src, 1 + shift : 19 + shift]), weight)
    pgrad = masked((agrad * dsilu[...]).astype(BF16).astype(F32), 1)
    for b, part in enumerate(three(pgrad)):
        pg3c[:, :, 256 * b : 256 * b + 256] = core_of(part).astype(BF16)
    pgc[...] = flat(core_of(pgrad)[1:17]).astype(BF16)

    for a in range(3):
        prod = tn(flat(botc[a : a + 16]), pgc[...])
        put(1, 768 * a, prod[:, :128])
        put(1, 2304 + 768 * a, prod[:, 128:])
    hand_out(*parts[1], lambda copy: copy.start())

    for par in range(2):
        total = flat(ext[3 + par, 1:19])
        for row_k, shift in (((1, 0), (3, -1)), ((0, 1), (2, 0)))[par]:
            k = [uk_ref[row_k, 3 - b] for b in range(4)]
            none = jnp.zeros((256, 128), BF16)
            weight = jnp.concatenate(
                [
                    jnp.concatenate([k[3], k[1], none], axis=0),
                    jnp.concatenate([none, k[2], k[0]], axis=0),
                ],
                axis=1,
            )
            total = total + nn(flat(act3[1 + shift : 19 + shift]), weight)
        mixed = masked(total.astype(BF16).astype(F32), 1)
        a, b, c = four(mixed)
        mix4c[par, :, :, 0:128] = core_of(a).astype(BF16)
        mix4c[par, :, :, 128:384] = core_of(b).astype(BF16)
        mix4c[par, :, :, 384:512] = core_of(c).astype(BF16)

    for a in range(3):
        prod = jnp.zeros((512, 256), F32)
        for par in range(2):
            src, shift = fine_row(par + a - 1)
            prod = prod + tn(
                flat(mix4c[src, 1 + shift : 17 + shift]), flat(z_ref[3 - par])
            )
        for b in range(3):
            tap = prod[128 * b : 128 * b + 128, :128] + prod[128 * b + 128 : 128 * b + 256, 128:]
            if a < 2:
                put(0, 4096 + (3 * a + b) * 128, tap)
            else:
                put(1, 4608 + b * 128, tap)
    put(0, 4864, jnp.zeros((HALF - 4864, 128), F32))
    put(1, 4992, jnp.zeros((HALF - 4992, 128), F32))

    for part in parts[2:]:
        hand_out(*part, lambda copy: copy.start())
    for part in parts:
        hand_out(*part, lambda copy: copy.wait())


def rest_kernel(mix4c, pg3c, bk_ref, lk_ref, level_ref, bgrad_ref, inter):
    zero = jnp.zeros((128, 128), BF16)

    for par in range(2):
        total = jnp.zeros((TILE * TILE, 256), F32)
        for a in range(3):
            src, shift = fine_row(par + a - 1)
            weight = pair_weight([lk_ref[a, b] for b in range(3)], zero)
            total = total + nn(flat(mix4c[src, 1 + shift : 17 + shift]), weight)
        total = total.reshape(TILE, TILE, 256)
        for col_par in range(2):
            inter[:, par, pl.ds(col_par, TILE, stride=2), :] = total[
                :, :, 128 * col_par : 128 * col_par + 128
            ]
    level_ref[...] = inter[...].reshape(2 * TILE, 2 * TILE, 128).astype(BF16)

    total = jnp.zeros((TILE * TILE, 256), F32)
    for a in range(3):
        weight = jnp.concatenate([bk_ref[2 - a, 2 - b] for b in range(3)], axis=1)
        total = total + nt(flat(pg3c[a : a + 16]), weight)
    bgrad_ref[...] = total.reshape(TILE, TILE, 256).astype(BF16)


def rest_work(mix4c, pg3c, bot_kernel, lvl_kernel):
    return pl.pallas_call(
        rest_kernel,
        out_shape=(
            jax.ShapeDtypeStruct((2 * TILE, 2 * TILE, 128), BF16),
            jax.ShapeDtypeStruct((TILE, TILE, 256), BF16),
        ),
        scratch_shapes=[pltpu.VMEM((TILE, 2, 2 * TILE, 128), F32)],
        compiler_params=pltpu.CompilerParams(vmem_limit_bytes=16 << 20),
        cost_estimate=pl.CostEstimate(
            flops=1000000000, bytes_accessed=3000000, transcendentals=0
        ),
    )(mix4c, pg3c, bot_kernel, lvl_kernel)


def local_work(scale, pos, *operands):
    vmem = pl.BlockSpec(memory_space=pltpu.VMEM)
    anywhere = pl.BlockSpec(memory_space=pl.ANY)
    shapes = ((2, 18, TILE, 512), (18, TILE, 768), (HALF, 128), (HALF, 128))
    return pl.pallas_call(
        functools.partial(main_kernel, scale),
        out_shape=tuple(jax.ShapeDtypeStruct(shape, BF16) for shape in shapes),
        in_specs=[pl.BlockSpec(memory_space=pltpu.SMEM)] + [vmem] * len(operands),
        out_specs=(vmem, vmem, anywhere, anywhere),
        scratch_shapes=[
            pltpu.VMEM((5, EXT, PITCH, 256), F32),
            pltpu.VMEM((EXT, PITCH, 768), BF16),
            pltpu.VMEM((18, TILE, 768), BF16),
            pltpu.VMEM((EXT, PITCH, 768), BF16),
            pltpu.VMEM((TILE * TILE, 256), BF16),
            pltpu.VMEM((18 * PITCH, 256), F32),
            pltpu.VMEM((2, EXT, PITCH, 512), BF16),
            pltpu.VMEM((2, EXT, PITCH, 512), BF16),
            pltpu.VMEM((2, EXT, TILE, 512), BF16),
            pltpu.VMEM((TILE * TILE, 256), BF16),
            pltpu.VMEM((2, HALF, 128), BF16),
            pltpu.VMEM((EXT * PITCH, 128), F32),
            pltpu.SemaphoreType.DMA((4,)),
        ],
        compiler_params=pltpu.CompilerParams(vmem_limit_bytes=MAIN_LIMIT),
    )(pos, *operands)


def unpack_kernel(half_of, pos_ref, half, *refs):
    up_hbm, bot_hbm, lvl_hbm, up, bot, lvl, sems = refs[-7:]

    @pl.when(pos_ref[4] == half_of)
    def _():
        copies = []
        for i in range(4):
            rows = pl.ds(1024 * i, 1024)
            up[rows] = half[rows].astype(F32)
            copies.append(pltpu.make_async_copy(up.at[rows], up_hbm.at[rows], sems.at[i]))
            copies[-1].start()
        rows = pl.ds(0, 768)
        lvl[rows] = half[4096:4864].astype(F32)
        copies.append(pltpu.make_async_copy(lvl.at[rows], lvl_hbm.at[rows], sems.at[4]))
        copies[-1].start()
        for copy in copies:
            copy.wait()

    @pl.when(pos_ref[4] != half_of)
    def _():
        copies = []
        for i in range(3):
            rows = pl.ds(768 * i, 768)
            bot[rows, 0:128] = half[768 * i : 768 * i + 768].astype(F32)
            bot[rows, 128:256] = half[2304 + 768 * i : 3072 + 768 * i].astype(F32)
            copies.append(pltpu.make_async_copy(bot.at[rows], bot_hbm.at[rows], sems.at[i]))
            copies[-1].start()
        rows = pl.ds(768, 384)
        lvl[rows] = half[4608:4992].astype(F32)
        copies.append(pltpu.make_async_copy(lvl.at[rows], lvl_hbm.at[rows], sems.at[3]))
        copies[-1].start()
        for copy in copies:
            copy.wait()


def unpack(pos, half, begun=()):
    vmem = pl.BlockSpec(memory_space=pltpu.VMEM)
    anywhere = pl.BlockSpec(memory_space=pl.ANY)
    shapes = ((4096, 128), (2304, 256), (1152, 128))
    return pl.pallas_call(
        functools.partial(unpack_kernel, 1 if begun else 0),
        out_shape=tuple(jax.ShapeDtypeStruct(shape, F32) for shape in shapes),
        in_specs=[pl.BlockSpec(memory_space=pltpu.SMEM), vmem] + [anywhere] * len(begun),
        out_specs=(anywhere,) * 3,
        scratch_shapes=[pltpu.VMEM(shape, F32) for shape in shapes]
        + [pltpu.SemaphoreType.DMA((5,))],
        input_output_aliases={2 + i: i for i in range(len(begun))},
        compiler_params=pltpu.CompilerParams(vmem_limit_bytes=16 << 20),
        cost_estimate=pl.CostEstimate(flops=0, bytes_accessed=4000000, transcendentals=0),
    )(pos, half, *begun)


def swapped(inner, outer, axis):
    return lax.ppermute(inner, axis, INNER_PAIRS), lax.ppermute(outer, axis, OUTER_PAIRS)


def exchange(x, groups):
    return lax.all_to_all(x, AXES, 0, 0, axis_index_groups=groups)


def total_over_devices(keep, send, rest):
    got, rest = lax.optimization_barrier((lax.ppermute(send, "row", CORE_SWAP), rest))
    half = (keep.astype(F32) + got.astype(F32)).astype(BF16)
    parts = exchange(half.reshape(BLOCK, HALF // BLOCK, 128), BLOCK_GROUPS)
    part = jnp.sum(parts.astype(F32), axis=0).astype(BF16)
    far = lax.ppermute(part, AXES, depth_shift(4)).astype(F32)
    near = [lax.ppermute(part, AXES, depth_shift(step)).astype(F32) for step in (2, 6)]
    total = ((near[0] + near[1]) + (far + part.astype(F32))).astype(BF16)
    half = exchange(jnp.broadcast_to(total[None], parts.shape), BLOCK_GROUPS).reshape(HALF, 128)
    return half, lax.ppermute(half, "row", CORE_SWAP), rest


def on_device(bottom_in, skip_feat, cotangent, bot_kernel, up_kernel, lvl_kernel):
    rows, cols = lax.axis_size("row"), lax.axis_size("col")
    scale = 1.0 / float(2 * TILE * rows * 2 * TILE * cols) ** 0.5
    z, inner, outer, own = split(bottom_in, skip_feat, cotangent)
    row_strips = swapped(inner, outer, "row")
    row_strips, z, turned = lax.optimization_barrier((row_strips, z, up_kernel))
    z, turned = z[::-1], turned[:, ::-1]
    col_strips = swapped(*with_ends(own[::-1], *row_strips), "col")
    row = lax.axis_index("row")
    pos = jnp.stack(
        [row, lax.axis_index("col"), jnp.int32(TILE * rows), jnp.int32(TILE * cols), row % 2]
    ).astype(jnp.int32)
    flip = lvl_kernel[::-1, ::-1]
    mix4c, pg3c, keep, send = local_work(
        scale, pos, z, *row_strips, *col_strips, bot_kernel, turned, flip
    )
    rest = rest_work(mix4c, pg3c, bot_kernel, lvl_kernel)
    half, other, (level_out, bottom_grad) = total_over_devices(keep, send, rest)
    up_grad, bot_grad, lvl_grad = unpack(pos, other, unpack(pos, half))
    return (
        level_out,
        bottom_grad,
        lvl_grad.reshape(3, 3, 128, 128),
        up_grad.reshape(4, 4, 256, 128),
        bot_grad.reshape(3, 3, 256, 256),
    )


def solution(mesh):
    return jax.shard_map(
        on_device,
        mesh=mesh,
        in_specs=(
            P("row", "col", None),
            P("row", "col", None),
            P("row", "col", None),
            P(),
            P(),
            P(),
        ),
        out_specs=(P("row", "col", None), P("row", "col", None), P(), P(), P()),
        check_vma=False,
    )
```

```python
import functools

import jax
import jax.numpy as jnp
from jax import lax
from jax.experimental import pallas as pl
from jax.experimental.pallas import tpu as pltpu
from jax.sharding import PartitionSpec as P

AXES = ("row", "col")
F32 = jnp.float32
BF16 = jnp.bfloat16
TILE = 16
EXT = TILE + 4
PITCH = 24
CORE = 2
MAIN_LIMIT = 40 << 20
FIRST_LIMIT = 56 << 20
HALF = 5120


def place(x, y, z, core):
    row = (((y >> 1) & 1) * 4 + x % 4) * 2 + core
    col = (z % 8) * 2 + (y & 1)
    return row * 16 + col


BLOCK = 32
BLOCK_GROUPS = [
    [place(x, y, z + dz, core) for dz in range(2) for x in range(4) for y in range(4)]
    for z in range(0, 8, 2)
    for core in range(2)
]


def depth_shift(step):
    return [
        (place(x, y, z, core), place(x, y, z + step, core))
        for x in range(4)
        for y in range(4)
        for z in range(8)
        for core in range(2)
    ]


CORE_SWAP = [(i, i ^ 1) for i in range(16)]
INNER_PAIRS = CORE_SWAP
OUTER_PAIRS = [pair for i in range(1, 15, 2) for pair in ((i, i + 1), (i + 1, i))]


COLUMNS = 3 * EXT + 18


def is_even(axis):
    return lax.rem(lax.axis_index(axis), 2) == 0


def both(even, first, last):
    return jnp.where(even, last, first).astype(BF16), jnp.where(even, first, last).astype(BF16)


def pair_of(first, second):
    shape = (first.shape[0], 2, 256)
    odd = lax.broadcasted_iota(jnp.int32, shape, 1) == 1
    return jnp.where(odd, jnp.broadcast_to(second, shape), jnp.broadcast_to(first, shape))


def split_kernel(
    bot_hbm, skip_hbm, cot_hbm, z_hbm, inner_hbm, outer_hbm, own_hbm,
    bot, skip, cot, wide, z, inner, outer, own, sems, out_sems,
):
    copies = [
        pltpu.make_async_copy(src, dst, sems.at[i])
        for i, (src, dst) in enumerate(((cot_hbm, cot), (skip_hbm, skip), (bot_hbm, bot)))
    ]
    for copy in copies:
        copy.start()
    for plane, ref, copy in ((1, cot, copies[0]), (3, skip, copies[1])):
        copy.wait()
        wide[...] = ref[...].astype(F32)
        for col_par in range(2):
            part = wide[:, pl.ds(col_par, TILE, stride=2), :].astype(BF16)
            part = part.reshape(TILE, 2, TILE, 128)
            lanes = slice(col_par * 128, col_par * 128 + 128)
            z[plane, :, :, lanes] = part[:, 0]
            z[plane + 1, :, :, lanes] = part[:, 1]
    copies[2].wait()
    z[0] = bot[...]

    even = is_even("row")
    for plane in range(3):
        two = slice(2 * plane, 2 * plane + 2)
        inner[two], outer[two] = both(even, z[plane, 0:2], z[plane, TILE - 2 : TILE])
    inner[6], outer[6] = both(even, z[3, 0], z[4, TILE - 1])
    outs = [
        pltpu.make_async_copy(src, dst, out_sems.at[i])
        for i, (src, dst) in enumerate(
            (
                (inner, inner_hbm),
                (outer, outer_hbm),
                (z, z_hbm),
                (own, own_hbm),
            )
        )
    ]
    for copy in outs[:3]:
        copy.start()

    even = is_even("col")
    own[...] = jnp.zeros((2, COLUMNS, 2, 256), BF16)
    for plane in range(3):
        rows = slice(EXT * plane + 2, EXT * plane + 2 + TILE)
        x = z[plane].astype(F32)
        own[0, rows], own[1, rows] = both(even, x[:, 0:2], x[:, TILE - 2 : TILE])
    x, y = z[3].astype(F32), z[4].astype(F32)
    rows = slice(3 * EXT + 1, 3 * EXT + 1 + TILE)
    own[0, rows], own[1, rows] = both(
        even, pair_of(x[:, 0:1], y[:, 0:1]), pair_of(x[:, TILE - 1 : TILE], y[:, TILE - 1 : TILE])
    )
    for copy in outs[3:]:
        copy.start()
    for copy in outs:
        copy.wait()


def split(bottom_in, skip_feat, cotangent):
    anywhere = pl.BlockSpec(memory_space=pl.ANY)
    fine = (2 * TILE, 2 * TILE, 128)
    shapes = ((5, TILE, TILE, 256),) + ((7, TILE, 256),) * 2 + ((2, COLUMNS, 2, 256),)
    return pl.pallas_call(
        split_kernel,
        out_shape=tuple(jax.ShapeDtypeStruct(shape, BF16) for shape in shapes),
        in_specs=[anywhere] * 3,
        out_specs=(anywhere,) * len(shapes),
        scratch_shapes=[
            pltpu.VMEM((TILE, TILE, 256), BF16),
            pltpu.VMEM(fine, BF16),
            pltpu.VMEM(fine, BF16),
            pltpu.VMEM(fine, F32),
        ]
        + [pltpu.VMEM(shape, BF16) for shape in shapes]
        + [pltpu.SemaphoreType.DMA((3,)), pltpu.SemaphoreType.DMA((len(shapes),))],
        compiler_params=pltpu.CompilerParams(vmem_limit_bytes=FIRST_LIMIT),
    )(bottom_in, skip_feat, cotangent)


def ends_kernel(own, got_inner, got_outer, inner_ref, outer_ref):
    inner_ref[...] = own[1]
    outer_ref[...] = own[0]
    got = got_inner[...].astype(F32), got_outer[...].astype(F32)
    even = is_even("row")
    up, down = jnp.where(even, got[1], got[0]), jnp.where(even, got[0], got[1])
    even = is_even("col")
    for plane in range(3):
        for x, at in ((up, EXT * plane), (down, EXT * plane + 2 + TILE)):
            x = x[2 * plane : 2 * plane + 2]
            inner_ref[at : at + 2], outer_ref[at : at + 2] = both(
                even, x[:, 0:2], x[:, TILE - 2 : TILE]
            )
    zero = jnp.zeros((1, 1, 256), F32)
    x, at = up[6:7], slice(3 * EXT, 3 * EXT + 1)
    inner_ref[at], outer_ref[at] = both(
        even, pair_of(zero, x[:, 0:1]), pair_of(zero, x[:, TILE - 1 : TILE])
    )
    x, at = down[6:7], slice(3 * EXT + 17, 3 * EXT + 18)
    inner_ref[at], outer_ref[at] = both(
        even, pair_of(x[:, 0:1], zero), pair_of(x[:, TILE - 1 : TILE], zero)
    )


def with_ends(*strips):
    vmem = pl.BlockSpec(memory_space=pltpu.VMEM)
    shape = jax.ShapeDtypeStruct((COLUMNS, 2, 256), BF16)
    return pl.pallas_call(
        ends_kernel,
        out_shape=(shape, shape),
        in_specs=[vmem] * 3,
        out_specs=(vmem, vmem),
        compiler_params=pltpu.CompilerParams(vmem_limit_bytes=8 << 20),
        cost_estimate=pl.CostEstimate(flops=0, bytes_accessed=20000000, transcendentals=0),
    )(*strips)


def nn(a, b):
    return lax.dot_general(a, b, (((1,), (0,)), ((), ())), preferred_element_type=F32)


def nt(a, b):
    return lax.dot_general(a, b, (((1,), (1,)), ((), ())), preferred_element_type=F32)


def tn(a, b):
    return lax.dot_general(a, b, (((0,), (0,)), ((), ())), preferred_element_type=F32)


def flat(x):
    return x.reshape(-1, x.shape[-1])


def left(x):
    return pltpu.roll(x, 1, 0)


def right(x):
    return pltpu.roll(x, x.shape[0] - 1, 0)


def core_of(x):
    rows = x.shape[0] // PITCH
    x = pltpu.roll(x, x.shape[0] - CORE, 0)
    return x.reshape(rows, PITCH, x.shape[1])[:, :TILE]


def rows_of(ref, first, count):
    return ref[first * PITCH : first * PITCH + count * PITCH].astype(BF16)


def three(x):
    return (left(x), x, right(x))


def four(x):
    return (left(x[:, 128:]), x, right(x[:, :128]))


def fine_row(offset):
    return offset % 2, offset // 2


def pair_weight(taps, zero):
    first = jnp.concatenate([taps[0], taps[1], taps[2], zero], axis=0)
    second = jnp.concatenate([zero, taps[0], taps[1], taps[2]], axis=0)
    return jnp.concatenate([first, second], axis=1)


def pair_weight_back(taps, zero):
    first = jnp.concatenate([taps[0], taps[1], taps[2], zero], axis=1)
    second = jnp.concatenate([zero, taps[0], taps[1], taps[2]], axis=1)
    return jnp.concatenate([first, second], axis=0)


def main_kernel(
    scale, pos_ref, z_ref, row_in, row_out, col_in, col_out, bk_ref, uk_ref, flip_ref,
    mix4c, pg3c, keep_ref, send_ref,
    ext, bot3, botc, act3, actc, dsilu, cot4, mg4, mg4c, pgc, packed, inside, sems,
):
    row0 = pos_ref[0] * TILE
    col0 = pos_ref[1] * TILE
    image_h = pos_ref[2]
    image_w = pos_ref[3]
    mine = pos_ref[4]

    def before_behind(inner, outer, even):
        inner, outer = inner.astype(F32), outer.astype(F32)
        return jnp.where(even, outer, inner), jnp.where(even, inner, outer)

    core = slice(CORE, CORE + TILE)
    low, high = slice(CORE - 2, CORE), slice(CORE + TILE, CORE + TILE + 2)
    even_row, even_col = is_even("row"), is_even("col")
    ext[...] = jnp.zeros_like(ext)
    for plane in range(5):
        ext[plane, 2 : 2 + TILE, core, :] = z_ref[4 - plane].astype(F32)
    for plane in range(3):
        two = slice(2 * plane, 2 * plane + 2)
        ext[plane, 0:2, core, :], ext[plane, 2 + TILE : EXT, core, :] = before_behind(
            row_in[two], row_out[two], even_row
        )
        side = slice(EXT * plane, EXT * plane + EXT)
        ext[plane, :, low, :], ext[plane, :, high, :] = before_behind(
            col_in[side], col_out[side], even_col
        )
    ext[4, 1, core, :], ext[3, 2 + TILE, core, :] = before_behind(row_in[6], row_out[6], even_row)
    low, high = slice(CORE - 1, CORE), slice(CORE + TILE, CORE + TILE + 1)
    for par in range(2):
        side = slice(3 * EXT, 3 * EXT + 18)
        ext[3 + par, 1:19, low, :], ext[3 + par, 1:19, high, :] = before_behind(
            col_in[side, par : par + 1], col_out[side, par : par + 1], even_col
        )

    shape = (EXT, PITCH, 128)
    i = lax.broadcasted_iota(jnp.int32, shape, 0) + (row0 - 2)
    w = lax.broadcasted_iota(jnp.int32, shape, 1)
    j = w + (col0 - CORE)
    keep = (i >= 0) & (i < image_h) & (j >= 0) & (j < image_w)
    keep = keep & (w >= CORE - 2) & (w < CORE + TILE + 2)
    inside[...] = flat(jnp.where(keep, 1.0, 0.0))

    def masked(x, first):
        rows = inside[first * PITCH : first * PITCH + x.shape[0]]
        return x * jnp.concatenate([rows, rows], axis=1)

    zero = jnp.zeros((128, 128), BF16)

    for b, part in enumerate(three(flat(ext[0]))):
        lanes = slice(256 * b, 256 * b + 256)
        bot3[:, lanes] = part
        botc[:, :, lanes] = core_of(part)[1 : 19].astype(BF16)
    pre = jnp.zeros((18 * PITCH, 256), F32)
    for a in range(3):
        pre = pre + nn(rows_of(bot3, a, 18), bk_ref[a].reshape(768, 256))
    sigma = jax.nn.sigmoid(pre)
    dsilu[...] = sigma * (1.0 + pre * (1.0 - sigma))
    activ = masked((pre * sigma).astype(BF16).astype(F32), 1)
    act3[0:PITCH] = jnp.zeros((PITCH, 768), F32)
    act3[19 * PITCH : EXT * PITCH] = jnp.zeros((PITCH, 768), F32)
    for b, part in enumerate(three(activ)):
        act3[PITCH : 19 * PITCH, 256 * b : 256 * b + 256] = part
    actc[...] = flat(core_of(activ)[1:17]).astype(BF16)

    for par in range(2):
        a, b, c = four(flat(ext[1 + par]))
        cot4[par, 0 : EXT * PITCH, 0:128] = a
        cot4[par, 0 : EXT * PITCH, 128:384] = b
        cot4[par, 0 : EXT * PITCH, 384:512] = c
        cot4[par, EXT * PITCH :] = jnp.zeros((8, 512), F32)
    for par in range(2):
        first = 1 - par
        total = jnp.zeros((19 * PITCH + 8, 256), F32)
        for a in range(3):
            src, shift = fine_row(par + a - 1)
            weight = pair_weight_back([flip_ref[a, b] for b in range(3)], zero)
            start = (first + shift) * PITCH
            rows = cot4[src, start : start + 19 * PITCH + 8].astype(BF16)
            total = total + nt(rows, weight)
        total = total[: 19 * PITCH]
        grad = masked(total.astype(BF16).astype(F32), first)
        a, b, c = four(grad)
        rows = slice(first * PITCH, (first + 19) * PITCH)
        mg4[par, rows, 0:128] = a
        mg4[par, rows, 128:384] = b
        mg4[par, rows, 384:512] = c
        mg4c[par, first : first + 19, :, 0:128] = core_of(a).astype(BF16)
        mg4c[par, first : first + 19, :, 128:384] = core_of(b).astype(BF16)
        mg4c[par, first : first + 19, :, 384:512] = core_of(c).astype(BF16)

    def put(half, row, value):
        packed[half, row : row + value.shape[0], :] = (value * scale).astype(BF16)

    def hand_out(number, half, first, count, act):
        rows = pl.ds(first, count)
        for which in range(2):

            @pl.when(mine == which)
            def _():
                out = keep_ref if half == which else send_ref
                act(pltpu.make_async_copy(packed.at[half, rows], out.at[rows], sems.at[number]))

    parts = ((0, 0, 0, 4096), (1, 1, 0, 4608), (2, 0, 4096, HALF - 4096), (3, 1, 4608, HALF - 4608))

    act_t = actc[...].T
    for a in range(4):
        src, shift = fine_row(a - 1)
        prod = nn(act_t, flat(mg4c[src, 2 + shift : 18 + shift]))
        for b in range(4):
            put(0, (4 * a + b) * 256, prod[:, 128 * b : 128 * b + 128])
    hand_out(*parts[0], lambda copy: copy.start())

    agrad = jnp.zeros((18 * PITCH, 256), F32)
    for a in range(4):
        src, shift = fine_row(a - 1)
        weight = jnp.concatenate([uk_ref[a, 3 - b] for b in range(4)], axis=1)
        agrad = agrad + nt(rows_of(mg4.at[src], 1 + shift, 18), weight)
    pgrad = masked((agrad * dsilu[...]).astype(BF16).astype(F32), 1)
    for b, part in enumerate(three(pgrad)):
        pg3c[:, :, 256 * b : 256 * b + 256] = core_of(part).astype(BF16)
    pgc[...] = flat(core_of(pgrad)[1:17]).astype(BF16)

    for a in range(3):
        prod = tn(flat(botc[a : a + 16]), pgc[...])
        put(1, 768 * a, prod[:, :128])
        put(1, 2304 + 768 * a, prod[:, 128:])
    hand_out(*parts[1], lambda copy: copy.start())

    for par in range(2):
        total = flat(ext[3 + par, 1:19])
        for row_k, shift in (((1, 0), (3, -1)), ((0, 1), (2, 0)))[par]:
            k = [uk_ref[row_k, 3 - b] for b in range(4)]
            none = jnp.zeros((256, 128), BF16)
            weight = jnp.concatenate(
                [
                    jnp.concatenate([k[3], k[1], none], axis=0),
                    jnp.concatenate([none, k[2], k[0]], axis=0),
                ],
                axis=1,
            )
            total = total + nn(rows_of(act3, 1 + shift, 18), weight)
        mixed = masked(total.astype(BF16).astype(F32), 1)
        a, b, c = four(mixed)
        mix4c[par, :, :, 0:128] = core_of(a).astype(BF16)
        mix4c[par, :, :, 128:384] = core_of(b).astype(BF16)
        mix4c[par, :, :, 384:512] = core_of(c).astype(BF16)

    for a in range(3):
        prod = jnp.zeros((512, 256), F32)
        for par in range(2):
            src, shift = fine_row(par + a - 1)
            prod = prod + tn(
                flat(mix4c[src, 1 + shift : 17 + shift]), flat(z_ref[3 - par])
            )
        for b in range(3):
            tap = prod[128 * b : 128 * b + 128, :128] + prod[128 * b + 128 : 128 * b + 256, 128:]
            if a < 2:
                put(0, 4096 + (3 * a + b) * 128, tap)
            else:
                put(1, 4608 + b * 128, tap)
    put(0, 4864, jnp.zeros((HALF - 4864, 128), F32))
    put(1, 4992, jnp.zeros((HALF - 4992, 128), F32))

    for part in parts[2:]:
        hand_out(*part, lambda copy: copy.start())
    for part in parts:
        hand_out(*part, lambda copy: copy.wait())


def rest_kernel(mix4c, pg3c, bk_ref, lk_ref, level_ref, bgrad_ref, inter):
    zero = jnp.zeros((128, 128), BF16)

    for par in range(2):
        total = jnp.zeros((TILE * TILE, 256), F32)
        for a in range(3):
            src, shift = fine_row(par + a - 1)
            weight = pair_weight([lk_ref[a, b] for b in range(3)], zero)
            total = total + nn(flat(mix4c[src, 1 + shift : 17 + shift]), weight)
        total = total.reshape(TILE, TILE, 256)
        for col_par in range(2):
            inter[:, par, pl.ds(col_par, TILE, stride=2), :] = total[
                :, :, 128 * col_par : 128 * col_par + 128
            ]
    level_ref[...] = inter[...].reshape(2 * TILE, 2 * TILE, 128).astype(BF16)

    total = jnp.zeros((TILE * TILE, 256), F32)
    for a in range(3):
        weight = jnp.concatenate([bk_ref[2 - a, 2 - b] for b in range(3)], axis=1)
        total = total + nt(flat(pg3c[a : a + 16]), weight)
    bgrad_ref[...] = total.reshape(TILE, TILE, 256).astype(BF16)


def rest_work(mix4c, pg3c, bot_kernel, lvl_kernel):
    return pl.pallas_call(
        rest_kernel,
        out_shape=(
            jax.ShapeDtypeStruct((2 * TILE, 2 * TILE, 128), BF16),
            jax.ShapeDtypeStruct((TILE, TILE, 256), BF16),
        ),
        scratch_shapes=[pltpu.VMEM((TILE, 2, 2 * TILE, 128), F32)],
        compiler_params=pltpu.CompilerParams(vmem_limit_bytes=16 << 20),
        cost_estimate=pl.CostEstimate(
            flops=1000000000, bytes_accessed=3000000, transcendentals=0
        ),
    )(mix4c, pg3c, bot_kernel, lvl_kernel)


def local_work(scale, pos, *operands):
    vmem = pl.BlockSpec(memory_space=pltpu.VMEM)
    anywhere = pl.BlockSpec(memory_space=pl.ANY)
    shapes = ((2, 18, TILE, 512), (18, TILE, 768), (HALF, 128), (HALF, 128))
    return pl.pallas_call(
        functools.partial(main_kernel, scale),
        out_shape=tuple(jax.ShapeDtypeStruct(shape, BF16) for shape in shapes),
        in_specs=[pl.BlockSpec(memory_space=pltpu.SMEM)] + [vmem] * len(operands),
        out_specs=(vmem, vmem, anywhere, anywhere),
        scratch_shapes=[
            pltpu.VMEM((5, EXT, PITCH, 256), F32),
            pltpu.VMEM((EXT * PITCH, 768), F32),
            pltpu.VMEM((18, TILE, 768), BF16),
            pltpu.VMEM((EXT * PITCH, 768), F32),
            pltpu.VMEM((TILE * TILE, 256), BF16),
            pltpu.VMEM((18 * PITCH, 256), F32),
            pltpu.VMEM((2, EXT * PITCH + 8, 512), F32),
            pltpu.VMEM((2, EXT * PITCH, 512), F32),
            pltpu.VMEM((2, EXT, TILE, 512), BF16),
            pltpu.VMEM((TILE * TILE, 256), BF16),
            pltpu.VMEM((2, HALF, 128), BF16),
            pltpu.VMEM((EXT * PITCH, 128), F32),
            pltpu.SemaphoreType.DMA((4,)),
        ],
        compiler_params=pltpu.CompilerParams(vmem_limit_bytes=MAIN_LIMIT),
    )(pos, *operands)


def unpack_kernel(half_of, pos_ref, half, *refs):
    up_hbm, bot_hbm, lvl_hbm, up, bot, lvl, sems = refs[-7:]

    @pl.when(pos_ref[4] == half_of)
    def _():
        copies = []
        for i in range(4):
            rows = pl.ds(1024 * i, 1024)
            up[rows] = half[rows].astype(F32)
            copies.append(pltpu.make_async_copy(up.at[rows], up_hbm.at[rows], sems.at[i]))
            copies[-1].start()
        rows = pl.ds(0, 768)
        lvl[rows] = half[4096:4864].astype(F32)
        copies.append(pltpu.make_async_copy(lvl.at[rows], lvl_hbm.at[rows], sems.at[4]))
        copies[-1].start()
        for copy in copies:
            copy.wait()

    @pl.when(pos_ref[4] != half_of)
    def _():
        copies = []
        for i in range(3):
            rows = pl.ds(768 * i, 768)
            bot[rows, 0:128] = half[768 * i : 768 * i + 768].astype(F32)
            bot[rows, 128:256] = half[2304 + 768 * i : 3072 + 768 * i].astype(F32)
            copies.append(pltpu.make_async_copy(bot.at[rows], bot_hbm.at[rows], sems.at[i]))
            copies[-1].start()
        rows = pl.ds(768, 384)
        lvl[rows] = half[4608:4992].astype(F32)
        copies.append(pltpu.make_async_copy(lvl.at[rows], lvl_hbm.at[rows], sems.at[3]))
        copies[-1].start()
        for copy in copies:
            copy.wait()


def unpack(pos, half, begun=()):
    vmem = pl.BlockSpec(memory_space=pltpu.VMEM)
    anywhere = pl.BlockSpec(memory_space=pl.ANY)
    shapes = ((4096, 128), (2304, 256), (1152, 128))
    return pl.pallas_call(
        functools.partial(unpack_kernel, 1 if begun else 0),
        out_shape=tuple(jax.ShapeDtypeStruct(shape, F32) for shape in shapes),
        in_specs=[pl.BlockSpec(memory_space=pltpu.SMEM), vmem] + [anywhere] * len(begun),
        out_specs=(anywhere,) * 3,
        scratch_shapes=[pltpu.VMEM(shape, F32) for shape in shapes]
        + [pltpu.SemaphoreType.DMA((5,))],
        input_output_aliases={2 + i: i for i in range(len(begun))},
        compiler_params=pltpu.CompilerParams(vmem_limit_bytes=16 << 20),
        cost_estimate=pl.CostEstimate(flops=0, bytes_accessed=4000000, transcendentals=0),
    )(pos, half, *begun)


def swapped(inner, outer, axis):
    return lax.ppermute(inner, axis, INNER_PAIRS), lax.ppermute(outer, axis, OUTER_PAIRS)


def exchange(x, groups):
    return lax.all_to_all(x, AXES, 0, 0, axis_index_groups=groups)


def total_over_devices(keep, send, rest):
    got, rest = lax.optimization_barrier((lax.ppermute(send, "row", CORE_SWAP), rest))
    half = (keep.astype(F32) + got.astype(F32)).astype(BF16)
    parts = exchange(half.reshape(BLOCK, HALF // BLOCK, 128), BLOCK_GROUPS)
    part = jnp.sum(parts.astype(F32), axis=0).astype(BF16)
    far = lax.ppermute(part, AXES, depth_shift(4)).astype(F32)
    near = [lax.ppermute(part, AXES, depth_shift(step)).astype(F32) for step in (2, 6)]
    total = ((near[0] + near[1]) + (far + part.astype(F32))).astype(BF16)
    half = exchange(jnp.broadcast_to(total[None], parts.shape), BLOCK_GROUPS).reshape(HALF, 128)
    return half, lax.ppermute(half, "row", CORE_SWAP), rest


def on_device(bottom_in, skip_feat, cotangent, bot_kernel, up_kernel, lvl_kernel):
    rows, cols = lax.axis_size("row"), lax.axis_size("col")
    scale = 1.0 / float(2 * TILE * rows * 2 * TILE * cols) ** 0.5
    z, inner, outer, own = split(bottom_in, skip_feat, cotangent)
    row_strips = swapped(inner, outer, "row")
    row_strips, z, turned = lax.optimization_barrier((row_strips, z, up_kernel))
    z, turned = z[::-1], turned[:, ::-1]
    col_strips = swapped(*with_ends(own[::-1], *row_strips), "col")
    row = lax.axis_index("row")
    pos = jnp.stack(
        [row, lax.axis_index("col"), jnp.int32(TILE * rows), jnp.int32(TILE * cols), row % 2]
    ).astype(jnp.int32)
    flip = lvl_kernel[::-1, ::-1]
    mix4c, pg3c, keep, send = local_work(
        scale, pos, z, *row_strips, *col_strips, bot_kernel, turned, flip
    )
    rest = rest_work(mix4c, pg3c, bot_kernel, lvl_kernel)
    half, other, (level_out, bottom_grad) = total_over_devices(keep, send, rest)
    up_grad, bot_grad, lvl_grad = unpack(pos, other, unpack(pos, half))
    return (
        level_out,
        bottom_grad,
        lvl_grad.reshape(3, 3, 128, 128),
        up_grad.reshape(4, 4, 256, 128),
        bot_grad.reshape(3, 3, 256, 256),
    )


def solution(mesh):
    return jax.shard_map(
        on_device,
        mesh=mesh,
        in_specs=(
            P("row", "col", None),
            P("row", "col", None),
            P("row", "col", None),
            P(),
            P(),
            P(),
        ),
        out_specs=(P("row", "col", None), P("row", "col", None), P(), P(), P()),
        check_vma=False,
    )
```

```python
import functools

import jax
import jax.numpy as jnp
from jax import lax
from jax.experimental import pallas as pl
from jax.experimental.pallas import tpu as pltpu
from jax.sharding import PartitionSpec as P

AXES = ("row", "col")
F32 = jnp.float32
BF16 = jnp.bfloat16
TILE = 16
EXT = TILE + 4
PITCH = 24
CORE = 2
MAIN_LIMIT = 40 << 20
FIRST_LIMIT = 56 << 20
HALF = 5120


def place(x, y, z, core):
    row = (((y >> 1) & 1) * 4 + x % 4) * 2 + core
    col = (z % 8) * 2 + (y & 1)
    return row * 16 + col


BLOCK = 32
BLOCK_GROUPS = [
    [place(x, y, z + dz, core) for dz in range(2) for x in range(4) for y in range(4)]
    for z in range(0, 8, 2)
    for core in range(2)
]


def depth_shift(step):
    return [
        (place(x, y, z, core), place(x, y, z + step, core))
        for x in range(4)
        for y in range(4)
        for z in range(8)
        for core in range(2)
    ]


CORE_SWAP = [(i, i ^ 1) for i in range(16)]
INNER_PAIRS = CORE_SWAP
OUTER_PAIRS = [pair for i in range(1, 15, 2) for pair in ((i, i + 1), (i + 1, i))]


COLUMNS = 3 * EXT + 18


def is_even(axis):
    return lax.rem(lax.axis_index(axis), 2) == 0


def both(even, first, last):
    return jnp.where(even, last, first).astype(BF16), jnp.where(even, first, last).astype(BF16)


def pair_of(first, second):
    shape = (first.shape[0], 2, 256)
    odd = lax.broadcasted_iota(jnp.int32, shape, 1) == 1
    return jnp.where(odd, jnp.broadcast_to(second, shape), jnp.broadcast_to(first, shape))


def split_kernel(
    bot_hbm, skip_hbm, cot_hbm, z_hbm, inner_hbm, outer_hbm, own_hbm,
    bot, skip, cot, wide, z, inner, outer, own, sems, out_sems,
):
    copies = [
        pltpu.make_async_copy(src, dst, sems.at[i])
        for i, (src, dst) in enumerate(((cot_hbm, cot), (skip_hbm, skip), (bot_hbm, bot)))
    ]
    for copy in copies:
        copy.start()
    for plane, ref, copy in ((1, cot, copies[0]), (3, skip, copies[1])):
        copy.wait()
        wide[...] = ref[...].astype(F32)
        for col_par in range(2):
            part = wide[:, pl.ds(col_par, TILE, stride=2), :].astype(BF16)
            part = part.reshape(TILE, 2, TILE, 128)
            lanes = slice(col_par * 128, col_par * 128 + 128)
            z[plane, :, :, lanes] = part[:, 0]
            z[plane + 1, :, :, lanes] = part[:, 1]
    copies[2].wait()
    z[0] = bot[...]

    even = is_even("row")
    for plane in range(3):
        two = slice(2 * plane, 2 * plane + 2)
        inner[two], outer[two] = both(even, z[plane, 0:2], z[plane, TILE - 2 : TILE])
    inner[6], outer[6] = both(even, z[3, 0], z[4, TILE - 1])
    outs = [
        pltpu.make_async_copy(src, dst, out_sems.at[i])
        for i, (src, dst) in enumerate(
            (
                (inner, inner_hbm),
                (outer, outer_hbm),
                (z, z_hbm),
                (own, own_hbm),
            )
        )
    ]
    for copy in outs[:3]:
        copy.start()

    even = is_even("col")
    own[...] = jnp.zeros((2, COLUMNS, 2, 256), BF16)
    for plane in range(3):
        rows = slice(EXT * plane + 2, EXT * plane + 2 + TILE)
        x = z[plane].astype(F32)
        own[0, rows], own[1, rows] = both(even, x[:, 0:2], x[:, TILE - 2 : TILE])
    x, y = z[3].astype(F32), z[4].astype(F32)
    rows = slice(3 * EXT + 1, 3 * EXT + 1 + TILE)
    own[0, rows], own[1, rows] = both(
        even, pair_of(x[:, 0:1], y[:, 0:1]), pair_of(x[:, TILE - 1 : TILE], y[:, TILE - 1 : TILE])
    )
    for copy in outs[3:]:
        copy.start()
    for copy in outs:
        copy.wait()


def split(bottom_in, skip_feat, cotangent):
    anywhere = pl.BlockSpec(memory_space=pl.ANY)
    fine = (2 * TILE, 2 * TILE, 128)
    shapes = ((5, TILE, TILE, 256),) + ((7, TILE, 256),) * 2 + ((2, COLUMNS, 2, 256),)
    return pl.pallas_call(
        split_kernel,
        out_shape=tuple(jax.ShapeDtypeStruct(shape, BF16) for shape in shapes),
        in_specs=[anywhere] * 3,
        out_specs=(anywhere,) * len(shapes),
        scratch_shapes=[
            pltpu.VMEM((TILE, TILE, 256), BF16),
            pltpu.VMEM(fine, BF16),
            pltpu.VMEM(fine, BF16),
            pltpu.VMEM(fine, F32),
        ]
        + [pltpu.VMEM(shape, BF16) for shape in shapes]
        + [pltpu.SemaphoreType.DMA((3,)), pltpu.SemaphoreType.DMA((len(shapes),))],
        compiler_params=pltpu.CompilerParams(vmem_limit_bytes=FIRST_LIMIT),
    )(bottom_in, skip_feat, cotangent)


def ends_kernel(own, got_outer, got_inner, inner_ref, outer_ref):
    inner_ref[...] = own[1]
    outer_ref[...] = own[0]
    got = got_inner[...].astype(F32), got_outer[...].astype(F32)
    even = is_even("row")
    up, down = jnp.where(even, got[1], got[0]), jnp.where(even, got[0], got[1])
    even = is_even("col")
    for plane in range(3):
        for x, at in ((up, EXT * plane), (down, EXT * plane + 2 + TILE)):
            x = x[2 * plane : 2 * plane + 2]
            inner_ref[at : at + 2], outer_ref[at : at + 2] = both(
                even, x[:, 0:2], x[:, TILE - 2 : TILE]
            )
    zero = jnp.zeros((1, 1, 256), F32)
    x, at = up[6:7], slice(3 * EXT, 3 * EXT + 1)
    inner_ref[at], outer_ref[at] = both(
        even, pair_of(zero, x[:, 0:1]), pair_of(zero, x[:, TILE - 1 : TILE])
    )
    x, at = down[6:7], slice(3 * EXT + 17, 3 * EXT + 18)
    inner_ref[at], outer_ref[at] = both(
        even, pair_of(x[:, 0:1], zero), pair_of(x[:, TILE - 1 : TILE], zero)
    )


def with_ends(*strips):
    vmem = pl.BlockSpec(memory_space=pltpu.VMEM)
    shape = jax.ShapeDtypeStruct((COLUMNS, 2, 256), BF16)
    return pl.pallas_call(
        ends_kernel,
        out_shape=(shape, shape),
        in_specs=[vmem] * 3,
        out_specs=(vmem, vmem),
        compiler_params=pltpu.CompilerParams(vmem_limit_bytes=8 << 20),
        cost_estimate=pl.CostEstimate(flops=0, bytes_accessed=20000000, transcendentals=0),
    )(*strips)


def nn(a, b):
    return lax.dot_general(a, b, (((1,), (0,)), ((), ())), preferred_element_type=F32)


def nt(a, b):
    return lax.dot_general(a, b, (((1,), (1,)), ((), ())), preferred_element_type=F32)


def tn(a, b):
    return lax.dot_general(a, b, (((0,), (0,)), ((), ())), preferred_element_type=F32)


def flat(x):
    return x.reshape(-1, x.shape[-1])


def left(x):
    return pltpu.roll(x, 1, 0)


def right(x):
    return pltpu.roll(x, x.shape[0] - 1, 0)


def core_of(x):
    rows = x.shape[0] // PITCH
    x = pltpu.roll(x, x.shape[0] - CORE, 0)
    return x.reshape(rows, PITCH, x.shape[1])[:, :TILE]


def rows_of(ref, first, count):
    return ref[first * PITCH : first * PITCH + count * PITCH].astype(BF16)


def three(x):
    return (left(x), x, right(x))


def four(x):
    return (left(x[:, 128:]), x, right(x[:, :128]))


def fine_row(offset):
    return offset % 2, offset // 2


def pair_weight(taps, zero):
    first = jnp.concatenate([taps[0], taps[1], taps[2], zero], axis=0)
    second = jnp.concatenate([zero, taps[0], taps[1], taps[2]], axis=0)
    return jnp.concatenate([first, second], axis=1)


def pair_weight_back(taps, zero):
    first = jnp.concatenate([taps[0], taps[1], taps[2], zero], axis=1)
    second = jnp.concatenate([zero, taps[0], taps[1], taps[2]], axis=1)
    return jnp.concatenate([first, second], axis=0)


def main_kernel(
    scale, pos_ref, z_ref, row_out, row_in, col_out, col_in, bk_ref, uk_ref, flip_ref,
    mix4c, pg3c, keep_ref, send_ref,
    ext, bot3, botc, act3, actc, dsilu, cot4, mg4, mg4c, pgc, packed, inside, sems,
):
    row0 = pos_ref[0] * TILE
    col0 = pos_ref[1] * TILE
    image_h = pos_ref[2]
    image_w = pos_ref[3]
    mine = pos_ref[4]

    def before_behind(inner, outer, even):
        inner, outer = inner.astype(F32), outer.astype(F32)
        return jnp.where(even, outer, inner), jnp.where(even, inner, outer)

    core = slice(CORE, CORE + TILE)
    low, high = slice(CORE - 2, CORE), slice(CORE + TILE, CORE + TILE + 2)
    even_row, even_col = is_even("row"), is_even("col")
    ext[...] = jnp.zeros_like(ext)
    for plane in range(5):
        ext[plane, 2 : 2 + TILE, core, :] = z_ref[4 - plane].astype(F32)
    for plane in range(3):
        two = slice(2 * plane, 2 * plane + 2)
        ext[plane, 0:2, core, :], ext[plane, 2 + TILE : EXT, core, :] = before_behind(
            row_in[two], row_out[two], even_row
        )
        side = slice(EXT * plane, EXT * plane + EXT)
        ext[plane, :, low, :], ext[plane, :, high, :] = before_behind(
            col_in[side], col_out[side], even_col
        )
    ext[4, 1, core, :], ext[3, 2 + TILE, core, :] = before_behind(row_in[6], row_out[6], even_row)
    low, high = slice(CORE - 1, CORE), slice(CORE + TILE, CORE + TILE + 1)
    for par in range(2):
        side = slice(3 * EXT, 3 * EXT + 18)
        ext[3 + par, 1:19, low, :], ext[3 + par, 1:19, high, :] = before_behind(
            col_in[side, par : par + 1], col_out[side, par : par + 1], even_col
        )

    shape = (EXT, PITCH, 128)
    i = lax.broadcasted_iota(jnp.int32, shape, 0) + (row0 - 2)
    w = lax.broadcasted_iota(jnp.int32, shape, 1)
    j = w + (col0 - CORE)
    keep = (i >= 0) & (i < image_h) & (j >= 0) & (j < image_w)
    keep = keep & (w >= CORE - 2) & (w < CORE + TILE + 2)
    inside[...] = flat(jnp.where(keep, 1.0, 0.0))

    def masked(x, first):
        rows = inside[first * PITCH : first * PITCH + x.shape[0]]
        return x * jnp.concatenate([rows, rows], axis=1)

    zero = jnp.zeros((128, 128), BF16)

    for b, part in enumerate(three(flat(ext[0]))):
        lanes = slice(256 * b, 256 * b + 256)
        bot3[:, lanes] = part
        botc[:, :, lanes] = core_of(part)[1 : 19].astype(BF16)
    pre = jnp.zeros((18 * PITCH, 256), F32)
    for a in range(3):
        pre = pre + nn(rows_of(bot3, a, 18), bk_ref[a].reshape(768, 256))
    sigma = jax.nn.sigmoid(pre)
    dsilu[...] = sigma * (1.0 + pre * (1.0 - sigma))
    activ = masked((pre * sigma).astype(BF16).astype(F32), 1)
    act3[0:PITCH] = jnp.zeros((PITCH, 768), F32)
    act3[19 * PITCH : EXT * PITCH] = jnp.zeros((PITCH, 768), F32)
    for b, part in enumerate(three(activ)):
        act3[PITCH : 19 * PITCH, 256 * b : 256 * b + 256] = part
    actc[...] = flat(core_of(activ)[1:17]).astype(BF16)

    for par in range(2):
        a, b, c = four(flat(ext[1 + par]))
        cot4[par, 0 : EXT * PITCH, 0:128] = a
        cot4[par, 0 : EXT * PITCH, 128:384] = b
        cot4[par, 0 : EXT * PITCH, 384:512] = c
        cot4[par, EXT * PITCH :] = jnp.zeros((8, 512), F32)
    for par in range(2):
        first = 1 - par
        total = jnp.zeros((19 * PITCH + 8, 256), F32)
        for a in range(3):
            src, shift = fine_row(par + a - 1)
            weight = pair_weight_back([flip_ref[a, b] for b in range(3)], zero)
            start = (first + shift) * PITCH
            rows = cot4[src, start : start + 19 * PITCH + 8].astype(BF16)
            total = total + nt(rows, weight)
        total = total[: 19 * PITCH]
        grad = masked(total.astype(BF16).astype(F32), first)
        a, b, c = four(grad)
        rows = slice(first * PITCH, (first + 19) * PITCH)
        mg4[par, rows, 0:128] = a
        mg4[par, rows, 128:384] = b
        mg4[par, rows, 384:512] = c
        mg4c[par, first : first + 19, :, 0:128] = core_of(a).astype(BF16)
        mg4c[par, first : first + 19, :, 128:384] = core_of(b).astype(BF16)
        mg4c[par, first : first + 19, :, 384:512] = core_of(c).astype(BF16)

    def put(half, row, value):
        packed[half, row : row + value.shape[0], :] = (value * scale).astype(BF16)

    def hand_out(number, half, first, count, act):
        rows = pl.ds(first, count)
        for which in range(2):

            @pl.when(mine == which)
            def _():
                out = keep_ref if half == which else send_ref
                act(pltpu.make_async_copy(packed.at[half, rows], out.at[rows], sems.at[number]))

    parts = ((0, 0, 0, 4096), (1, 1, 0, 4608), (2, 0, 4096, HALF - 4096), (3, 1, 4608, HALF - 4608))

    act_t = actc[...].T
    for a in range(4):
        src, shift = fine_row(a - 1)
        prod = nn(act_t, flat(mg4c[src, 2 + shift : 18 + shift]))
        for b in range(4):
            put(0, (4 * a + b) * 256, prod[:, 128 * b : 128 * b + 128])
    hand_out(*parts[0], lambda copy: copy.start())

    agrad = jnp.zeros((18 * PITCH, 256), F32)
    for a in range(4):
        src, shift = fine_row(a - 1)
        weight = jnp.concatenate([uk_ref[a, 3 - b] for b in range(4)], axis=1)
        agrad = agrad + nt(rows_of(mg4.at[src], 1 + shift, 18), weight)
    pgrad = masked((agrad * dsilu[...]).astype(BF16).astype(F32), 1)
    for b, part in enumerate(three(pgrad)):
        pg3c[:, :, 256 * b : 256 * b + 256] = core_of(part).astype(BF16)
    pgc[...] = flat(core_of(pgrad)[1:17]).astype(BF16)

    for a in range(3):
        prod = tn(flat(botc[a : a + 16]), pgc[...])
        put(1, 768 * a, prod[:, :128])
        put(1, 2304 + 768 * a, prod[:, 128:])
    hand_out(*parts[1], lambda copy: copy.start())

    for par in range(2):
        total = flat(ext[3 + par, 1:19])
        for row_k, shift in (((1, 0), (3, -1)), ((0, 1), (2, 0)))[par]:
            k = [uk_ref[row_k, 3 - b] for b in range(4)]
            none = jnp.zeros((256, 128), BF16)
            weight = jnp.concatenate(
                [
                    jnp.concatenate([k[3], k[1], none], axis=0),
                    jnp.concatenate([none, k[2], k[0]], axis=0),
                ],
                axis=1,
            )
            total = total + nn(rows_of(act3, 1 + shift, 18), weight)
        mixed = masked(total.astype(BF16).astype(F32), 1)
        a, b, c = four(mixed)
        mix4c[par, :, :, 0:128] = core_of(a).astype(BF16)
        mix4c[par, :, :, 128:384] = core_of(b).astype(BF16)
        mix4c[par, :, :, 384:512] = core_of(c).astype(BF16)

    for a in range(3):
        prod = jnp.zeros((512, 256), F32)
        for par in range(2):
            src, shift = fine_row(par + a - 1)
            prod = prod + tn(
                flat(mix4c[src, 1 + shift : 17 + shift]), flat(z_ref[3 - par])
            )
        for b in range(3):
            tap = prod[128 * b : 128 * b + 128, :128] + prod[128 * b + 128 : 128 * b + 256, 128:]
            if a < 2:
                put(0, 4096 + (3 * a + b) * 128, tap)
            else:
                put(1, 4608 + b * 128, tap)
    put(0, 4864, jnp.zeros((HALF - 4864, 128), F32))
    put(1, 4992, jnp.zeros((HALF - 4992, 128), F32))

    for part in parts[2:]:
        hand_out(*part, lambda copy: copy.start())
    for part in parts:
        hand_out(*part, lambda copy: copy.wait())


def rest_kernel(mix4c, pg3c, bk_ref, lk_ref, level_ref, bgrad_ref, inter):
    zero = jnp.zeros((128, 128), BF16)

    for par in range(2):
        total = jnp.zeros((TILE * TILE, 256), F32)
        for a in range(3):
            src, shift = fine_row(par + a - 1)
            weight = pair_weight([lk_ref[a, b] for b in range(3)], zero)
            total = total + nn(flat(mix4c[src, 1 + shift : 17 + shift]), weight)
        total = total.reshape(TILE, TILE, 256)
        for col_par in range(2):
            inter[:, par, pl.ds(col_par, TILE, stride=2), :] = total[
                :, :, 128 * col_par : 128 * col_par + 128
            ]
    level_ref[...] = inter[...].reshape(2 * TILE, 2 * TILE, 128).astype(BF16)

    total = jnp.zeros((TILE * TILE, 256), F32)
    for a in range(3):
        weight = jnp.concatenate([bk_ref[2 - a, 2 - b] for b in range(3)], axis=1)
        total = total + nt(flat(pg3c[a : a + 16]), weight)
    bgrad_ref[...] = total.reshape(TILE, TILE, 256).astype(BF16)


def rest_work(mix4c, pg3c, bot_kernel, lvl_kernel):
    return pl.pallas_call(
        rest_kernel,
        out_shape=(
            jax.ShapeDtypeStruct((2 * TILE, 2 * TILE, 128), BF16),
            jax.ShapeDtypeStruct((TILE, TILE, 256), BF16),
        ),
        scratch_shapes=[pltpu.VMEM((TILE, 2, 2 * TILE, 128), F32)],
        compiler_params=pltpu.CompilerParams(vmem_limit_bytes=16 << 20),
        cost_estimate=pl.CostEstimate(
            flops=1000000000, bytes_accessed=3000000, transcendentals=0
        ),
    )(mix4c, pg3c, bot_kernel, lvl_kernel)


def local_work(scale, pos, *operands):
    vmem = pl.BlockSpec(memory_space=pltpu.VMEM)
    anywhere = pl.BlockSpec(memory_space=pl.ANY)
    shapes = ((2, 18, TILE, 512), (18, TILE, 768), (HALF, 128), (HALF, 128))
    return pl.pallas_call(
        functools.partial(main_kernel, scale),
        out_shape=tuple(jax.ShapeDtypeStruct(shape, BF16) for shape in shapes),
        in_specs=[pl.BlockSpec(memory_space=pltpu.SMEM)] + [vmem] * len(operands),
        out_specs=(vmem, vmem, anywhere, anywhere),
        scratch_shapes=[
            pltpu.VMEM((5, EXT, PITCH, 256), F32),
            pltpu.VMEM((EXT * PITCH, 768), F32),
            pltpu.VMEM((18, TILE, 768), BF16),
            pltpu.VMEM((EXT * PITCH, 768), F32),
            pltpu.VMEM((TILE * TILE, 256), BF16),
            pltpu.VMEM((18 * PITCH, 256), F32),
            pltpu.VMEM((2, EXT * PITCH + 8, 512), F32),
            pltpu.VMEM((2, EXT * PITCH, 512), F32),
            pltpu.VMEM((2, EXT, TILE, 512), BF16),
            pltpu.VMEM((TILE * TILE, 256), BF16),
            pltpu.VMEM((2, HALF, 128), BF16),
            pltpu.VMEM((EXT * PITCH, 128), F32),
            pltpu.SemaphoreType.DMA((4,)),
        ],
        compiler_params=pltpu.CompilerParams(vmem_limit_bytes=MAIN_LIMIT),
    )(pos, *operands)


def unpack_kernel(half_of, pos_ref, half, *refs):
    up_hbm, bot_hbm, lvl_hbm, up, bot, lvl, sems = refs[-7:]

    @pl.when(pos_ref[4] == half_of)
    def _():
        copies = []
        for i in range(4):
            rows = pl.ds(1024 * i, 1024)
            up[rows] = half[rows].astype(F32)
            copies.append(pltpu.make_async_copy(up.at[rows], up_hbm.at[rows], sems.at[i]))
            copies[-1].start()
        rows = pl.ds(0, 768)
        lvl[rows] = half[4096:4864].astype(F32)
        copies.append(pltpu.make_async_copy(lvl.at[rows], lvl_hbm.at[rows], sems.at[4]))
        copies[-1].start()
        for copy in copies:
            copy.wait()

    @pl.when(pos_ref[4] != half_of)
    def _():
        copies = []
        for i in range(3):
            rows = pl.ds(768 * i, 768)
            bot[rows, 0:128] = half[768 * i : 768 * i + 768].astype(F32)
            bot[rows, 128:256] = half[2304 + 768 * i : 3072 + 768 * i].astype(F32)
            copies.append(pltpu.make_async_copy(bot.at[rows], bot_hbm.at[rows], sems.at[i]))
            copies[-1].start()
        rows = pl.ds(768, 384)
        lvl[rows] = half[4608:4992].astype(F32)
        copies.append(pltpu.make_async_copy(lvl.at[rows], lvl_hbm.at[rows], sems.at[3]))
        copies[-1].start()
        for copy in copies:
            copy.wait()


def unpack(pos, half, begun=()):
    vmem = pl.BlockSpec(memory_space=pltpu.VMEM)
    anywhere = pl.BlockSpec(memory_space=pl.ANY)
    shapes = ((4096, 128), (2304, 256), (1152, 128))
    return pl.pallas_call(
        functools.partial(unpack_kernel, 1 if begun else 0),
        out_shape=tuple(jax.ShapeDtypeStruct(shape, F32) for shape in shapes),
        in_specs=[pl.BlockSpec(memory_space=pltpu.SMEM), vmem] + [anywhere] * len(begun),
        out_specs=(anywhere,) * 3,
        scratch_shapes=[pltpu.VMEM(shape, F32) for shape in shapes]
        + [pltpu.SemaphoreType.DMA((5,))],
        input_output_aliases={2 + i: i for i in range(len(begun))},
        compiler_params=pltpu.CompilerParams(vmem_limit_bytes=16 << 20),
        cost_estimate=pl.CostEstimate(flops=0, bytes_accessed=4000000, transcendentals=0),
    )(pos, half, *begun)


def swapped(inner, outer, axis):
    got_outer = lax.ppermute(outer, axis, OUTER_PAIRS)
    return got_outer, lax.ppermute(inner, axis, INNER_PAIRS)


def exchange(x, groups):
    return lax.all_to_all(x, AXES, 0, 0, axis_index_groups=groups)


def total_over_devices(keep, send, rest):
    got, rest = lax.optimization_barrier((lax.ppermute(send, "row", CORE_SWAP), rest))
    half = (keep.astype(F32) + got.astype(F32)).astype(BF16)
    parts = exchange(half.reshape(BLOCK, HALF // BLOCK, 128), BLOCK_GROUPS)
    part = jnp.sum(parts.astype(F32), axis=0).astype(BF16)
    far = lax.ppermute(part, AXES, depth_shift(4)).astype(F32)
    near = [lax.ppermute(part, AXES, depth_shift(step)).astype(F32) for step in (2, 6)]
    total = ((near[0] + near[1]) + (far + part.astype(F32))).astype(BF16)
    half = exchange(jnp.broadcast_to(total[None], parts.shape), BLOCK_GROUPS).reshape(HALF, 128)
    return half, lax.ppermute(half, "row", CORE_SWAP), rest


def on_device(bottom_in, skip_feat, cotangent, bot_kernel, up_kernel, lvl_kernel):
    rows, cols = lax.axis_size("row"), lax.axis_size("col")
    scale = 1.0 / float(2 * TILE * rows * 2 * TILE * cols) ** 0.5
    z, inner, outer, own = split(bottom_in, skip_feat, cotangent)
    row_strips = swapped(inner, outer, "row")
    row_strips, z, turned = lax.optimization_barrier((row_strips, z, up_kernel))
    z, turned = z[::-1], turned[:, ::-1]
    col_strips = swapped(*with_ends(own[::-1], *row_strips), "col")
    row = lax.axis_index("row")
    pos = jnp.stack(
        [row, lax.axis_index("col"), jnp.int32(TILE * rows), jnp.int32(TILE * cols), row % 2]
    ).astype(jnp.int32)
    flip = lvl_kernel[::-1, ::-1]
    mix4c, pg3c, keep, send = local_work(
        scale, pos, z, *row_strips, *col_strips, bot_kernel, turned, flip
    )
    rest = rest_work(mix4c, pg3c, bot_kernel, lvl_kernel)
    half, other, (level_out, bottom_grad) = total_over_devices(keep, send, rest)
    up_grad, bot_grad, lvl_grad = unpack(pos, other, unpack(pos, half))
    return (
        level_out,
        bottom_grad,
        lvl_grad.reshape(3, 3, 128, 128),
        up_grad.reshape(4, 4, 256, 128),
        bot_grad.reshape(3, 3, 256, 256),
    )


def solution(mesh):
    return jax.shard_map(
        on_device,
        mesh=mesh,
        in_specs=(
            P("row", "col", None),
            P("row", "col", None),
            P("row", "col", None),
            P(),
            P(),
            P(),
        ),
        out_specs=(P("row", "col", None), P("row", "col", None), P(), P(), P()),
        check_vma=False,
    )
```

```python
import functools

import jax
import jax.numpy as jnp
from jax import lax
from jax.experimental import pallas as pl
from jax.experimental.pallas import tpu as pltpu
from jax.sharding import PartitionSpec as P

AXES = ("row", "col")
F32 = jnp.float32
BF16 = jnp.bfloat16
TILE = 16
EXT = TILE + 4
PITCH = 24
CORE = 2
MAIN_LIMIT = 40 << 20
FIRST_LIMIT = 56 << 20
HALF = 5120


def place(x, y, z, core):
    row = (((y >> 1) & 1) * 4 + x % 4) * 2 + core
    col = (z % 8) * 2 + (y & 1)
    return row * 16 + col


BLOCK = 32
BLOCK_GROUPS = [
    [place(x, y, z + dz, core) for dz in range(2) for x in range(4) for y in range(4)]
    for z in range(0, 8, 2)
    for core in range(2)
]


def depth_swap(bit):
    return [
        (place(x, y, z, core), place(x, y, z ^ bit, core))
        for x in range(4)
        for y in range(4)
        for z in range(8)
        for core in range(2)
    ]


CORE_SWAP = [(i, i ^ 1) for i in range(16)]
INNER_PAIRS = CORE_SWAP
OUTER_PAIRS = [pair for i in range(1, 15, 2) for pair in ((i, i + 1), (i + 1, i))]


COLUMNS = 3 * EXT + 18


def is_even(axis):
    return lax.rem(lax.axis_index(axis), 2) == 0


def both(even, first, last):
    return jnp.where(even, last, first).astype(BF16), jnp.where(even, first, last).astype(BF16)


def pair_of(first, second):
    shape = (first.shape[0], 2, 256)
    odd = lax.broadcasted_iota(jnp.int32, shape, 1) == 1
    return jnp.where(odd, jnp.broadcast_to(second, shape), jnp.broadcast_to(first, shape))


def split_kernel(
    bot_hbm, skip_hbm, cot_hbm, z_hbm, inner_hbm, outer_hbm, own_hbm,
    bot, skip, cot, wide, z, inner, outer, own, sems, out_sems,
):
    copies = [
        pltpu.make_async_copy(src, dst, sems.at[i])
        for i, (src, dst) in enumerate(((cot_hbm, cot), (skip_hbm, skip), (bot_hbm, bot)))
    ]
    for copy in copies:
        copy.start()
    for plane, ref, copy in ((1, cot, copies[0]), (3, skip, copies[1])):
        copy.wait()
        wide[...] = ref[...].astype(F32)
        for col_par in range(2):
            part = wide[:, pl.ds(col_par, TILE, stride=2), :].astype(BF16)
            part = part.reshape(TILE, 2, TILE, 128)
            lanes = slice(col_par * 128, col_par * 128 + 128)
            z[plane, :, :, lanes] = part[:, 0]
            z[plane + 1, :, :, lanes] = part[:, 1]
    copies[2].wait()
    z[0] = bot[...]

    even = is_even("row")
    for plane in range(3):
        two = slice(2 * plane, 2 * plane + 2)
        inner[two], outer[two] = both(even, z[plane, 0:2], z[plane, TILE - 2 : TILE])
    inner[6], outer[6] = both(even, z[3, 0], z[4, TILE - 1])
    outs = [
        pltpu.make_async_copy(src, dst, out_sems.at[i])
        for i, (src, dst) in enumerate(
            (
                (inner, inner_hbm),
                (outer, outer_hbm),
                (z, z_hbm),
                (own, own_hbm),
            )
        )
    ]
    for copy in outs[:3]:
        copy.start()

    even = is_even("col")
    own[...] = jnp.zeros((2, COLUMNS, 2, 256), BF16)
    for plane in range(3):
        rows = slice(EXT * plane + 2, EXT * plane + 2 + TILE)
        x = z[plane].astype(F32)
        own[0, rows], own[1, rows] = both(even, x[:, 0:2], x[:, TILE - 2 : TILE])
    x, y = z[3].astype(F32), z[4].astype(F32)
    rows = slice(3 * EXT + 1, 3 * EXT + 1 + TILE)
    own[0, rows], own[1, rows] = both(
        even, pair_of(x[:, 0:1], y[:, 0:1]), pair_of(x[:, TILE - 1 : TILE], y[:, TILE - 1 : TILE])
    )
    for copy in outs[3:]:
        copy.start()
    for copy in outs:
        copy.wait()


def split(bottom_in, skip_feat, cotangent):
    anywhere = pl.BlockSpec(memory_space=pl.ANY)
    fine = (2 * TILE, 2 * TILE, 128)
    shapes = ((5, TILE, TILE, 256),) + ((7, TILE, 256),) * 2 + ((2, COLUMNS, 2, 256),)
    return pl.pallas_call(
        split_kernel,
        out_shape=tuple(jax.ShapeDtypeStruct(shape, BF16) for shape in shapes),
        in_specs=[anywhere] * 3,
        out_specs=(anywhere,) * len(shapes),
        scratch_shapes=[
            pltpu.VMEM((TILE, TILE, 256), BF16),
            pltpu.VMEM(fine, BF16),
            pltpu.VMEM(fine, BF16),
            pltpu.VMEM(fine, F32),
        ]
        + [pltpu.VMEM(shape, BF16) for shape in shapes]
        + [pltpu.SemaphoreType.DMA((3,)), pltpu.SemaphoreType.DMA((len(shapes),))],
        compiler_params=pltpu.CompilerParams(vmem_limit_bytes=FIRST_LIMIT),
    )(bottom_in, skip_feat, cotangent)


def ends_kernel(own, got_outer, got_inner, inner_ref, outer_ref):
    inner_ref[...] = own[1]
    outer_ref[...] = own[0]
    got = got_inner[...].astype(F32), got_outer[...].astype(F32)
    even = is_even("row")
    up, down = jnp.where(even, got[1], got[0]), jnp.where(even, got[0], got[1])
    even = is_even("col")
    for plane in range(3):
        for x, at in ((up, EXT * plane), (down, EXT * plane + 2 + TILE)):
            x = x[2 * plane : 2 * plane + 2]
            inner_ref[at : at + 2], outer_ref[at : at + 2] = both(
                even, x[:, 0:2], x[:, TILE - 2 : TILE]
            )
    zero = jnp.zeros((1, 1, 256), F32)
    x, at = up[6:7], slice(3 * EXT, 3 * EXT + 1)
    inner_ref[at], outer_ref[at] = both(
        even, pair_of(zero, x[:, 0:1]), pair_of(zero, x[:, TILE - 1 : TILE])
    )
    x, at = down[6:7], slice(3 * EXT + 17, 3 * EXT + 18)
    inner_ref[at], outer_ref[at] = both(
        even, pair_of(x[:, 0:1], zero), pair_of(x[:, TILE - 1 : TILE], zero)
    )


def with_ends(*strips):
    vmem = pl.BlockSpec(memory_space=pltpu.VMEM)
    shape = jax.ShapeDtypeStruct((COLUMNS, 2, 256), BF16)
    return pl.pallas_call(
        ends_kernel,
        out_shape=(shape, shape),
        in_specs=[vmem] * 3,
        out_specs=(vmem, vmem),
        compiler_params=pltpu.CompilerParams(vmem_limit_bytes=8 << 20),
        cost_estimate=pl.CostEstimate(flops=0, bytes_accessed=20000000, transcendentals=0),
    )(*strips)


def nn(a, b):
    return lax.dot_general(a, b, (((1,), (0,)), ((), ())), preferred_element_type=F32)


def nt(a, b):
    return lax.dot_general(a, b, (((1,), (1,)), ((), ())), preferred_element_type=F32)


def tn(a, b):
    return lax.dot_general(a, b, (((0,), (0,)), ((), ())), preferred_element_type=F32)


def flat(x):
    return x.reshape(-1, x.shape[-1])


def left(x):
    return pltpu.roll(x, 1, 0)


def right(x):
    return pltpu.roll(x, x.shape[0] - 1, 0)


def core_of(x):
    rows = x.shape[0] // PITCH
    x = pltpu.roll(x, x.shape[0] - CORE, 0)
    return x.reshape(rows, PITCH, x.shape[1])[:, :TILE]


def rows_of(ref, first, count):
    return ref[first * PITCH : first * PITCH + count * PITCH].astype(BF16)


def three(x):
    return (left(x), x, right(x))


def four(x):
    return (left(x[:, 128:]), x, right(x[:, :128]))


def fine_row(offset):
    return offset % 2, offset // 2


def pair_weight(taps, zero):
    first = jnp.concatenate([taps[0], taps[1], taps[2], zero], axis=0)
    second = jnp.concatenate([zero, taps[0], taps[1], taps[2]], axis=0)
    return jnp.concatenate([first, second], axis=1)


def pair_weight_back(taps, zero):
    first = jnp.concatenate([taps[0], taps[1], taps[2], zero], axis=1)
    second = jnp.concatenate([zero, taps[0], taps[1], taps[2]], axis=1)
    return jnp.concatenate([first, second], axis=0)


def main_kernel(
    scale, pos_ref, z_ref, row_out, row_in, col_out, col_in, bk_ref, uk_ref, flip_ref,
    mix4c, pg3c, keep_ref, send_ref,
    ext, bot3, botc, act3, actc, dsilu, cot4, mg4, mg4c, pgc, packed, inside, sems,
):
    row0 = pos_ref[0] * TILE
    col0 = pos_ref[1] * TILE
    image_h = pos_ref[2]
    image_w = pos_ref[3]
    mine = pos_ref[4]

    def before_behind(inner, outer, even):
        inner, outer = inner.astype(F32), outer.astype(F32)
        return jnp.where(even, outer, inner), jnp.where(even, inner, outer)

    core = slice(CORE, CORE + TILE)
    low, high = slice(CORE - 2, CORE), slice(CORE + TILE, CORE + TILE + 2)
    even_row, even_col = is_even("row"), is_even("col")
    ext[...] = jnp.zeros_like(ext)
    for plane in range(5):
        ext[plane, 2 : 2 + TILE, core, :] = z_ref[4 - plane].astype(F32)
    for plane in range(3):
        two = slice(2 * plane, 2 * plane + 2)
        ext[plane, 0:2, core, :], ext[plane, 2 + TILE : EXT, core, :] = before_behind(
            row_in[two], row_out[two], even_row
        )
        side = slice(EXT * plane, EXT * plane + EXT)
        ext[plane, :, low, :], ext[plane, :, high, :] = before_behind(
            col_in[side], col_out[side], even_col
        )
    ext[4, 1, core, :], ext[3, 2 + TILE, core, :] = before_behind(row_in[6], row_out[6], even_row)
    low, high = slice(CORE - 1, CORE), slice(CORE + TILE, CORE + TILE + 1)
    for par in range(2):
        side = slice(3 * EXT, 3 * EXT + 18)
        ext[3 + par, 1:19, low, :], ext[3 + par, 1:19, high, :] = before_behind(
            col_in[side, par : par + 1], col_out[side, par : par + 1], even_col
        )

    shape = (EXT, PITCH, 128)
    i = lax.broadcasted_iota(jnp.int32, shape, 0) + (row0 - 2)
    w = lax.broadcasted_iota(jnp.int32, shape, 1)
    j = w + (col0 - CORE)
    keep = (i >= 0) & (i < image_h) & (j >= 0) & (j < image_w)
    keep = keep & (w >= CORE - 2) & (w < CORE + TILE + 2)
    inside[...] = flat(jnp.where(keep, 1.0, 0.0))

    def masked(x, first):
        rows = inside[first * PITCH : first * PITCH + x.shape[0]]
        return x * jnp.concatenate([rows, rows], axis=1)

    zero = jnp.zeros((128, 128), BF16)

    for b, part in enumerate(three(flat(ext[0]))):
        lanes = slice(256 * b, 256 * b + 256)
        bot3[:, lanes] = part
        botc[:, :, lanes] = core_of(part)[1 : 19].astype(BF16)
    pre = jnp.zeros((18 * PITCH, 256), F32)
    for a in range(3):
        pre = pre + nn(rows_of(bot3, a, 18), bk_ref[a].reshape(768, 256))
    sigma = jax.nn.sigmoid(pre)
    dsilu[...] = sigma * (1.0 + pre * (1.0 - sigma))
    activ = masked((pre * sigma).astype(BF16).astype(F32), 1)
    act3[0:PITCH] = jnp.zeros((PITCH, 768), F32)
    act3[19 * PITCH : EXT * PITCH] = jnp.zeros((PITCH, 768), F32)
    for b, part in enumerate(three(activ)):
        act3[PITCH : 19 * PITCH, 256 * b : 256 * b + 256] = part
    actc[...] = flat(core_of(activ)[1:17]).astype(BF16)

    for par in range(2):
        a, b, c = four(flat(ext[1 + par]))
        cot4[par, 0 : EXT * PITCH, 0:128] = a
        cot4[par, 0 : EXT * PITCH, 128:384] = b
        cot4[par, 0 : EXT * PITCH, 384:512] = c
        cot4[par, EXT * PITCH :] = jnp.zeros((8, 512), F32)
    for par in range(2):
        first = 1 - par
        total = jnp.zeros((19 * PITCH + 8, 256), F32)
        for a in range(3):
            src, shift = fine_row(par + a - 1)
            weight = pair_weight_back([flip_ref[a, b] for b in range(3)], zero)
            start = (first + shift) * PITCH
            rows = cot4[src, start : start + 19 * PITCH + 8].astype(BF16)
            total = total + nt(rows, weight)
        total = total[: 19 * PITCH]
        grad = masked(total.astype(BF16).astype(F32), first)
        a, b, c = four(grad)
        rows = slice(first * PITCH, (first + 19) * PITCH)
        mg4[par, rows, 0:128] = a
        mg4[par, rows, 128:384] = b
        mg4[par, rows, 384:512] = c
        mg4c[par, first : first + 19, :, 0:128] = core_of(a).astype(BF16)
        mg4c[par, first : first + 19, :, 128:384] = core_of(b).astype(BF16)
        mg4c[par, first : first + 19, :, 384:512] = core_of(c).astype(BF16)

    def put(half, row, value):
        packed[half, row : row + value.shape[0], :] = (value * scale).astype(BF16)

    def hand_out(number, half, first, count, act):
        rows = pl.ds(first, count)
        for which in range(2):

            @pl.when(mine == which)
            def _():
                out = keep_ref if half == which else send_ref
                act(pltpu.make_async_copy(packed.at[half, rows], out.at[rows], sems.at[number]))

    parts = ((0, 0, 0, 4096), (1, 1, 0, 4608), (2, 0, 4096, HALF - 4096), (3, 1, 4608, HALF - 4608))

    act_t = actc[...].T
    for a in range(4):
        src, shift = fine_row(a - 1)
        prod = nn(act_t, flat(mg4c[src, 2 + shift : 18 + shift]))
        for b in range(4):
            put(0, (4 * a + b) * 256, prod[:, 128 * b : 128 * b + 128])
    hand_out(*parts[0], lambda copy: copy.start())

    agrad = jnp.zeros((18 * PITCH, 256), F32)
    for a in range(4):
        src, shift = fine_row(a - 1)
        weight = jnp.concatenate([uk_ref[a, 3 - b] for b in range(4)], axis=1)
        agrad = agrad + nt(rows_of(mg4.at[src], 1 + shift, 18), weight)
    pgrad = masked((agrad * dsilu[...]).astype(BF16).astype(F32), 1)
    for b, part in enumerate(three(pgrad)):
        pg3c[:, :, 256 * b : 256 * b + 256] = core_of(part).astype(BF16)
    pgc[...] = flat(core_of(pgrad)[1:17]).astype(BF16)

    for a in range(3):
        prod = tn(flat(botc[a : a + 16]), pgc[...])
        put(1, 768 * a, prod[:, :128])
        put(1, 2304 + 768 * a, prod[:, 128:])
    hand_out(*parts[1], lambda copy: copy.start())

    for par in range(2):
        total = flat(ext[3 + par, 1:19])
        for row_k, shift in (((1, 0), (3, -1)), ((0, 1), (2, 0)))[par]:
            k = [uk_ref[row_k, 3 - b] for b in range(4)]
            none = jnp.zeros((256, 128), BF16)
            weight = jnp.concatenate(
                [
                    jnp.concatenate([k[3], k[1], none], axis=0),
                    jnp.concatenate([none, k[2], k[0]], axis=0),
                ],
                axis=1,
            )
            total = total + nn(rows_of(act3, 1 + shift, 18), weight)
        mixed = masked(total.astype(BF16).astype(F32), 1)
        a, b, c = four(mixed)
        mix4c[par, :, :, 0:128] = core_of(a).astype(BF16)
        mix4c[par, :, :, 128:384] = core_of(b).astype(BF16)
        mix4c[par, :, :, 384:512] = core_of(c).astype(BF16)

    for a in range(3):
        prod = jnp.zeros((512, 256), F32)
        for par in range(2):
            src, shift = fine_row(par + a - 1)
            prod = prod + tn(
                flat(mix4c[src, 1 + shift : 17 + shift]), flat(z_ref[3 - par])
            )
        for b in range(3):
            tap = prod[128 * b : 128 * b + 128, :128] + prod[128 * b + 128 : 128 * b + 256, 128:]
            if a < 2:
                put(0, 4096 + (3 * a + b) * 128, tap)
            else:
                put(1, 4608 + b * 128, tap)
    put(0, 4864, jnp.zeros((HALF - 4864, 128), F32))
    put(1, 4992, jnp.zeros((HALF - 4992, 128), F32))

    for part in parts[2:]:
        hand_out(*part, lambda copy: copy.start())
    for part in parts:
        hand_out(*part, lambda copy: copy.wait())


def rest_kernel(mix4c, pg3c, bk_ref, lk_ref, level_ref, bgrad_ref, inter):
    zero = jnp.zeros((128, 128), BF16)

    for par in range(2):
        total = jnp.zeros((TILE * TILE, 256), F32)
        for a in range(3):
            src, shift = fine_row(par + a - 1)
            weight = pair_weight([lk_ref[a, b] for b in range(3)], zero)
            total = total + nn(flat(mix4c[src, 1 + shift : 17 + shift]), weight)
        total = total.reshape(TILE, TILE, 256)
        for col_par in range(2):
            inter[:, par, pl.ds(col_par, TILE, stride=2), :] = total[
                :, :, 128 * col_par : 128 * col_par + 128
            ]
    level_ref[...] = inter[...].reshape(2 * TILE, 2 * TILE, 128).astype(BF16)

    total = jnp.zeros((TILE * TILE, 256), F32)
    for a in range(3):
        weight = jnp.concatenate([bk_ref[2 - a, 2 - b] for b in range(3)], axis=1)
        total = total + nt(flat(pg3c[a : a + 16]), weight)
    bgrad_ref[...] = total.reshape(TILE, TILE, 256).astype(BF16)


def rest_work(mix4c, pg3c, bot_kernel, lvl_kernel):
    return pl.pallas_call(
        rest_kernel,
        out_shape=(
            jax.ShapeDtypeStruct((2 * TILE, 2 * TILE, 128), BF16),
            jax.ShapeDtypeStruct((TILE, TILE, 256), BF16),
        ),
        scratch_shapes=[pltpu.VMEM((TILE, 2, 2 * TILE, 128), F32)],
        compiler_params=pltpu.CompilerParams(vmem_limit_bytes=16 << 20),
        cost_estimate=pl.CostEstimate(
            flops=1000000000, bytes_accessed=3000000, transcendentals=0
        ),
    )(mix4c, pg3c, bot_kernel, lvl_kernel)


def local_work(scale, pos, *operands):
    vmem = pl.BlockSpec(memory_space=pltpu.VMEM)
    anywhere = pl.BlockSpec(memory_space=pl.ANY)
    shapes = ((2, 18, TILE, 512), (18, TILE, 768), (HALF, 128), (HALF, 128))
    return pl.pallas_call(
        functools.partial(main_kernel, scale),
        out_shape=tuple(jax.ShapeDtypeStruct(shape, BF16) for shape in shapes),
        in_specs=[pl.BlockSpec(memory_space=pltpu.SMEM)] + [vmem] * len(operands),
        out_specs=(vmem, vmem, anywhere, anywhere),
        scratch_shapes=[
            pltpu.VMEM((5, EXT, PITCH, 256), F32),
            pltpu.VMEM((EXT * PITCH, 768), F32),
            pltpu.VMEM((18, TILE, 768), BF16),
            pltpu.VMEM((EXT * PITCH, 768), F32),
            pltpu.VMEM((TILE * TILE, 256), BF16),
            pltpu.VMEM((18 * PITCH, 256), F32),
            pltpu.VMEM((2, EXT * PITCH + 8, 512), F32),
            pltpu.VMEM((2, EXT * PITCH, 512), F32),
            pltpu.VMEM((2, EXT, TILE, 512), BF16),
            pltpu.VMEM((TILE * TILE, 256), BF16),
            pltpu.VMEM((2, HALF, 128), BF16),
            pltpu.VMEM((EXT * PITCH, 128), F32),
            pltpu.SemaphoreType.DMA((4,)),
        ],
        compiler_params=pltpu.CompilerParams(vmem_limit_bytes=MAIN_LIMIT),
    )(pos, *operands)


def unpack_kernel(half_of, pos_ref, half, *refs):
    up_hbm, bot_hbm, lvl_hbm, up, bot, lvl, sems = refs[-7:]

    @pl.when(pos_ref[4] == half_of)
    def _():
        copies = []
        for i in range(4):
            rows = pl.ds(1024 * i, 1024)
            up[rows] = half[rows].astype(F32)
            copies.append(pltpu.make_async_copy(up.at[rows], up_hbm.at[rows], sems.at[i]))
            copies[-1].start()
        rows = pl.ds(0, 768)
        lvl[rows] = half[4096:4864].astype(F32)
        copies.append(pltpu.make_async_copy(lvl.at[rows], lvl_hbm.at[rows], sems.at[4]))
        copies[-1].start()
        for copy in copies:
            copy.wait()

    @pl.when(pos_ref[4] != half_of)
    def _():
        copies = []
        for i in range(3):
            rows = pl.ds(768 * i, 768)
            bot[rows, 0:128] = half[768 * i : 768 * i + 768].astype(F32)
            bot[rows, 128:256] = half[2304 + 768 * i : 3072 + 768 * i].astype(F32)
            copies.append(pltpu.make_async_copy(bot.at[rows], bot_hbm.at[rows], sems.at[i]))
            copies[-1].start()
        rows = pl.ds(768, 384)
        lvl[rows] = half[4608:4992].astype(F32)
        copies.append(pltpu.make_async_copy(lvl.at[rows], lvl_hbm.at[rows], sems.at[3]))
        copies[-1].start()
        for copy in copies:
            copy.wait()


def unpack(pos, half, begun=()):
    vmem = pl.BlockSpec(memory_space=pltpu.VMEM)
    anywhere = pl.BlockSpec(memory_space=pl.ANY)
    shapes = ((4096, 128), (2304, 256), (1152, 128))
    return pl.pallas_call(
        functools.partial(unpack_kernel, 1 if begun else 0),
        out_shape=tuple(jax.ShapeDtypeStruct(shape, F32) for shape in shapes),
        in_specs=[pl.BlockSpec(memory_space=pltpu.SMEM), vmem] + [anywhere] * len(begun),
        out_specs=(anywhere,) * 3,
        scratch_shapes=[pltpu.VMEM(shape, F32) for shape in shapes]
        + [pltpu.SemaphoreType.DMA((5,))],
        input_output_aliases={2 + i: i for i in range(len(begun))},
        compiler_params=pltpu.CompilerParams(vmem_limit_bytes=16 << 20),
        cost_estimate=pl.CostEstimate(flops=0, bytes_accessed=4000000, transcendentals=0),
    )(pos, half, *begun)


def swapped(inner, outer, axis):
    got_outer = lax.ppermute(outer, axis, OUTER_PAIRS)
    return got_outer, lax.ppermute(inner, axis, INNER_PAIRS)


def exchange(x, groups):
    return lax.all_to_all(x, AXES, 0, 0, axis_index_groups=groups)


def total_over_devices(keep, send, rest):
    got, rest = lax.optimization_barrier((lax.ppermute(send, "row", CORE_SWAP), rest))
    half = (keep.astype(F32) + got.astype(F32)).astype(BF16)
    parts = exchange(half.reshape(BLOCK, HALF // BLOCK, 128), BLOCK_GROUPS)
    part = jnp.sum(parts.astype(F32), axis=0).astype(BF16)
    total = part
    for bit in (2, 4):
        got = lax.ppermute(total, AXES, depth_swap(bit))
        total = (total.astype(F32) + got.astype(F32)).astype(BF16)
    half = exchange(jnp.broadcast_to(total[None], parts.shape), BLOCK_GROUPS).reshape(HALF, 128)
    return half, lax.ppermute(half, "row", CORE_SWAP), rest


def on_device(bottom_in, skip_feat, cotangent, bot_kernel, up_kernel, lvl_kernel):
    rows, cols = lax.axis_size("row"), lax.axis_size("col")
    scale = 1.0 / float(2 * TILE * rows * 2 * TILE * cols) ** 0.5
    z, inner, outer, own = split(bottom_in, skip_feat, cotangent)
    row_strips = swapped(inner, outer, "row")
    row_strips, z, turned = lax.optimization_barrier((row_strips, z, up_kernel))
    z, turned = z[::-1], turned[:, ::-1]
    col_strips = swapped(*with_ends(own[::-1], *row_strips), "col")
    row = lax.axis_index("row")
    pos = jnp.stack(
        [row, lax.axis_index("col"), jnp.int32(TILE * rows), jnp.int32(TILE * cols), row % 2]
    ).astype(jnp.int32)
    flip = lvl_kernel[::-1, ::-1]
    mix4c, pg3c, keep, send = local_work(
        scale, pos, z, *row_strips, *col_strips, bot_kernel, turned, flip
    )
    rest = rest_work(mix4c, pg3c, bot_kernel, lvl_kernel)
    half, other, (level_out, bottom_grad) = total_over_devices(keep, send, rest)
    up_grad, bot_grad, lvl_grad = unpack(pos, other, unpack(pos, half))
    return (
        level_out,
        bottom_grad,
        lvl_grad.reshape(3, 3, 128, 128),
        up_grad.reshape(4, 4, 256, 128),
        bot_grad.reshape(3, 3, 256, 256),
    )


def solution(mesh):
    return jax.shard_map(
        on_device,
        mesh=mesh,
        in_specs=(
            P("row", "col", None),
            P("row", "col", None),
            P("row", "col", None),
            P(),
            P(),
            P(),
        ),
        out_specs=(P("row", "col", None), P("row", "col", None), P(), P(), P()),
        check_vma=False,
    )
```
